256 devices in a mesh: interp: 16 (over z_lo, y), bte: 16 (over z_hi, x, core).
Axes of the slice: x: 4, y: 4, z: 8 (z_hi: 2, z_lo: 4; z = z_hi * 4 + z_lo), core: 2. Of those that a mesh axis runs over, the one named last changes fastest.
Arguments:
- coupling: bfloat16 [2, 64, 120, 4608], P(None, 'interp', None, 'bte'), may hold values from -0.009765625 to 0.009765625
- rvectors: int32 [64, 3], replicated, may hold values from -2 to 2
- qpoints: int32 [2048, 3], P('interp'), may hold values from 0 to 159
- polarization: bfloat16 [2048, 2, 120, 120], P('interp'), may hold values from -0.5 to 0.5
- frequencies: float32 [2048, 120], P('interp'), may hold values from 0.1 to 1
- kbatch: int32 [32], P('bte'), may hold values from 0 to 511
- kq_owner: int32 [65536, 1], P(('interp', 'bte')), may hold values from 0 to 15; in each aligned block of 256 rows (0 to 255, 256 to 511, ...) at most 64 rows name the same one
- kq_row: int32 [65536], P(('interp', 'bte')), may hold values from 0 to 511
- energy: float32 [8192, 12], P('bte'), may hold values from -4 to 4
- band_mask: int32 [8192, 12], P('bte'), may hold values 0 or 1
- deviation: float32 [8192, 3, 12], P('bte'), may hold values from -4.4 to 4.4
- velocity: float32 [32, 3, 12], P('bte'), may hold values from -5 to 5
- impurity: float32 [32, 12], P('bte'), may hold values from 0.2 to 2
Outputs:
- updated_deviation: float32 [32, 3, 12], P('bte')
The draws below stay inside these ranges and needn't reach their ends.
Inputs may be any that keep to these rules, and one draw needn't show every extreme that they name: `kq_owner`: in the [2, 128] pairs of one device, no owner is named more than 64 times, a bound that some block reaches.
All inputs are finite; a program needn't handle non-finite values. No bound on the sum of `band_mask` on one device may be relied on, other than what follows from the above.
Results may differ from the reference program's by a relative error of at most 0.00091.
Values may be sent and summed in bfloat16 or wider, within the bound.
No kernel may reach another device: no remote copies, remote signals or barrier semaphores. Data moves between devices by JAX's collectives and lax.ppermute only.
A program may use at most 192 MiB of HBM per device.

```python
import math
import jax
import jax.numpy as jnp
import numpy as np
from jax import lax

M = 12
NU = 120
R = 64
GRID = 160
KB = 2
QS = 128
ROWS_OWN = 512
CAP = 64
Q_TOTAL = 2048
K_TOTAL = 32
ROWS = 8192
PAIRS = 65536
N_INTERP = 16
N_BTE = 16


def draw_deviation(key, part):
    key = jax.random.fold_in(key, 11)
    size_key, sign_key, noise_key = jax.random.split(key, 3)
    signs = (2 * jax.random.randint(sign_key, (1, 3, M), 0, 2) - 1).astype(jnp.float32)
    magnitude = jax.random.uniform(size_key, (1, 3, M), jnp.float32, 0.8, 1.6)
    noise = jnp.clip(0.7 * jax.random.normal(noise_key, (ROWS, 3, M), jnp.float32), -2.8, 2.8)
    return signs * magnitude + noise


def touch_ends(entries, own_key, low, high):
    index_at = [jax.random.randint(jax.random.fold_in(own_key, axis), (), 0, length) for axis, length in enumerate(entries.shape)]
    widest = entries.shape.index(max(entries.shape))
    neighbour = index_at[:widest] + [(index_at[widest] + 1) % entries.shape[widest]] + index_at[widest + 1:]
    return entries.at[tuple(index_at)].set(low).at[tuple(neighbour)].set(high)


def steps_of(own_key, shape, shards, least, top_value):
    factor_of, own = 1.0, jax.random.fold_in(own_key, 6)
    for position, shards_of in shards:
        heights = jnp.exp(jax.random.uniform(jax.random.fold_in(own, position), (shards_of,), jnp.float32, least / len(shards), top_value / len(shards)))
        factor_of = factor_of * jnp.repeat(heights, shape[position] // shards_of).reshape([-1 if axis == position else 1 for axis in range(len(shape))])
    return factor_of


def routed_block(stream_key, own, number, rows, count, top, limit, lean):
    sequence = jax.random.permutation(stream_key, count)
    heavy_load, usual = portions_of(count, rows * top, limit, lean, True), portions_of(count, rows * top, limit, lean, False)
    places = jnp.arange(count)

    def named(tallies, turn):
        used = int((tallies > 0).sum())
        fixed = max(1, used // 4)
        passed = fixed + (places - fixed + turn * (used - fixed)) % max(1, count - fixed)
        return jnp.zeros((count,), jnp.int32).at[sequence[jnp.where(places < fixed, places, passed)]].set(jnp.asarray(tallies, jnp.int32))

    tallies = jnp.where(number % 4 == 0, named(heavy_load, number // 4), named(usual, number - number // 4 - 1))
    mixed = jax.random.permutation(jax.random.fold_in(own, 3), count)
    source_of, taker = mixed[0:count // 2 * 2:2], mixed[1:count // 2 * 2:2]
    slack = jnp.minimum(tallies[source_of] - 1, limit - tallies[taker]) // 2
    slack = jnp.where((source_of == sequence[0]) | (taker == sequence[0]) | (tallies[taker] == 0), 0, jnp.maximum(slack, 0))
    passed = jax.random.randint(jax.random.fold_in(own, 4), (count // 2,), 0, 1 << 20) % (slack + 1)
    tallies = tallies.at[source_of].add(-passed).at[taker].add(passed)
    members = jnp.searchsorted(jnp.cumsum(tallies), jnp.arange(rows * top), side="right").astype(jnp.int32)
    table = members.reshape(top, rows).T
    table = table[jax.random.permutation(jax.random.fold_in(own, 1), rows)]
    turn = jax.random.randint(jax.random.fold_in(own, 2), (rows, 1), 0, top)
    return jnp.take_along_axis(table, (jnp.arange(top)[None, :] + turn) % top, axis=1)


def portions_of(number_of, total, most, skew, full):
    weights = [(1 << 20) // math.isqrt(rank ** skew) + 1 for rank in range(1, number_of + 1)]
    largest = most if full else min(most, max(-(-total // number_of), total * weights[0] // sum(weights)))
    least = 1 if total - largest >= number_of - 1 else 0
    given, rest = [largest] + [least] * (number_of - 1), total - largest - least * (number_of - 1)
    while rest > 0:
        candidates = [i for i in range(1, number_of) if given[i] < largest] or [i for i in range(1, number_of) if given[i] < most]
        whole, left = sum([weights[i] for i in candidates]), rest
        for i in candidates:
            addition = min(most - given[i], max(1, left * weights[i] // whole), rest)
            given[i] = given[i] + addition
            rest = rest - addition
    return np.array(given)


def gaussian(stream_key, dims, spread, reach, cuts=(), held_as=jnp.bfloat16):
    values = jax.random.normal(stream_key, dims, jnp.float32) * spread
    if len(cuts) > 0:
        values = steps_of(stream_key, dims, cuts, -0.22, 0.18) * values
    return jnp.clip(values, min=-reach, max=reach).astype(held_as)


def setup_inputs(seed: int = 0) -> dict:
    arg_keys = jax.random.split(jax.random.key(seed), 14)
    coupling = gaussian(arg_keys[0], (2, R, NU, K_TOTAL * M * M), (4 * R * M * NU) ** -0.5, 0.009765625, ((1, 16), (3, 16)))
    rvectors = touch_ends(jax.random.randint(arg_keys[1], (R, 3), -2, 3), jax.random.fold_in(arg_keys[1], 1), -2, 2).astype(jnp.int32)
    qpoints = touch_ends(jax.random.randint(arg_keys[2], (Q_TOTAL, 3), 0, GRID), jax.random.fold_in(arg_keys[2], 1), 0, GRID - 1).astype(jnp.int32)
    polarization = gaussian(arg_keys[3], (Q_TOTAL, 2, NU, NU), NU ** -0.5, 0.5, ((0, 16),))
    frequencies = jnp.clip(jnp.exp(math.log(1.0) - 2.3025851 * jax.random.uniform(arg_keys[4], (Q_TOTAL, NU), jnp.float32) ** steps_of(arg_keys[4], (Q_TOTAL, NU), ((0, 16),), -0.2, 0.2)), 0.1, 1.0)
    kbatch = touch_ends(jax.random.randint(arg_keys[5], (K_TOTAL,), 0, ROWS_OWN), jax.random.fold_in(arg_keys[5], 1), 0, ROWS_OWN - 1).astype(jnp.int32)
    kq_owner_keys = jax.random.split(jax.random.fold_in(arg_keys[6], 1), PAIRS // (KB * QS))
    kq_owner_turns = jax.random.permutation(jax.random.fold_in(arg_keys[6], 3), PAIRS // (KB * QS))
    kq_owner = jax.vmap(lambda own, number: routed_block(jax.random.fold_in(arg_keys[6], 2), own, number, KB * QS, N_BTE, 1, CAP, 2))(kq_owner_keys, kq_owner_turns).reshape((PAIRS, 1))
    kq_row = touch_ends(jax.random.randint(arg_keys[7], (PAIRS,), 0, ROWS_OWN), jax.random.fold_in(arg_keys[7], 1), 0, ROWS_OWN - 1).astype(jnp.int32)
    energy = gaussian(arg_keys[8], (ROWS, M), 1.0, 4.0, ((0, 16),), jnp.float32)
    band_mask = touch_ends((jax.random.randint(arg_keys[9], (ROWS, M), 0, 4) < 3).astype(jnp.int32), jax.random.fold_in(arg_keys[9], 1), 0, 1)
    deviation = draw_deviation(jax.random.fold_in(arg_keys[13], 71), 0)
    velocity = gaussian(arg_keys[11], (K_TOTAL, 3, M), 1.0, 5.0, ((0, 16),), jnp.float32)
    impurity = jnp.clip(jnp.exp(math.log(2.0) - 2.3025851 * jax.random.uniform(arg_keys[12], (K_TOTAL, M), jnp.float32) ** steps_of(arg_keys[12], (K_TOTAL, M), ((0, 16),), -0.2, 0.2)), 0.2, 2.0)
    return dict(coupling=coupling, rvectors=rvectors, qpoints=qpoints, polarization=polarization, frequencies=frequencies, kbatch=kbatch, kq_owner=kq_owner, kq_row=kq_row, energy=energy, band_mask=band_mask, deviation=deviation, velocity=velocity, impurity=impurity)


SMEARING = 0.5
THERMAL = 0.3


def phase_rows(qpoints, rvectors):
    product = jnp.sum(qpoints[:, None, :] * rvectors[None, :, :], axis=2)
    phase_angle = (2.0 * jnp.pi / GRID) * jnp.mod(product, GRID).astype(jnp.float32)
    cosine = jnp.cos(phase_angle)
    sine_part = jnp.sin(phase_angle)
    top_rows = jnp.concatenate([cosine, -sine_part], axis=1)
    low_rows = jnp.concatenate([sine_part, cosine], axis=1)
    stacked = jnp.stack([top_rows, low_rows], axis=1)
    return stacked.reshape(2 * qpoints.shape[0], 2 * rvectors.shape[0]).astype(jnp.bfloat16)


def rotation_blocks(polarization):
    real_tr = jnp.swapaxes(polarization[:, 0], 1, 2)
    imag_tr = jnp.swapaxes(polarization[:, 1], 1, 2)
    top_rows = jnp.concatenate([real_tr, -imag_tr], axis=2)
    low_rows = jnp.concatenate([imag_tr, real_tr], axis=2)
    return jnp.concatenate([top_rows, low_rows], axis=1)


def scatter_weights(power, frequencies, near_energy, far_energy):
    energy_gap = (near_energy[None, :, None, :] - far_energy[:, :, :, None])[:, None]
    frequency = frequencies[:, :, None, None, None]
    occupy = 1.0 / (jnp.exp(frequency / THERMAL) - 1.0)
    absorb = jnp.exp(-(energy_gap + frequency) ** 2 / (2.0 * SMEARING ** 2))
    emission = jnp.exp(-(energy_gap - frequency) ** 2 / (2.0 * SMEARING ** 2))
    return jnp.sum(power * (occupy * absorb + (occupy + 1.0) * emission) / frequency, axis=1)


def reference(coupling, rvectors, qpoints, polarization, frequencies, kbatch, kq_owner, kq_row, energy, band_mask, deviation, velocity, impurity):
    columns = K_TOTAL * M * M
    stacked = coupling.reshape(2 * R, NU * columns)
    owners_map = kq_owner[:, 0].reshape(N_INTERP, N_BTE, KB, QS)
    rows_map = kq_row.reshape(N_INTERP, N_BTE, KB, QS)
    global_rows = owners_map * ROWS_OWN + rows_map
    global_rows = jnp.transpose(global_rows, (0, 3, 1, 2)).reshape(Q_TOTAL, K_TOTAL)
    masked = deviation * band_mask[:, None, :].astype(jnp.float32)
    fetched = masked[global_rows]
    far_energy = energy[global_rows]
    near_rows = (jnp.arange(K_TOTAL, dtype=jnp.int32) // KB) * ROWS_OWN + kbatch
    near_energy = energy[near_rows]
    near_mask = band_mask[near_rows].astype(jnp.float32)

    def q_block(inputs):
        q_slab, polar_slab, freq_slab, fetch_slab, far_slab = inputs
        phase_mat = phase_rows(q_slab, rvectors)
        field = jnp.dot(phase_mat, stacked, preferred_element_type=jnp.float32)
        coarse = field.astype(jnp.bfloat16).reshape(QS, 2 * NU, columns)
        blocks = rotation_blocks(polar_slab)
        rotated = jnp.einsum("qij,qjk->qik", blocks.astype(jnp.float32), coarse.astype(jnp.float32))
        real_part = rotated[:, :NU]
        imag_part = rotated[:, NU:]
        power = (real_part * real_part + imag_part * imag_part).reshape(QS, NU, K_TOTAL, M, M)
        kernel = scatter_weights(power, freq_slab, near_energy, far_slab) / Q_TOTAL
        scatter_rate = jnp.sum(kernel, axis=(0, 2))
        inflow = jnp.einsum("qkmn,qkcm->kcn", kernel, fetch_slab)
        return scatter_rate, inflow

    inputs = (qpoints.reshape(N_INTERP, QS, 3), polarization.reshape(N_INTERP, QS, 2, NU, NU),
              frequencies.reshape(N_INTERP, QS, NU), fetched.reshape(N_INTERP, QS, K_TOTAL, 3, M),
              far_energy.reshape(N_INTERP, QS, K_TOTAL, M))
    rates_all, inflow_all = lax.map(q_block, inputs)
    scatter_rate = jnp.sum(rates_all, axis=0)
    inflow = jnp.sum(inflow_all, axis=0)
    return near_mask[:, None, :] * (velocity + inflow) / (scatter_rate + impurity)[:, None, :]
```

```python
import functools

import jax
import jax.numpy as jnp
from jax import lax
from jax.experimental import pallas as pl
from jax.experimental.pallas import tpu as pltpu
from jax.sharding import PartitionSpec as P

GRID = 160
SMEARING = 0.5
THERMAL = 0.3
LOG2_E = 1.4426950408889634
SCALE = (LOG2_E / (2.0 * SMEARING**2)) ** 0.5

BF16 = jnp.bfloat16
F32 = jnp.float32
LANES = 128
SUB = 8
VMEM_LIMIT = 58 * 1024 * 1024

NZ, NY, NX = 4, 4, 4

M_HALF, N_THIRD = 6, 3
GROUPS = 2 * M_HALF * N_THIRD
PARTS = ((0, 12), (12, 15), (27, 9))

Q_BLOCK = 16
COL_STRIDE = 264
D_STRIDE = 136
D_BLOCK = 30
UNROLL = 8
PHASE_UNROLL = 3


def params():
    return pltpu.CompilerParams(vmem_limit_bytes=VMEM_LIMIT)


def whole(memory_space=pltpu.VMEM):
    return pl.BlockSpec(memory_space=memory_space)


def cost(flops, bytes_accessed, transcendentals=0):
    return pl.CostEstimate(
        flops=int(flops), bytes_accessed=int(bytes_accessed), transcendentals=int(transcendentals)
    )


def prepare_kernel(kbatch_ref, x_ref, energy_ref, mask_ref, dev_ref, owner_ref, row_ref, *refs):
    outs, (table, ids, near, rows) = refs[:-4], refs[-4:]
    planes, columns, nd = x_ref.shape
    bands, rows_own = energy_ref.shape
    stride = columns + SUB
    for j in range(planes):
        rows[pl.ds(j * stride, columns), 0:nd] = x_ref[j].astype(F32)
    keep = lax.broadcasted_iota(jnp.int32, (2 * SUB, LANES), 1) < nd
    for out, (first, count) in zip(outs, PARTS):
        for g in range(count):
            k, rest = divmod(first + g, M_HALF * N_THIRD)
            m_half, n_third = divmod(rest, N_THIRD)
            for pair in range(4):
                m = 2 * m_half + pair // 2
                n = 4 * n_third + 2 * (pair % 2)
                old = k * 144 + m * 12 + n
                one = rows[pl.ds(old, SUB, stride=stride), :]
                two = rows[pl.ds(old + 1, SUB, stride=stride), :]
                both = jnp.where(keep, jnp.concatenate([one, two], axis=0), 0.0)
                out[4 * g + pair] = both.astype(BF16)
    energies = energy_ref[...]
    mask = mask_ref[...].astype(F32)
    table[0:bands, :] = energies
    for c in range(3):
        table[(c + 1) * bands : (c + 2) * bands, :] = dev_ref[c] * mask
    ids[...] = owner_ref[...] * rows_own + row_ref[...]
    lane = lax.broadcasted_iota(jnp.int32, (bands, rows_own), 1)
    for k in range(2):
        line = jnp.sum(jnp.where(lane == kbatch_ref[k], energies, 0.0), axis=1, keepdims=True)
        line = jnp.broadcast_to(line * SCALE, (bands, LANES))
        for n_third in range(N_THIRD):
            some = line[4 * n_third : 4 * n_third + 4]
            first = (k * N_THIRD + n_third) * SUB
            near[first : first + SUB, :] = jnp.concatenate([some, some], axis=0)


def prepare(kbatch, planes, energy, mask, dev, owner, row):
    n, columns, _ = planes.shape
    bands, rows_own = energy.shape
    return pl.pallas_call(
        prepare_kernel,
        out_shape=[jax.ShapeDtypeStruct((4 * c, 16, LANES), BF16) for _, c in PARTS]
        + [
            jax.ShapeDtypeStruct((4 * bands, rows_own), F32),
            jax.ShapeDtypeStruct(owner.shape, jnp.int32),
            jax.ShapeDtypeStruct((2 * N_THIRD * SUB, LANES), F32),
        ],
        in_specs=[whole(pltpu.SMEM)] + [whole()] * 6,
        out_specs=[whole()] * (len(PARTS) + 3),
        scratch_shapes=[pltpu.VMEM((n * (columns + SUB), LANES), F32)],
        compiler_params=params(),
        cost_estimate=cost(0, 4e6),
        name="prepare",
    )(kbatch, planes, energy, mask, dev, owner, row)


def tables_kernel(n_q_total, q_ref, vec_ref, freq_ref, z_first, y_first, freq_out):
    n_q = q_ref.shape[1]
    own = lax.axis_index("interp")
    z, y = own // NY, own % NY
    points = [
        jnp.transpose(jnp.broadcast_to(q_ref[c : c + 1, :].astype(F32), (LANES, n_q)))
        for c in range(3)
    ]
    points = [jnp.concatenate([p, p], axis=1) for p in points]
    vectors = vec_ref[...].astype(F32).astype(BF16)
    lane = lax.broadcasted_iota(jnp.int32, (1, 2 * LANES), 1)
    block, parity, part, vector = lane // 16, lane // 8 % 2, lane // 4 % 2, lane % 4
    number = lax.broadcasted_iota(jnp.int32, (vec_ref.shape[1], 2 * LANES), 0)
    for out, dz, turn in ((z_first, block % 4, block // 4), (y_first, block // 4, block % 4)):
        dy = jnp.where(turn == 2, 3, jnp.where(turn == 3, 2, turn))
        source = (z - dz + NZ) % NZ * NY + (y - dy + NY) % NY
        pick = jnp.where(number == source * 4 + vector, 1.0, 0.0).astype(BF16)
        chosen = jnp.dot(vectors, pick, preferred_element_type=F32)
        product = sum(points[c] * chosen[c : c + 1, :] for c in range(3))
        product = product + (part * (GRID // 4)).astype(F32)
        for row, turned in enumerate((product, product - GRID // 4)):
            turned = turned - GRID * jnp.floor((turned + 0.5) * (1.0 / GRID))
            value = jnp.cos((2.0 * jnp.pi / GRID) * turned)
            for side in range(2):
                first = (2 * side + row) * n_q
                out[first : first + n_q, :] = jnp.where(parity == side, value, 0.0).astype(BF16)
    modes = freq_ref.shape[0]
    w = jnp.concatenate([freq_ref[...], jnp.ones((LANES - modes, n_q), F32)], axis=0)
    w = jnp.transpose(w)
    occupy = 1.0 / (jnp.exp(w / THERMAL) - 1.0)
    share = 1.0 / (w * n_q_total)
    freq_out[0:n_q, :] = w * SCALE
    freq_out[n_q : 2 * n_q, :] = jnp.log(occupy * share) * LOG2_E
    freq_out[2 * n_q : 3 * n_q, :] = jnp.log((occupy + 1.0) * share) * LOG2_E


def tables(n_q_total, points, vectors, freq):
    n_q = points.shape[1]
    return pl.pallas_call(
        functools.partial(tables_kernel, n_q_total),
        out_shape=[jax.ShapeDtypeStruct((4 * n_q, 2 * LANES), BF16)] * 2
        + [jax.ShapeDtypeStruct((3 * n_q, LANES), F32)],
        in_specs=[whole()] * 3,
        out_specs=[whole()] * 3,
        compiler_params=params(),
        cost_estimate=cost(1e7, 1e6),
        name="tables",
    )(points, vectors, freq)


def modes_kernel(nd, nu, turn_steps, pol_ref, out_ref, rows):
    step = pl.program_id(0)

    @pl.when(step < turn_steps)
    def _():
        pad = jnp.zeros((LANES - nu, LANES), F32)

        def one(t, carry):
            plane = jnp.concatenate([pol_ref[t].astype(F32), pad], axis=0)
            first = pl.multiple_of((step * D_BLOCK + t) * D_STRIDE, SUB)
            rows[pl.ds(first, LANES), :] = jnp.transpose(plane)
            return carry

        lax.fori_loop(0, D_BLOCK, one, 0, unroll=10)

    @pl.when(step >= turn_steps)
    def _():
        pad = jnp.zeros((LANES - nd, LANES), F32)

        def one_q(i, carry):
            q = (step - turn_steps) * Q_BLOCK + i
            real = rows[pl.ds(q, nd, stride=D_STRIDE), :]
            imag = rows[pl.ds(nd * D_STRIDE + q, nd, stride=D_STRIDE), :]
            out_ref[i, :, 0:LANES] = jnp.concatenate([real, pad], axis=0).astype(BF16)
            out_ref[i, :, LANES:] = jnp.concatenate([imag, pad], axis=0).astype(BF16)
            return carry

        lax.fori_loop(0, Q_BLOCK, one_q, 0, unroll=4)


def modes(pol):
    planes, nu, n_q = pol.shape
    nd = planes // 2
    turn_steps = planes // D_BLOCK
    return pl.pallas_call(
        functools.partial(modes_kernel, nd, nu, turn_steps),
        grid=(turn_steps + n_q // Q_BLOCK,),
        out_shape=jax.ShapeDtypeStruct((n_q, LANES, 2 * LANES), BF16),
        in_specs=[
            pl.BlockSpec((D_BLOCK, nu, n_q), lambda s: (jnp.minimum(s, turn_steps - 1), 0, 0))
        ],
        out_specs=pl.BlockSpec(
            (Q_BLOCK, LANES, 2 * LANES), lambda s: (jnp.maximum(s - turn_steps, 0), 0, 0)
        ),
        scratch_shapes=[pltpu.VMEM((planes * D_STRIDE, LANES), F32)],
        compiler_params=params(),
        cost_estimate=cost(1e8, 30e6),
        name="modes",
    )(pol)


def lookup_kernel(ids_ref, *refs):
    out = refs[-1]
    n_rows = refs[0].shape[-1]
    me = lax.axis_index("bte")
    half, x, core = me // (2 * NX), me // 2 % NX, me % 2
    ids = ids_ref[...]
    wanted = ids.shape[1]
    row = lax.broadcasted_iota(jnp.int32, (n_rows, wanted), 0)
    total = None
    for ref, dx in zip(refs[:-1], (0, 1, -1, 2)):
        for dc in range(2):
            owner = (half * NX + (x - dx + NX) % NX) * 2 + (core + dc) % 2
            table = ref[dc]
            high = table.astype(BF16)
            rest = table - high.astype(F32)
            middle = rest.astype(BF16)
            low = (rest - middle.astype(F32)).astype(BF16)
            pick = jnp.where(row == ids - owner * n_rows, 1.0, 0.0).astype(BF16)
            got = jnp.dot(
                jnp.concatenate([high, middle, low], axis=0), pick, preferred_element_type=F32
            )
            total = got if total is None else total + got
    n = refs[0].shape[1]
    found = (total[2 * n :] + total[n : 2 * n]) + total[:n]
    out[0] = found[:, : wanted // 2]
    out[1] = found[:, wanted // 2 :]


def lookup(ids, tables):
    n = tables[0].shape[1]
    return pl.pallas_call(
        lookup_kernel,
        out_shape=jax.ShapeDtypeStruct((2, n, ids.shape[1] // 2), F32),
        in_specs=[whole()] * (1 + len(tables)),
        out_specs=whole(),
        compiler_params=params(),
        cost_estimate=cost(2 * 144 * 4096 * 512, 2e6),
        name="lookup",
    )(ids, *tables)


def columns_kernel(segments, n_q, *refs):
    refs = list(refs)
    taken = []
    for _, _, n in segments:
        taken.append((refs[0], refs[1 : 1 + n]))
        refs = refs[1 + n :]
    mode_ref, near_ref, mine_ref, theirs_ref, freq_ref, out_ref, field, far_rows = refs
    columns = out_ref.shape[0]
    first_group = segments[0][0]
    step = pl.program_id(0)

    @pl.when(step == 0)
    def _():
        start = 0
        for (_, groups, _), (phase_ref, blocks) in zip(segments, taken):

            def two_pairs(p, carry, start=start, phase_ref=phase_ref, blocks=blocks):
                sides = []
                for side in range(2):
                    sides.append(
                        jnp.concatenate(
                            [b[:, 2 * p + side].reshape(b.shape[0] * 16, LANES) for b in blocks],
                            axis=0,
                        )
                    )
                both = jnp.concatenate(sides, axis=1)
                for parity in range(2):
                    got = jnp.dot(
                        phase_ref[2 * n_q * parity : 2 * n_q * (parity + 1), :],
                        both,
                        preferred_element_type=F32,
                    )
                    for side in range(2):
                        column = start + 4 * p + 2 * side + parity
                        field[pl.ds(pl.multiple_of(column * COL_STRIDE, SUB), 2 * n_q), :] = got[
                            :, side * LANES : (side + 1) * LANES
                        ]
                return carry

            lax.fori_loop(0, groups * SUB // 4, two_pairs, 0, unroll=PHASE_UNROLL)
            start += groups * SUB
        far = (mine_ref[0, 0:16, :] + theirs_ref[0, 0:16, :]) * SCALE
        for unit in range(columns // (N_THIRD * SUB)):
            k, m_half = divmod(first_group // N_THIRD + unit, M_HALF)
            for side in range(2):
                m = 2 * m_half + side
                line = far[m : m + 1, k * LANES : (k + 1) * LANES]
                turned = jnp.transpose(jnp.broadcast_to(line, (LANES, LANES)))
                for j in range(4):
                    row = unit * SUB + side * 4 + j
                    far_rows[pl.ds(row * D_STRIDE, LANES), :] = turned

    lane = lax.broadcasted_iota(jnp.int32, (columns, LANES), 1)
    units = columns // (N_THIRD * SUB)
    nears = []
    for unit in range(units):
        k = (first_group // N_THIRD + unit) // M_HALF
        nears.append(near_ref[k * N_THIRD * SUB : (k + 1) * N_THIRD * SUB, :])
    near = jnp.concatenate(nears, axis=0).reshape(units, N_THIRD, SUB, LANES)

    def some_q(i, carry):
        rotated = []
        for j in range(UNROLL):
            q = step * Q_BLOCK + i * UNROLL + j
            real = field[pl.ds(q, columns, stride=COL_STRIDE), :].astype(BF16)
            imag = field[pl.ds(q + n_q, columns, stride=COL_STRIDE), :].astype(BF16)
            mode = mode_ref[i * UNROLL + j]
            turn = jnp.concatenate([-mode[:, LANES:], mode[:, :LANES]], axis=1)
            rotated.append(
                jnp.dot(
                    jnp.concatenate([real, imag], axis=1),
                    jnp.concatenate([mode, turn], axis=0),
                    preferred_element_type=F32,
                )
            )
        out = out_ref[...]
        for j in range(UNROLL):
            q = step * Q_BLOCK + i * UNROLL + j
            far = far_rows[pl.ds(q, units * SUB, stride=D_STRIDE), :]
            gap = (near - far.reshape(units, 1, SUB, LANES)).reshape(columns, LANES)
            w = freq_ref[pl.ds(q, 1), :]
            plus, minus = gap + w, gap - w
            weight = jnp.exp2(freq_ref[pl.ds(n_q + q, 1), :] - plus * plus) + jnp.exp2(
                freq_ref[pl.ds(2 * n_q + q, 1), :] - minus * minus
            )
            real, imag = rotated[j][:, :LANES], rotated[j][:, LANES:]
            terms = (real * real + imag * imag) * weight
            out = jnp.where(lane == q, jnp.sum(terms, axis=1, keepdims=True), out)
        out_ref[...] = out
        return carry

    lax.fori_loop(0, Q_BLOCK // UNROLL, some_q, 0)


def columns_of(parts, mode, near, mine, theirs, freq):
    n_q = mode.shape[0]
    columns = SUB * sum(PARTS[index][1] for index, _, _ in parts)
    fixed = lambda shape: pl.BlockSpec(shape, lambda s: (0,) * len(shape))
    operands = []
    for _, phase, blocks in parts:
        operands += [phase, *blocks]
    rest = [near, mine, theirs, freq]
    return pl.pallas_call(
        functools.partial(
            columns_kernel, tuple(PARTS[index] + (len(blocks),) for index, _, blocks in parts), n_q
        ),
        grid=(n_q // Q_BLOCK,),
        out_shape=jax.ShapeDtypeStruct((columns, LANES), F32),
        in_specs=[fixed(o.shape) for o in operands]
        + [pl.BlockSpec((Q_BLOCK, LANES, 2 * LANES), lambda s: (s, 0, 0))]
        + [fixed(o.shape) for o in rest],
        out_specs=fixed((columns, LANES)),
        scratch_shapes=[
            pltpu.VMEM((columns * COL_STRIDE, LANES), F32),
            pltpu.VMEM((columns // N_THIRD * D_STRIDE, LANES), F32),
        ],
        compiler_params=params(),
        cost_estimate=cost(2 * n_q * columns * 65536 * 2, 30e6),
        name="columns",
    )(*operands, mode, *rest)


def totals_kernel(mine_ref, theirs_ref, *refs):
    parts, out = refs[:-1], refs[-1]
    got = mine_ref[0] + theirs_ref[0]
    upper = lax.broadcasted_iota(jnp.int32, (SUB, LANES), 0) < 4
    totals = {}
    g = 0
    for part in parts:
        for at in range(part.shape[0] // SUB):
            k, rest = divmod(g, M_HALF * N_THIRD)
            m_half, n_third = divmod(rest, N_THIRD)
            kernel = part[at * SUB : (at + 1) * SUB, :]
            for j in range(4):
                term = kernel
                if j:
                    line = j * 12 + 2 * m_half
                    lanes = slice(k * LANES, (k + 1) * LANES)
                    term = kernel * jnp.where(
                        upper,
                        jnp.broadcast_to(got[line : line + 1, lanes], (SUB, LANES)),
                        jnp.broadcast_to(got[line + 1 : line + 2, lanes], (SUB, LANES)),
                    )
                key = (j, k, n_third)
                totals[key] = totals[key] + term if key in totals else term
            g += 1
    stacked = jnp.concatenate([totals[key] for key in sorted(totals)], axis=0)
    pad = jnp.zeros((2 * LANES - stacked.shape[0], LANES), F32)
    sums = lax.dot_general(
        jnp.ones((SUB, LANES), F32),
        jnp.concatenate([stacked, pad], axis=0),
        (((1,), (1,)), ((), ())),
        preferred_element_type=F32,
        precision=lax.Precision.HIGHEST,
    )
    out[...] = sums[0:1]


def totals_of(mine, theirs, parts):
    return pl.pallas_call(
        totals_kernel,
        out_shape=jax.ShapeDtypeStruct((1, 2 * LANES), F32),
        in_specs=[whole()] * (2 + len(parts)),
        out_specs=whole(),
        compiler_params=params(),
        cost_estimate=cost(1e6, 3e5),
        name="totals",
    )(mine, theirs, *parts)


def interp_pairs(dz, dy):
    return [
        (z * NY + y, (z + dz) % NZ * NY + (y + dy) % NY) for z in range(NZ) for y in range(NY)
    ]


def bte_pairs(dh, dx, dc):
    return [
        ((h * NX + x) * 2 + c, ((h + dh) % 2 * NX + (x + dx) % NX) * 2 + (c + dc) % 2)
        for h in range(2)
        for x in range(NX)
        for c in range(2)
    ]


def along_interp(value, dz, dy):
    return lax.ppermute(value, "interp", interp_pairs(dz, dy))


def along_bte(value, dh, dx, dc):
    return lax.ppermute(value, "bte", bte_pairs(dh, dx, dc))


def gather_z_first(own):
    ring = [own]
    for _ in range(3):
        ring.append(along_interp(ring[-1], 1, 0))
    mine = jnp.stack(ring)
    up, down = along_interp(mine, 0, 1), along_interp(mine, 0, -1)
    far_up, far_down = along_interp(up[:2], 0, 1), along_interp(down[2:], 0, -1)
    return mine, up, down, far_up, far_down


def gather_y_first(own):
    up, down = along_interp(own, 0, 1), along_interp(own, 0, -1)
    half = own.shape[0] // 2
    far_up, far_down = along_interp(up[:half], 0, 1), along_interp(down[half:], 0, -1)
    mine = jnp.stack([own, up, down, jnp.concatenate([far_up, far_down])])
    ring = [mine]
    for _ in range(3):
        ring.append(along_interp(ring[-1], 1, 0))
    return tuple(ring)


def local(
    coupling,
    rvectors,
    qpoints,
    polarization,
    frequencies,
    kbatch,
    kq_owner,
    kq_row,
    energy,
    band_mask,
    deviation,
    velocity,
    impurity,
):
    n_q = qpoints.shape[0]
    nbands = energy.shape[1]
    nmodes = frequencies.shape[1]
    q_total = n_q * lax.axis_size("interp")
    columns = coupling.shape[3]

    planes = jnp.swapaxes(coupling, 2, 3).reshape(-1, columns, nmodes)
    *own_parts, own_table, ids, near = prepare(
        kbatch,
        planes,
        energy.T,
        band_mask.T,
        jnp.transpose(deviation, (1, 2, 0)),
        kq_owner.reshape(1, -1),
        kq_row.reshape(1, -1),
    )
    phase_z, phase_y, freq = tables(q_total, qpoints.T, rvectors.T, frequencies.T)

    ids = jnp.concatenate([ids, along_bte(ids, 1, 0, 0)], axis=1)
    chip_table = jnp.stack([own_table, along_bte(own_table, 0, 0, 1)])
    found = lookup(ids, [chip_table] + [along_bte(chip_table, 0, dx, 0) for dx in (1, -1, 2)])
    mine, theirs = found, along_bte(found[1:], 1, 0, 0)

    pol = jnp.transpose(polarization, (1, 2, 3, 0)).reshape(2 * nmodes, nmodes, n_q)
    mode = modes(pol)

    y_first = gather_y_first(own_parts[2])
    first = gather_z_first(own_parts[0])
    second = gather_z_first(own_parts[1])
    rest = (mode, near, mine, theirs, freq)
    parts = [
        columns_of([(0, phase_z, first)], *rest),
        columns_of([(1, phase_z, second), (2, phase_y, y_first)], *rest),
    ]
    total = totals_of(mine, theirs, parts)
    near_mask = band_mask[kbatch].astype(F32)

    total = total + along_interp(total, 0, 1) + along_interp(total, 0, -1) + along_interp(total, 0, 2)
    flip = lambda v, bits: lax.ppermute(v, "interp", [(i, i ^ bits) for i in range(NZ * NY)])
    total = total + flip(total, 4) + flip(total, 8) + flip(total, 12)

    total = total[0, : 4 * 48].reshape(4, 2, N_THIRD, 2, 4).sum(axis=3).reshape(4, 2, nbands)
    scatter_rate = total[0]
    inflow = jnp.transpose(total[1:], (1, 0, 2))
    return near_mask[:, None, :] * (velocity + inflow) / (scatter_rate + impurity)[:, None, :]


def solution(mesh):
    in_specs = (
        P(None, "interp", None, "bte"),
        P(),
        P("interp", None),
        P("interp", None, None, None),
        P("interp", None),
        P("bte"),
        P(("interp", "bte"), None),
        P(("interp", "bte")),
        P("bte", None),
        P("bte", None),
        P("bte", None, None),
        P("bte", None, None),
        P("bte", None),
    )
    out_specs = P("bte", None, None)
    return jax.shard_map(local, mesh=mesh, in_specs=in_specs, out_specs=out_specs, check_vma=False)
```

```python
import functools

import jax
import jax.numpy as jnp
from jax import lax
from jax.experimental import pallas as pl
from jax.experimental.pallas import tpu as pltpu
from jax.sharding import PartitionSpec as P

GRID = 160
SMEARING = 0.5
THERMAL = 0.3
LOG2_E = 1.4426950408889634
SCALE = (LOG2_E / (2.0 * SMEARING**2)) ** 0.5

BF16 = jnp.bfloat16
F32 = jnp.float32
LANES = 128
SUB = 8
VMEM_LIMIT = 58 * 1024 * 1024

NZ, NY, NX = 4, 4, 4

M_HALF, N_THIRD = 6, 3
GROUPS = 2 * M_HALF * N_THIRD
PARTS = ((0, 12), (12, 15), (27, 9))

Q_BLOCK = 16
COL_STRIDE = 264
D_STRIDE = 136
D_PIECE = 32
UNROLL = 8
PHASE_UNROLL = 3


def params():
    return pltpu.CompilerParams(vmem_limit_bytes=VMEM_LIMIT)


def whole(memory_space=pltpu.VMEM):
    return pl.BlockSpec(memory_space=memory_space)


def cost(flops, bytes_accessed, transcendentals=0):
    return pl.CostEstimate(
        flops=int(flops), bytes_accessed=int(bytes_accessed), transcendentals=int(transcendentals)
    )


def prepare_kernel(kbatch_ref, x_ref, energy_ref, mask_ref, dev_ref, owner_ref, row_ref, *refs):
    outs, (table, ids, near, rows) = refs[:-4], refs[-4:]
    planes, columns, nd = x_ref.shape
    bands, rows_own = energy_ref.shape
    stride = columns + SUB
    for j in range(planes):
        rows[pl.ds(j * stride, columns), 0:nd] = x_ref[j].astype(F32)
    keep = lax.broadcasted_iota(jnp.int32, (2 * SUB, LANES), 1) < nd
    for out, (first, count) in zip(outs, PARTS):
        for g in range(count):
            k, rest = divmod(first + g, M_HALF * N_THIRD)
            m_half, n_third = divmod(rest, N_THIRD)
            for pair in range(4):
                m = 2 * m_half + pair // 2
                n = 4 * n_third + 2 * (pair % 2)
                old = k * 144 + m * 12 + n
                one = rows[pl.ds(old, SUB, stride=stride), :]
                two = rows[pl.ds(old + 1, SUB, stride=stride), :]
                both = jnp.where(keep, jnp.concatenate([one, two], axis=0), 0.0)
                out[4 * g + pair] = both.astype(BF16)
    energies = energy_ref[...]
    mask = mask_ref[...].astype(F32)
    table[0:bands, :] = energies
    for c in range(3):
        table[(c + 1) * bands : (c + 2) * bands, :] = dev_ref[c] * mask
    ids[...] = owner_ref[...] * rows_own + row_ref[...]
    lane = lax.broadcasted_iota(jnp.int32, (bands, rows_own), 1)
    for k in range(2):
        line = jnp.sum(jnp.where(lane == kbatch_ref[k], energies, 0.0), axis=1, keepdims=True)
        line = jnp.broadcast_to(line * SCALE, (bands, LANES))
        for n_third in range(N_THIRD):
            some = line[4 * n_third : 4 * n_third + 4]
            first = (k * N_THIRD + n_third) * SUB
            near[first : first + SUB, :] = jnp.concatenate([some, some], axis=0)


def prepare(kbatch, planes, energy, mask, dev, owner, row):
    n, columns, _ = planes.shape
    bands, rows_own = energy.shape
    return pl.pallas_call(
        prepare_kernel,
        out_shape=[jax.ShapeDtypeStruct((4 * c, 16, LANES), BF16) for _, c in PARTS]
        + [
            jax.ShapeDtypeStruct((4 * bands, rows_own), F32),
            jax.ShapeDtypeStruct(owner.shape, jnp.int32),
            jax.ShapeDtypeStruct((2 * N_THIRD * SUB, LANES), F32),
        ],
        in_specs=[whole(pltpu.SMEM)] + [whole()] * 6,
        out_specs=[whole()] * (len(PARTS) + 3),
        scratch_shapes=[pltpu.VMEM((n * (columns + SUB), LANES), F32)],
        compiler_params=params(),
        cost_estimate=cost(1e5, 1e5),
        name="prepare",
    )(kbatch, planes, energy, mask, dev, owner, row)


def tables_kernel(n_q_total, q_ref, vec_ref, freq_ref, z_first, y_first, freq_out):
    n_q = q_ref.shape[1]
    own = lax.axis_index("interp")
    z, y = own // NY, own % NY
    points = [
        jnp.transpose(jnp.broadcast_to(q_ref[c : c + 1, :].astype(F32), (LANES, n_q)))
        for c in range(3)
    ]
    points = [jnp.concatenate([p, p], axis=1) for p in points]
    vectors = vec_ref[...].astype(F32).astype(BF16)
    lane = lax.broadcasted_iota(jnp.int32, (1, 2 * LANES), 1)
    block, parity, part, vector = lane // 16, lane // 8 % 2, lane // 4 % 2, lane % 4
    number = lax.broadcasted_iota(jnp.int32, (vec_ref.shape[1], 2 * LANES), 0)
    for out, dz, turn in ((z_first, block % 4, block // 4), (y_first, block // 4, block % 4)):
        dy = jnp.where(turn == 2, 3, jnp.where(turn == 3, 2, turn))
        source = (z - dz + NZ) % NZ * NY + (y - dy + NY) % NY
        pick = jnp.where(number == source * 4 + vector, 1.0, 0.0).astype(BF16)
        chosen = jnp.dot(vectors, pick, preferred_element_type=F32)
        product = sum(points[c] * chosen[c : c + 1, :] for c in range(3))
        product = product + (part * (GRID // 4)).astype(F32)
        for row, turned in enumerate((product, product - GRID // 4)):
            turned = turned - GRID * jnp.floor((turned + 0.5) * (1.0 / GRID))
            value = jnp.cos((2.0 * jnp.pi / GRID) * turned)
            for side in range(2):
                first = (2 * side + row) * n_q
                out[first : first + n_q, :] = jnp.where(parity == side, value, 0.0).astype(BF16)
    modes = freq_ref.shape[0]
    w = jnp.concatenate([freq_ref[...], jnp.ones((LANES - modes, n_q), F32)], axis=0)
    w = jnp.transpose(w)
    occupy = 1.0 / (jnp.exp(w / THERMAL) - 1.0)
    share = 1.0 / (w * n_q_total)
    freq_out[0:n_q, :] = w * SCALE
    freq_out[n_q : 2 * n_q, :] = jnp.log(occupy * share) * LOG2_E
    freq_out[2 * n_q : 3 * n_q, :] = jnp.log((occupy + 1.0) * share) * LOG2_E


def tables(n_q_total, points, vectors, freq):
    n_q = points.shape[1]
    return pl.pallas_call(
        functools.partial(tables_kernel, n_q_total),
        out_shape=[jax.ShapeDtypeStruct((4 * n_q, 2 * LANES), BF16)] * 2
        + [jax.ShapeDtypeStruct((3 * n_q, LANES), F32)],
        in_specs=[whole()] * 3,
        out_specs=[whole()] * 3,
        compiler_params=params(),
        cost_estimate=cost(1e5, 1e5),
        name="tables",
    )(points, vectors, freq)


def modes_kernel(nd, turn_steps, pol_ref, out_ref, rows):
    step = pl.program_id(0)
    _, per_step, nu, _ = pol_ref.shape
    per_q = out_ref.shape[0]

    @pl.when(step < turn_steps)
    def _():
        pad = jnp.zeros((LANES - nu, LANES), F32)

        def one(t, carry):
            for part in range(2):
                plane = jnp.concatenate([pol_ref[part, t].astype(F32), pad], axis=0)
                first = (part * D_PIECE + step * per_step + t) * D_STRIDE
                rows[pl.ds(pl.multiple_of(first, SUB), LANES), :] = jnp.transpose(plane)
            return carry

        lax.fori_loop(0, per_step, one, 0, unroll=4)

    @pl.when(step >= turn_steps)
    def _():
        def one_q(i, carry):
            q = (step - turn_steps) * per_q + i
            for part in range(2):
                some = rows[pl.ds(part * D_PIECE * D_STRIDE + q, nd, stride=D_STRIDE), :]
                if nd < D_PIECE:
                    some = jnp.concatenate([some, jnp.zeros((D_PIECE - nd, LANES), F32)], axis=0)
                out_ref[i, :, part * LANES : (part + 1) * LANES] = some.astype(BF16)
            return carry

        lax.fori_loop(0, per_q, one_q, 0, unroll=8)


def modes(pol, first, nd):
    _, _, nu, n_q = pol.shape
    turn_steps, q_steps = nd // SUB, 4
    start = first // SUB
    return pl.pallas_call(
        functools.partial(modes_kernel, nd, turn_steps),
        grid=(turn_steps + q_steps,),
        out_shape=jax.ShapeDtypeStruct((n_q, D_PIECE, 2 * LANES), BF16),
        in_specs=[
            pl.BlockSpec(
                (2, SUB, nu, n_q), lambda s: (0, start + jnp.minimum(s, turn_steps - 1), 0, 0)
            )
        ],
        out_specs=pl.BlockSpec(
            (n_q // q_steps, D_PIECE, 2 * LANES), lambda s: (jnp.maximum(s - turn_steps, 0), 0, 0)
        ),
        scratch_shapes=[pltpu.VMEM((2 * D_PIECE * D_STRIDE, LANES), F32)],
        compiler_params=params(),
        cost_estimate=cost(1e5, 1e5),
        name="modes",
    )(pol)


def lookup_kernel(ids_ref, *refs):
    out = refs[-1]
    n_rows = refs[0].shape[-1]
    me = lax.axis_index("bte")
    half, x, core = me // (2 * NX), me // 2 % NX, me % 2
    ids = ids_ref[...]
    wanted = ids.shape[1]
    row = lax.broadcasted_iota(jnp.int32, (n_rows, wanted), 0)
    total = None
    for ref, dx in zip(refs[:-1], (0, 1, -1, 2)):
        for dc in range(2):
            owner = (half * NX + (x - dx + NX) % NX) * 2 + (core + dc) % 2
            table = ref[dc]
            high = table.astype(BF16)
            rest = table - high.astype(F32)
            middle = rest.astype(BF16)
            low = (rest - middle.astype(F32)).astype(BF16)
            pick = jnp.where(row == ids - owner * n_rows, 1.0, 0.0).astype(BF16)
            got = jnp.dot(
                jnp.concatenate([high, middle, low], axis=0), pick, preferred_element_type=F32
            )
            total = got if total is None else total + got
    n = refs[0].shape[1]
    found = (total[2 * n :] + total[n : 2 * n]) + total[:n]
    out[0] = found[:, : wanted // 2]
    out[1] = found[:, wanted // 2 :]


def lookup(ids, tables):
    n = tables[0].shape[1]
    return pl.pallas_call(
        lookup_kernel,
        out_shape=jax.ShapeDtypeStruct((2, n, ids.shape[1] // 2), F32),
        in_specs=[whole()] * (1 + len(tables)),
        out_specs=whole(),
        compiler_params=params(),
        cost_estimate=cost(1e5, 1e5),
        name="lookup",
    )(ids, *tables)


def columns_kernel(segments, n_q, *refs):
    refs = list(refs)
    taken = []
    for _, _, n in segments:
        taken.append((refs[0], refs[1 : 1 + n]))
        refs = refs[1 + n :]
    pieces = refs[: -7]
    near_ref, mine_ref, theirs_ref, freq_ref, out_ref, field, far_rows = refs[-7:]
    columns = out_ref.shape[0]
    first_group = segments[0][0]
    step = pl.program_id(0)

    @pl.when(step == 0)
    def _():
        start = 0
        for (_, groups, _), (phase_ref, blocks) in zip(segments, taken):

            def two_pairs(p, carry, start=start, phase_ref=phase_ref, blocks=blocks):
                sides = []
                for side in range(2):
                    sides.append(
                        jnp.concatenate(
                            [b[:, 2 * p + side].reshape(b.shape[0] * 16, LANES) for b in blocks],
                            axis=0,
                        )
                    )
                both = jnp.concatenate(sides, axis=1)
                for parity in range(2):
                    got = jnp.dot(
                        phase_ref[2 * n_q * parity : 2 * n_q * (parity + 1), :],
                        both,
                        preferred_element_type=F32,
                    )
                    for side in range(2):
                        column = start + 4 * p + 2 * side + parity
                        field[pl.ds(pl.multiple_of(column * COL_STRIDE, SUB), 2 * n_q), :] = got[
                            :, side * LANES : (side + 1) * LANES
                        ]
                return carry

            lax.fori_loop(0, groups * SUB // 4, two_pairs, 0, unroll=PHASE_UNROLL)
            start += groups * SUB
        far = (mine_ref[0, 0:16, :] + theirs_ref[0, 0:16, :]) * SCALE
        for unit in range(columns // (N_THIRD * SUB)):
            k, m_half = divmod(first_group // N_THIRD + unit, M_HALF)
            for side in range(2):
                m = 2 * m_half + side
                line = far[m : m + 1, k * LANES : (k + 1) * LANES]
                turned = jnp.transpose(jnp.broadcast_to(line, (LANES, LANES)))
                for j in range(4):
                    row = unit * SUB + side * 4 + j
                    far_rows[pl.ds(row * D_STRIDE, LANES), :] = turned

    lane = lax.broadcasted_iota(jnp.int32, (columns, LANES), 1)
    units = columns // (N_THIRD * SUB)
    nears = []
    for unit in range(units):
        k = (first_group // N_THIRD + unit) // M_HALF
        nears.append(near_ref[k * N_THIRD * SUB : (k + 1) * N_THIRD * SUB, :])
    near = jnp.concatenate(nears, axis=0).reshape(units, N_THIRD, SUB, LANES)

    def some_q(i, carry):
        rotated = []
        for j in range(UNROLL):
            q = step * Q_BLOCK + i * UNROLL + j
            real = field[pl.ds(q, columns, stride=COL_STRIDE), :].astype(BF16)
            imag = field[pl.ds(q + n_q, columns, stride=COL_STRIDE), :].astype(BF16)
            mode = jnp.concatenate([p[i * UNROLL + j] for p in pieces], axis=0)
            turn = jnp.concatenate([-mode[:, LANES:], mode[:, :LANES]], axis=1)
            rotated.append(
                jnp.dot(
                    jnp.concatenate([real, imag], axis=1),
                    jnp.concatenate([mode, turn], axis=0),
                    preferred_element_type=F32,
                )
            )
        out = out_ref[...]
        for j in range(UNROLL):
            q = step * Q_BLOCK + i * UNROLL + j
            far = far_rows[pl.ds(q, units * SUB, stride=D_STRIDE), :]
            gap = (near - far.reshape(units, 1, SUB, LANES)).reshape(columns, LANES)
            w = freq_ref[pl.ds(q, 1), :]
            plus, minus = gap + w, gap - w
            weight = jnp.exp2(freq_ref[pl.ds(n_q + q, 1), :] - plus * plus) + jnp.exp2(
                freq_ref[pl.ds(2 * n_q + q, 1), :] - minus * minus
            )
            real, imag = rotated[j][:, :LANES], rotated[j][:, LANES:]
            terms = (real * real + imag * imag) * weight
            out = jnp.where(lane == q, jnp.sum(terms, axis=1, keepdims=True), out)
        out_ref[...] = out
        return carry

    lax.fori_loop(0, Q_BLOCK // UNROLL, some_q, 0)


def columns_of(parts, pieces, near, mine, theirs, freq):
    n_q = pieces[0].shape[0]
    columns = SUB * sum(PARTS[index][1] for index, _, _ in parts)
    fixed = lambda shape: pl.BlockSpec(shape, lambda s: (0,) * len(shape))
    operands = []
    for _, phase, blocks in parts:
        operands += [phase, *blocks]
    rest = [near, mine, theirs, freq]
    return pl.pallas_call(
        functools.partial(
            columns_kernel, tuple(PARTS[index] + (len(blocks),) for index, _, blocks in parts), n_q
        ),
        grid=(n_q // Q_BLOCK,),
        out_shape=jax.ShapeDtypeStruct((columns, LANES), F32),
        in_specs=[fixed(o.shape) for o in operands]
        + [pl.BlockSpec((Q_BLOCK, D_PIECE, 2 * LANES), lambda s: (s, 0, 0))] * len(pieces)
        + [fixed(o.shape) for o in rest],
        out_specs=fixed((columns, LANES)),
        scratch_shapes=[
            pltpu.VMEM((columns * COL_STRIDE, LANES), F32),
            pltpu.VMEM((columns // N_THIRD * D_STRIDE, LANES), F32),
        ],
        compiler_params=params(),
        cost_estimate=cost(1e5, 1e5),
        name="columns",
    )(*operands, *pieces, *rest)


def totals_kernel(mine_ref, theirs_ref, *refs):
    parts, out = refs[:-1], refs[-1]
    got = mine_ref[0] + theirs_ref[0]
    upper = lax.broadcasted_iota(jnp.int32, (SUB, LANES), 0) < 4
    totals = {}
    g = 0
    for part in parts:
        for at in range(part.shape[0] // SUB):
            k, rest = divmod(g, M_HALF * N_THIRD)
            m_half, n_third = divmod(rest, N_THIRD)
            kernel = part[at * SUB : (at + 1) * SUB, :]
            for j in range(4):
                term = kernel
                if j:
                    line = j * 12 + 2 * m_half
                    lanes = slice(k * LANES, (k + 1) * LANES)
                    term = kernel * jnp.where(
                        upper,
                        jnp.broadcast_to(got[line : line + 1, lanes], (SUB, LANES)),
                        jnp.broadcast_to(got[line + 1 : line + 2, lanes], (SUB, LANES)),
                    )
                key = (j, k, n_third)
                totals[key] = totals[key] + term if key in totals else term
            g += 1
    stacked = jnp.concatenate([totals[key] for key in sorted(totals)], axis=0)
    pad = jnp.zeros((2 * LANES - stacked.shape[0], LANES), F32)
    sums = lax.dot_general(
        jnp.ones((SUB, LANES), F32),
        jnp.concatenate([stacked, pad], axis=0),
        (((1,), (1,)), ((), ())),
        preferred_element_type=F32,
        precision=lax.Precision.HIGHEST,
    )
    out[...] = sums[0:1]


def totals_of(mine, theirs, parts):
    return pl.pallas_call(
        totals_kernel,
        out_shape=jax.ShapeDtypeStruct((1, 2 * LANES), F32),
        in_specs=[whole()] * (2 + len(parts)),
        out_specs=whole(),
        compiler_params=params(),
        cost_estimate=cost(1e5, 1e5),
        name="totals",
    )(mine, theirs, *parts)


def interp_pairs(dz, dy):
    return [
        (z * NY + y, (z + dz) % NZ * NY + (y + dy) % NY) for z in range(NZ) for y in range(NY)
    ]


def bte_pairs(dh, dx, dc):
    return [
        ((h * NX + x) * 2 + c, ((h + dh) % 2 * NX + (x + dx) % NX) * 2 + (c + dc) % 2)
        for h in range(2)
        for x in range(NX)
        for c in range(2)
    ]


def along_interp(value, dz, dy):
    return lax.ppermute(value, "interp", interp_pairs(dz, dy))


def along_bte(value, dh, dx, dc):
    return lax.ppermute(value, "bte", bte_pairs(dh, dx, dc))


def after(value, *others):
    return lax.optimization_barrier((value, *others))[0]


def ring_of(own, *before):
    one, three = along_interp(own, 1, 0), along_interp(own, -1, 0)
    return own, one, along_interp(after(one, *before) if before else one, 1, 0), three


def both_ways(own):
    return along_interp(own, 0, 1), along_interp(own, 0, -1)


def local(
    coupling,
    rvectors,
    qpoints,
    polarization,
    frequencies,
    kbatch,
    kq_owner,
    kq_row,
    energy,
    band_mask,
    deviation,
    velocity,
    impurity,
):
    n_q = qpoints.shape[0]
    nbands = energy.shape[1]
    nmodes = frequencies.shape[1]
    q_total = n_q * lax.axis_size("interp")
    columns = coupling.shape[3]

    planes = jnp.swapaxes(coupling, 2, 3).reshape(-1, columns, nmodes)
    *own_parts, own_table, ids, near = prepare(
        kbatch,
        planes,
        energy.T,
        band_mask.T,
        jnp.transpose(deviation, (1, 2, 0)),
        kq_owner.reshape(1, -1),
        kq_row.reshape(1, -1),
    )
    own_first, own_second, own_last = own_parts

    pol = jnp.transpose(polarization, (1, 2, 3, 0))
    cuts = [(first, min(D_PIECE, nmodes - first)) for first in range(0, nmodes, D_PIECE)]
    pieces = []

    def piece(*others):
        pieces.append(modes(after(pol, *others), *cuts[len(pieces)]))
        return pieces[-1]

    phase_z, phase_y, freq = tables(
        q_total, *after((qpoints.T, rvectors.T, frequencies.T), ids)
    )
    up, down = both_ways(own_last)
    first = ring_of(own_first, freq, piece(ids))
    other_table, other_ids = along_bte(own_table, 0, 0, 1), along_bte(ids, 1, 0, 0)

    half = own_last.shape[0] // 2
    far_up, far_down = along_interp(up[:half], 0, 1), along_interp(down[half:], 0, -1)
    chip_table = jnp.stack([own_table, other_table])
    near_tables = [along_bte(chip_table, 0, dx, 0) for dx in (1, -1, 2)]

    first_mine = after(jnp.stack(first), piece(first[1], up, down))
    first_up, first_down = both_ways(first_mine)
    second = ring_of(after(own_second, first[3]))
    piece(first_mine, far_up, far_down, second[1], second[3])

    all_ids = jnp.concatenate([ids, other_ids], axis=1)
    found = lookup(after(all_ids, pieces[2]), [chip_table] + near_tables)
    mine, theirs = found, along_bte(found[1:], 1, 0, 0)

    last_mine = jnp.stack([own_last, up, down, jnp.concatenate([far_up, far_down])])
    last = ring_of(after(last_mine, second[1]), piece(second[1]))

    second_mine = after(jnp.stack(second), found, pieces[2], first_up, first_down)
    first_far = along_interp(first_up[:2], 0, 1), along_interp(first_down[2:], 0, -1)
    second_up, second_down = both_ways(second_mine)

    rest = (pieces, near, mine, theirs, freq)
    first = (first_mine, first_up, first_down, *first_far)
    parts = [columns_of([(0, phase_z, first)], *rest)]
    second_far = (
        along_interp(after(second_up, parts[0])[:2], 0, 1),
        along_interp(after(second_down, parts[0])[2:], 0, -1),
    )
    second = (second_mine, second_up, second_down, *second_far)
    parts.append(columns_of([(1, phase_z, second), (2, phase_y, last)], *rest))
    total = totals_of(mine, theirs, parts)
    near_mask = band_mask[kbatch].astype(F32)

    total = total + along_interp(total, 0, 1) + along_interp(total, 0, -1) + along_interp(total, 0, 2)
    flip = lambda v, bits: lax.ppermute(v, "interp", [(i, i ^ bits) for i in range(NZ * NY)])
    total = total + flip(total, 4) + flip(total, 8) + flip(total, 12)

    total = total[0, : 4 * 48].reshape(4, 2, N_THIRD, 2, 4).sum(axis=3).reshape(4, 2, nbands)
    scatter_rate = total[0]
    inflow = jnp.transpose(total[1:], (1, 0, 2))
    return near_mask[:, None, :] * (velocity + inflow) / (scatter_rate + impurity)[:, None, :]


def solution(mesh):
    in_specs = (
        P(None, "interp", None, "bte"),
        P(),
        P("interp", None),
        P("interp", None, None, None),
        P("interp", None),
        P("bte"),
        P(("interp", "bte"), None),
        P(("interp", "bte")),
        P("bte", None),
        P("bte", None),
        P("bte", None, None),
        P("bte", None, None),
        P("bte", None),
    )
    out_specs = P("bte", None, None)
    return jax.shard_map(local, mesh=mesh, in_specs=in_specs, out_specs=out_specs, check_vma=False)
```

```python
import functools

import jax
import jax.numpy as jnp
from jax import lax
from jax.experimental import pallas as pl
from jax.experimental.pallas import tpu as pltpu
from jax.sharding import PartitionSpec as P

GRID = 160
SMEARING = 0.5
THERMAL = 0.3
LOG2_E = 1.4426950408889634
SCALE = (LOG2_E / (2.0 * SMEARING**2)) ** 0.5

BF16 = jnp.bfloat16
F32 = jnp.float32
LANES = 128
SUB = 8
VMEM_LIMIT = 58 * 1024 * 1024

NZ, NY, NX = 4, 4, 4

M_HALF, N_THIRD = 6, 3
GROUPS = 2 * M_HALF * N_THIRD
PARTS = ((0, 12), (12, 15), (27, 9))

Q_BLOCK = 16
COL_STRIDE = 264
D_STRIDE = 136
D_BLOCK = 30
UNROLL = 8
PHASE_UNROLL = 3


def params():
    return pltpu.CompilerParams(vmem_limit_bytes=VMEM_LIMIT)


def whole(memory_space=pltpu.VMEM):
    return pl.BlockSpec(memory_space=memory_space)


def cost(flops, bytes_accessed, transcendentals=0):
    return pl.CostEstimate(
        flops=int(flops), bytes_accessed=int(bytes_accessed), transcendentals=int(transcendentals)
    )


def prepare_kernel(kbatch_ref, x_ref, energy_ref, mask_ref, dev_ref, owner_ref, row_ref, *refs):
    outs, (table, ids, near, rows) = refs[:-4], refs[-4:]
    planes, columns, nd = x_ref.shape
    bands, rows_own = energy_ref.shape
    stride = columns + SUB
    for j in range(planes):
        rows[pl.ds(j * stride, columns), 0:nd] = x_ref[j].astype(F32)
    keep = lax.broadcasted_iota(jnp.int32, (2 * SUB, LANES), 1) < nd
    for out, (first, count) in zip(outs, PARTS):
        for g in range(count):
            k, rest = divmod(first + g, M_HALF * N_THIRD)
            m_half, n_third = divmod(rest, N_THIRD)
            for pair in range(4):
                m = 2 * m_half + pair // 2
                n = 4 * n_third + 2 * (pair % 2)
                old = k * 144 + m * 12 + n
                one = rows[pl.ds(old, SUB, stride=stride), :]
                two = rows[pl.ds(old + 1, SUB, stride=stride), :]
                both = jnp.where(keep, jnp.concatenate([one, two], axis=0), 0.0)
                out[4 * g + pair] = both.astype(BF16)
    energies = energy_ref[...]
    mask = mask_ref[...].astype(F32)
    table[0:bands, :] = energies
    for c in range(3):
        table[(c + 1) * bands : (c + 2) * bands, :] = dev_ref[c] * mask
    ids[...] = owner_ref[...] * rows_own + row_ref[...]
    lane = lax.broadcasted_iota(jnp.int32, (bands, rows_own), 1)
    for k in range(2):
        line = jnp.sum(jnp.where(lane == kbatch_ref[k], energies, 0.0), axis=1, keepdims=True)
        line = jnp.broadcast_to(line * SCALE, (bands, LANES))
        for n_third in range(N_THIRD):
            some = line[4 * n_third : 4 * n_third + 4]
            first = (k * N_THIRD + n_third) * SUB
            near[first : first + SUB, :] = jnp.concatenate([some, some], axis=0)


def prepare(kbatch, planes, energy, mask, dev, owner, row):
    n, columns, _ = planes.shape
    bands, rows_own = energy.shape
    return pl.pallas_call(
        prepare_kernel,
        out_shape=[jax.ShapeDtypeStruct((4 * c, 16, LANES), BF16) for _, c in PARTS]
        + [
            jax.ShapeDtypeStruct((4 * bands, rows_own), F32),
            jax.ShapeDtypeStruct(owner.shape, jnp.int32),
            jax.ShapeDtypeStruct((2 * N_THIRD * SUB, LANES), F32),
        ],
        in_specs=[whole(pltpu.SMEM)] + [whole()] * 6,
        out_specs=[whole()] * (len(PARTS) + 3),
        scratch_shapes=[pltpu.VMEM((n * (columns + SUB), LANES), F32)],
        compiler_params=params(),
        cost_estimate=cost(1e5, 1e5),
        name="prepare",
    )(kbatch, planes, energy, mask, dev, owner, row)


def tables_kernel(n_q_total, q_ref, vec_ref, freq_ref, z_first, y_first, in_order, freq_out):
    n_q = q_ref.shape[1]
    own = lax.axis_index("interp")
    z, y = own // NY, own % NY
    points = [
        jnp.transpose(jnp.broadcast_to(q_ref[c : c + 1, :].astype(F32), (LANES, n_q)))
        for c in range(3)
    ]
    points = [jnp.concatenate([p, p], axis=1) for p in points]
    vectors = vec_ref[...].astype(F32).astype(BF16)
    lane = lax.broadcasted_iota(jnp.int32, (1, 2 * LANES), 1)
    block, parity, part, vector = lane // 16, lane // 8 % 2, lane // 4 % 2, lane % 4
    number = lax.broadcasted_iota(jnp.int32, (vec_ref.shape[1], 2 * LANES), 0)
    sources = []
    for dz, turn in ((block % 4, block // 4), (block // 4, block % 4)):
        dy = jnp.where(turn == 2, 3, jnp.where(turn == 3, 2, turn))
        sources.append((z - dz + NZ) % NZ * NY + (y - dy + NY) % NY)
    for out, source in zip((z_first, y_first, in_order), (*sources, block)):
        pick = jnp.where(number == source * 4 + vector, 1.0, 0.0).astype(BF16)
        chosen = jnp.dot(vectors, pick, preferred_element_type=F32)
        product = sum(points[c] * chosen[c : c + 1, :] for c in range(3))
        product = product + (part * (GRID // 4)).astype(F32)
        for row, turned in enumerate((product, product - GRID // 4)):
            turned = turned - GRID * jnp.floor((turned + 0.5) * (1.0 / GRID))
            value = jnp.cos((2.0 * jnp.pi / GRID) * turned)
            for side in range(2):
                first = (2 * side + row) * n_q
                out[first : first + n_q, :] = jnp.where(parity == side, value, 0.0).astype(BF16)
    modes = freq_ref.shape[0]
    w = jnp.concatenate([freq_ref[...], jnp.ones((LANES - modes, n_q), F32)], axis=0)
    w = jnp.transpose(w)
    occupy = 1.0 / (jnp.exp(w / THERMAL) - 1.0)
    share = 1.0 / (w * n_q_total)
    freq_out[0:n_q, :] = w * SCALE
    freq_out[n_q : 2 * n_q, :] = jnp.log(occupy * share) * LOG2_E
    freq_out[2 * n_q : 3 * n_q, :] = jnp.log((occupy + 1.0) * share) * LOG2_E


def tables(n_q_total, points, vectors, freq):
    n_q = points.shape[1]
    return pl.pallas_call(
        functools.partial(tables_kernel, n_q_total),
        out_shape=[jax.ShapeDtypeStruct((4 * n_q, 2 * LANES), BF16)] * 3
        + [jax.ShapeDtypeStruct((3 * n_q, LANES), F32)],
        in_specs=[whole()] * 3,
        out_specs=[whole()] * 4,
        compiler_params=params(),
        cost_estimate=cost(1e5, 1e5),
        name="tables",
    )(points, vectors, freq)


def modes_kernel(nd, nu, turn_steps, pol_ref, out_ref, rows):
    step = pl.program_id(0)

    @pl.when(step < turn_steps)
    def _():
        pad = jnp.zeros((LANES - nu, LANES), F32)

        def one(t, carry):
            plane = jnp.concatenate([pol_ref[t].astype(F32), pad], axis=0)
            first = pl.multiple_of((step * D_BLOCK + t) * D_STRIDE, SUB)
            rows[pl.ds(first, LANES), :] = jnp.transpose(plane)
            return carry

        lax.fori_loop(0, D_BLOCK, one, 0, unroll=10)

    @pl.when(step >= turn_steps)
    def _():
        pad = jnp.zeros((LANES - nd, LANES), F32)

        def one_q(i, carry):
            q = (step - turn_steps) * Q_BLOCK + i
            real = rows[pl.ds(q, nd, stride=D_STRIDE), :]
            imag = rows[pl.ds(nd * D_STRIDE + q, nd, stride=D_STRIDE), :]
            out_ref[i, :, 0:LANES] = jnp.concatenate([real, pad], axis=0).astype(BF16)
            out_ref[i, :, LANES:] = jnp.concatenate([imag, pad], axis=0).astype(BF16)
            return carry

        lax.fori_loop(0, Q_BLOCK, one_q, 0, unroll=4)


def modes(pol):
    planes, nu, n_q = pol.shape
    nd = planes // 2
    turn_steps = planes // D_BLOCK
    return pl.pallas_call(
        functools.partial(modes_kernel, nd, nu, turn_steps),
        grid=(turn_steps + n_q // Q_BLOCK,),
        out_shape=jax.ShapeDtypeStruct((n_q, LANES, 2 * LANES), BF16),
        in_specs=[
            pl.BlockSpec((D_BLOCK, nu, n_q), lambda s: (jnp.minimum(s, turn_steps - 1), 0, 0))
        ],
        out_specs=pl.BlockSpec(
            (Q_BLOCK, LANES, 2 * LANES), lambda s: (jnp.maximum(s - turn_steps, 0), 0, 0)
        ),
        scratch_shapes=[pltpu.VMEM((planes * D_STRIDE, LANES), F32)],
        compiler_params=params(),
        cost_estimate=cost(1e5, 1e5),
        name="modes",
    )(pol)


def lookup_kernel(ids_ref, *refs):
    out = refs[-1]
    n_rows = refs[0].shape[-1]
    me = lax.axis_index("bte")
    half, x, core = me // (2 * NX), me // 2 % NX, me % 2
    ids = ids_ref[...]
    wanted = ids.shape[1]
    row = lax.broadcasted_iota(jnp.int32, (n_rows, wanted), 0)
    total = None
    for ref, dx in zip(refs[:-1], (0, 1, -1, 2)):
        for dc in range(2):
            owner = (half * NX + (x - dx + NX) % NX) * 2 + (core + dc) % 2
            table = ref[dc]
            high = table.astype(BF16)
            rest = table - high.astype(F32)
            middle = rest.astype(BF16)
            low = (rest - middle.astype(F32)).astype(BF16)
            pick = jnp.where(row == ids - owner * n_rows, 1.0, 0.0).astype(BF16)
            got = jnp.dot(
                jnp.concatenate([high, middle, low], axis=0), pick, preferred_element_type=F32
            )
            total = got if total is None else total + got
    n = refs[0].shape[1]
    found = (total[2 * n :] + total[n : 2 * n]) + total[:n]
    out[0] = found[:, : wanted // 2]
    out[1] = found[:, wanted // 2 :]


def lookup(ids, tables):
    n = tables[0].shape[1]
    return pl.pallas_call(
        lookup_kernel,
        out_shape=jax.ShapeDtypeStruct((2, n, ids.shape[1] // 2), F32),
        in_specs=[whole()] * (1 + len(tables)),
        out_specs=whole(),
        compiler_params=params(),
        cost_estimate=cost(1e5, 1e5),
        name="lookup",
    )(ids, *tables)


def columns_kernel(segments, n_q, *refs):
    refs = list(refs)
    taken = []
    for _, _, n in segments:
        taken.append((refs[0], refs[1 : 1 + n]))
        refs = refs[1 + n :]
    mode_ref, near_ref, mine_ref, theirs_ref, freq_ref, out_ref, field, far_rows = refs
    columns = out_ref.shape[0]
    first_group = segments[0][0]
    step = pl.program_id(0)

    @pl.when(step == 0)
    def _():
        start = 0
        for (_, groups, _), (phase_ref, blocks) in zip(segments, taken):

            def two_pairs(p, carry, start=start, phase_ref=phase_ref, blocks=blocks):
                sides = []
                for side in range(2):
                    sides.append(
                        jnp.concatenate(
                            [b[:, 2 * p + side].reshape(b.shape[0] * 16, LANES) for b in blocks],
                            axis=0,
                        )
                    )
                both = jnp.concatenate(sides, axis=1)
                for parity in range(2):
                    got = jnp.dot(
                        phase_ref[2 * n_q * parity : 2 * n_q * (parity + 1), :],
                        both,
                        preferred_element_type=F32,
                    )
                    for side in range(2):
                        column = start + 4 * p + 2 * side + parity
                        field[pl.ds(pl.multiple_of(column * COL_STRIDE, SUB), 2 * n_q), :] = got[
                            :, side * LANES : (side + 1) * LANES
                        ]
                return carry

            lax.fori_loop(0, groups * SUB // 4, two_pairs, 0, unroll=PHASE_UNROLL)
            start += groups * SUB
        far = (mine_ref[0, 0:16, :] + theirs_ref[0, 0:16, :]) * SCALE
        for unit in range(columns // (N_THIRD * SUB)):
            k, m_half = divmod(first_group // N_THIRD + unit, M_HALF)
            for side in range(2):
                m = 2 * m_half + side
                line = far[m : m + 1, k * LANES : (k + 1) * LANES]
                turned = jnp.transpose(jnp.broadcast_to(line, (LANES, LANES)))
                for j in range(4):
                    row = unit * SUB + side * 4 + j
                    far_rows[pl.ds(row * D_STRIDE, LANES), :] = turned

    lane = lax.broadcasted_iota(jnp.int32, (columns, LANES), 1)
    units = columns // (N_THIRD * SUB)
    nears = []
    for unit in range(units):
        k = (first_group // N_THIRD + unit) // M_HALF
        nears.append(near_ref[k * N_THIRD * SUB : (k + 1) * N_THIRD * SUB, :])
    near = jnp.concatenate(nears, axis=0).reshape(units, N_THIRD, SUB, LANES)

    def some_q(i, carry):
        rotated = []
        for j in range(UNROLL):
            q = step * Q_BLOCK + i * UNROLL + j
            real = field[pl.ds(q, columns, stride=COL_STRIDE), :].astype(BF16)
            imag = field[pl.ds(q + n_q, columns, stride=COL_STRIDE), :].astype(BF16)
            mode = mode_ref[i * UNROLL + j]
            turn = jnp.concatenate([-mode[:, LANES:], mode[:, :LANES]], axis=1)
            rotated.append(
                jnp.dot(
                    jnp.concatenate([real, imag], axis=1),
                    jnp.concatenate([mode, turn], axis=0),
                    preferred_element_type=F32,
                )
            )
        out = out_ref[...]
        for j in range(UNROLL):
            q = step * Q_BLOCK + i * UNROLL + j
            far = far_rows[pl.ds(q, units * SUB, stride=D_STRIDE), :]
            gap = (near - far.reshape(units, 1, SUB, LANES)).reshape(columns, LANES)
            w = freq_ref[pl.ds(q, 1), :]
            plus, minus = gap + w, gap - w
            weight = jnp.exp2(freq_ref[pl.ds(n_q + q, 1), :] - plus * plus) + jnp.exp2(
                freq_ref[pl.ds(2 * n_q + q, 1), :] - minus * minus
            )
            real, imag = rotated[j][:, :LANES], rotated[j][:, LANES:]
            terms = (real * real + imag * imag) * weight
            out = jnp.where(lane == q, jnp.sum(terms, axis=1, keepdims=True), out)
        out_ref[...] = out
        return carry

    lax.fori_loop(0, Q_BLOCK // UNROLL, some_q, 0)


def columns_of(parts, mode, near, mine, theirs, freq):
    n_q = mode.shape[0]
    columns = SUB * sum(PARTS[index][1] for index, _, _ in parts)
    fixed = lambda shape: pl.BlockSpec(shape, lambda s: (0,) * len(shape))
    operands = []
    for _, phase, blocks in parts:
        operands += [phase, *blocks]
    rest = [near, mine, theirs, freq]
    return pl.pallas_call(
        functools.partial(
            columns_kernel, tuple(PARTS[index] + (len(blocks),) for index, _, blocks in parts), n_q
        ),
        grid=(n_q // Q_BLOCK,),
        out_shape=jax.ShapeDtypeStruct((columns, LANES), F32),
        in_specs=[fixed(o.shape) for o in operands]
        + [pl.BlockSpec((Q_BLOCK, LANES, 2 * LANES), lambda s: (s, 0, 0))]
        + [fixed(o.shape) for o in rest],
        out_specs=fixed((columns, LANES)),
        scratch_shapes=[
            pltpu.VMEM((columns * COL_STRIDE, LANES), F32),
            pltpu.VMEM((columns // N_THIRD * D_STRIDE, LANES), F32),
        ],
        compiler_params=params(),
        cost_estimate=cost(1e5, 1e5),
        name="columns",
    )(*operands, mode, *rest)


def totals_kernel(mine_ref, theirs_ref, *refs):
    parts, out = refs[:-1], refs[-1]
    got = mine_ref[0] + theirs_ref[0]
    upper = lax.broadcasted_iota(jnp.int32, (SUB, LANES), 0) < 4
    totals = {}
    g = 0
    for part in parts:
        for at in range(part.shape[0] // SUB):
            k, rest = divmod(g, M_HALF * N_THIRD)
            m_half, n_third = divmod(rest, N_THIRD)
            kernel = part[at * SUB : (at + 1) * SUB, :]
            for j in range(4):
                term = kernel
                if j:
                    line = j * 12 + 2 * m_half
                    lanes = slice(k * LANES, (k + 1) * LANES)
                    term = kernel * jnp.where(
                        upper,
                        jnp.broadcast_to(got[line : line + 1, lanes], (SUB, LANES)),
                        jnp.broadcast_to(got[line + 1 : line + 2, lanes], (SUB, LANES)),
                    )
                key = (j, k, n_third)
                totals[key] = totals[key] + term if key in totals else term
            g += 1
    stacked = jnp.concatenate([totals[key] for key in sorted(totals)], axis=0)
    pad = jnp.zeros((2 * LANES - stacked.shape[0], LANES), F32)
    sums = lax.dot_general(
        jnp.ones((SUB, LANES), F32),
        jnp.concatenate([stacked, pad], axis=0),
        (((1,), (1,)), ((), ())),
        preferred_element_type=F32,
        precision=lax.Precision.HIGHEST,
    )
    out[...] = sums[0:1]


def totals_of(mine, theirs, parts):
    return pl.pallas_call(
        totals_kernel,
        out_shape=jax.ShapeDtypeStruct((1, 2 * LANES), F32),
        in_specs=[whole()] * (2 + len(parts)),
        out_specs=whole(),
        compiler_params=params(),
        cost_estimate=cost(1e5, 1e5),
        name="totals",
    )(mine, theirs, *parts)


def interp_pairs(dz, dy):
    return [
        (z * NY + y, (z + dz) % NZ * NY + (y + dy) % NY) for z in range(NZ) for y in range(NY)
    ]


def bte_pairs(dh, dx, dc):
    return [
        ((h * NX + x) * 2 + c, ((h + dh) % 2 * NX + (x + dx) % NX) * 2 + (c + dc) % 2)
        for h in range(2)
        for x in range(NX)
        for c in range(2)
    ]


def along_interp(value, dz, dy):
    return lax.ppermute(value, "interp", interp_pairs(dz, dy))


def along_bte(value, dh, dx, dc):
    return lax.ppermute(value, "bte", bte_pairs(dh, dx, dc))


def after(value, *others):
    return lax.optimization_barrier((value, *others))[0]


def ring_of(own, *before):
    one, three = along_interp(own, 1, 0), along_interp(own, -1, 0)
    return own, one, along_interp(after(one, *before) if before else one, 1, 0), three


def both_ways(own):
    return along_interp(own, 0, 1), along_interp(own, 0, -1)


def local(
    coupling,
    rvectors,
    qpoints,
    polarization,
    frequencies,
    kbatch,
    kq_owner,
    kq_row,
    energy,
    band_mask,
    deviation,
    velocity,
    impurity,
):
    n_q = qpoints.shape[0]
    nbands = energy.shape[1]
    nmodes = frequencies.shape[1]
    q_total = n_q * lax.axis_size("interp")
    columns = coupling.shape[3]

    planes = jnp.swapaxes(coupling, 2, 3).reshape(-1, columns, nmodes)
    *own_parts, own_table, ids, near = prepare(
        kbatch,
        planes,
        energy.T,
        band_mask.T,
        jnp.transpose(deviation, (1, 2, 0)),
        kq_owner.reshape(1, -1),
        kq_row.reshape(1, -1),
    )
    own_first, own_second, own_last = own_parts

    first = lax.all_gather(own_first, "interp")
    phase_z, phase_y, phase_all, freq = tables(
        q_total, *after((qpoints.T, rvectors.T, frequencies.T), ids)
    )
    pol = jnp.transpose(polarization, (1, 2, 3, 0)).reshape(2 * nmodes, nmodes, n_q)
    up, down = both_ways(own_last)
    mode = modes(after(pol, freq, up, down))
    second = ring_of(own_second, mode)
    half = own_last.shape[0] // 2
    far_up, far_down = along_interp(up[:half], 0, 1), along_interp(down[half:], 0, -1)
    last_mine = jnp.stack([own_last, up, down, jnp.concatenate([far_up, far_down])])
    last = ring_of(last_mine)

    other_table, other_ids = along_bte(own_table, 0, 0, 1), along_bte(ids, 1, 0, 0)
    chip_table = jnp.stack([own_table, other_table])
    near_tables = [along_bte(chip_table, 0, dx, 0) for dx in (1, -1, 2)]
    all_ids = jnp.concatenate([ids, other_ids], axis=1)
    found = lookup(all_ids, [chip_table] + near_tables)
    mine, theirs = found, along_bte(found[1:], 1, 0, 0)

    second_mine = jnp.stack(second)
    second_up, second_down = both_ways(second_mine)
    second_far = (
        along_interp(second_up[:2], 0, 1),
        along_interp(second_down[2:], 0, -1),
    )
    rest = (mode, near, mine, theirs, freq)
    second = (second_mine, second_up, second_down, *second_far)
    parts = [columns_of([(0, phase_all, [first])], *rest)]
    rest = (after(mode, parts[0]), *rest[1:])
    parts.append(columns_of([(1, phase_z, second), (2, phase_y, last)], *rest))
    total = totals_of(mine, theirs, parts)
    near_mask = band_mask[kbatch].astype(F32)

    total = total + along_interp(total, 0, 1) + along_interp(total, 0, -1) + along_interp(total, 0, 2)
    flip = lambda v, bits: lax.ppermute(v, "interp", [(i, i ^ bits) for i in range(NZ * NY)])
    total = total + flip(total, 4) + flip(total, 8) + flip(total, 12)

    total = total[0, : 4 * 48].reshape(4, 2, N_THIRD, 2, 4).sum(axis=3).reshape(4, 2, nbands)
    scatter_rate = total[0]
    inflow = jnp.transpose(total[1:], (1, 0, 2))
    return near_mask[:, None, :] * (velocity + inflow) / (scatter_rate + impurity)[:, None, :]


def solution(mesh):
    in_specs = (
        P(None, "interp", None, "bte"),
        P(),
        P("interp", None),
        P("interp", None, None, None),
        P("interp", None),
        P("bte"),
        P(("interp", "bte"), None),
        P(("interp", "bte")),
        P("bte", None),
        P("bte", None),
        P("bte", None, None),
        P("bte", None, None),
        P("bte", None),
    )
    out_specs = P("bte", None, None)
    return jax.shard_map(local, mesh=mesh, in_specs=in_specs, out_specs=out_specs, check_vma=False)
```

```python
import functools

import jax
import jax.numpy as jnp
from jax import lax
from jax.experimental import pallas as pl
from jax.experimental.pallas import tpu as pltpu
from jax.sharding import PartitionSpec as P

GRID = 160
SMEARING = 0.5
THERMAL = 0.3
LOG2_E = 1.4426950408889634
SCALE = (LOG2_E / (2.0 * SMEARING**2)) ** 0.5

BF16 = jnp.bfloat16
F32 = jnp.float32
LANES = 128
SUB = 8
VMEM_LIMIT = 58 * 1024 * 1024

NZ, NY, NX = 4, 4, 4

M_HALF, N_THIRD = 6, 3
GROUPS = 2 * M_HALF * N_THIRD
PARTS = ((0, 12), (12, 15), (27, 9))

Q_BLOCK = 16
COL_STRIDE = 264
D_STRIDE = 136
D_BLOCK = 30
UNROLL = 8
PHASE_UNROLL = 3


def params():
    return pltpu.CompilerParams(vmem_limit_bytes=VMEM_LIMIT)


def whole(memory_space=pltpu.VMEM):
    return pl.BlockSpec(memory_space=memory_space)


def cost(flops, bytes_accessed, transcendentals=0):
    return pl.CostEstimate(
        flops=int(flops), bytes_accessed=int(bytes_accessed), transcendentals=int(transcendentals)
    )


def prepare_kernel(kbatch_ref, x_ref, energy_ref, mask_ref, dev_ref, owner_ref, row_ref, *refs):
    outs, (table, ids, near, rows) = refs[:-4], refs[-4:]
    planes, columns, nd = x_ref.shape
    bands, rows_own = energy_ref.shape
    stride = columns + SUB
    for j in range(planes):
        rows[pl.ds(j * stride, columns), 0:nd] = x_ref[j].astype(F32)
    keep = lax.broadcasted_iota(jnp.int32, (2 * SUB, LANES), 1) < nd
    for out, (first, count) in zip(outs, PARTS):
        for g in range(count):
            k, rest = divmod(first + g, M_HALF * N_THIRD)
            m_half, n_third = divmod(rest, N_THIRD)
            for pair in range(4):
                m = 2 * m_half + pair // 2
                n = 4 * n_third + 2 * (pair % 2)
                old = k * 144 + m * 12 + n
                one = rows[pl.ds(old, SUB, stride=stride), :]
                two = rows[pl.ds(old + 1, SUB, stride=stride), :]
                both = jnp.where(keep, jnp.concatenate([one, two], axis=0), 0.0)
                out[4 * g + pair] = both.astype(BF16)
    energies = energy_ref[...]
    mask = mask_ref[...].astype(F32)
    table[0:bands, :] = energies
    for c in range(3):
        table[(c + 1) * bands : (c + 2) * bands, :] = dev_ref[c] * mask
    ids[...] = owner_ref[...] * rows_own + row_ref[...]
    lane = lax.broadcasted_iota(jnp.int32, (bands, rows_own), 1)
    for k in range(2):
        line = jnp.sum(jnp.where(lane == kbatch_ref[k], energies, 0.0), axis=1, keepdims=True)
        line = jnp.broadcast_to(line * SCALE, (bands, LANES))
        for n_third in range(N_THIRD):
            some = line[4 * n_third : 4 * n_third + 4]
            first = (k * N_THIRD + n_third) * SUB
            near[first : first + SUB, :] = jnp.concatenate([some, some], axis=0)


def prepare(kbatch, planes, energy, mask, dev, owner, row):
    n, columns, _ = planes.shape
    bands, rows_own = energy.shape
    return pl.pallas_call(
        prepare_kernel,
        out_shape=[jax.ShapeDtypeStruct((4 * c, 16, LANES), BF16) for _, c in PARTS]
        + [
            jax.ShapeDtypeStruct((4 * bands, rows_own), F32),
            jax.ShapeDtypeStruct(owner.shape, jnp.int32),
            jax.ShapeDtypeStruct((2 * N_THIRD * SUB, LANES), F32),
        ],
        in_specs=[whole(pltpu.SMEM)] + [whole()] * 6,
        out_specs=[whole()] * (len(PARTS) + 3),
        scratch_shapes=[pltpu.VMEM((n * (columns + SUB), LANES), F32)],
        compiler_params=params(),
        cost_estimate=cost(1e5, 1e5),
        name="prepare",
    )(kbatch, planes, energy, mask, dev, owner, row)


def tables_kernel(n_q_total, q_ref, vec_ref, freq_ref, z_first, y_first, freq_out):
    n_q = q_ref.shape[1]
    own = lax.axis_index("interp")
    z, y = own // NY, own % NY
    points = [
        jnp.transpose(jnp.broadcast_to(q_ref[c : c + 1, :].astype(F32), (LANES, n_q)))
        for c in range(3)
    ]
    points = [jnp.concatenate([p, p], axis=1) for p in points]
    vectors = vec_ref[...].astype(F32).astype(BF16)
    lane = lax.broadcasted_iota(jnp.int32, (1, 2 * LANES), 1)
    block, parity, part, vector = lane // 16, lane // 8 % 2, lane // 4 % 2, lane % 4
    number = lax.broadcasted_iota(jnp.int32, (vec_ref.shape[1], 2 * LANES), 0)
    for out, dz, turn in ((z_first, block % 4, block // 4), (y_first, block // 4, block % 4)):
        dy = jnp.where(turn == 2, 3, jnp.where(turn == 3, 2, turn))
        source = (z - dz + NZ) % NZ * NY + (y - dy + NY) % NY
        pick = jnp.where(number == source * 4 + vector, 1.0, 0.0).astype(BF16)
        chosen = jnp.dot(vectors, pick, preferred_element_type=F32)
        product = sum(points[c] * chosen[c : c + 1, :] for c in range(3))
        product = product + (part * (GRID // 4)).astype(F32)
        for row, turned in enumerate((product, product - GRID // 4)):
            turned = turned - GRID * jnp.floor((turned + 0.5) * (1.0 / GRID))
            value = jnp.cos((2.0 * jnp.pi / GRID) * turned)
            for side in range(2):
                first = (2 * side + row) * n_q
                out[first : first + n_q, :] = jnp.where(parity == side, value, 0.0).astype(BF16)
    modes = freq_ref.shape[0]
    w = jnp.concatenate([freq_ref[...], jnp.ones((LANES - modes, n_q), F32)], axis=0)
    w = jnp.transpose(w)
    occupy = 1.0 / (jnp.exp(w / THERMAL) - 1.0)
    share = 1.0 / (w * n_q_total)
    freq_out[0:n_q, :] = w * SCALE
    freq_out[n_q : 2 * n_q, :] = jnp.log(occupy * share) * LOG2_E
    freq_out[2 * n_q : 3 * n_q, :] = jnp.log((occupy + 1.0) * share) * LOG2_E


def tables(n_q_total, points, vectors, freq):
    n_q = points.shape[1]
    return pl.pallas_call(
        functools.partial(tables_kernel, n_q_total),
        out_shape=[jax.ShapeDtypeStruct((4 * n_q, 2 * LANES), BF16)] * 2
        + [jax.ShapeDtypeStruct((3 * n_q, LANES), F32)],
        in_specs=[whole()] * 3,
        out_specs=[whole()] * 3,
        compiler_params=params(),
        cost_estimate=cost(1e5, 1e5),
        name="tables",
    )(points, vectors, freq)


def modes_kernel(nd, nu, turn_steps, pol_ref, out_ref, rows):
    step = pl.program_id(0)

    @pl.when(step < turn_steps)
    def _():
        pad = jnp.zeros((LANES - nu, LANES), F32)

        def one(t, carry):
            plane = jnp.concatenate([pol_ref[t].astype(F32), pad], axis=0)
            first = pl.multiple_of((step * D_BLOCK + t) * D_STRIDE, SUB)
            rows[pl.ds(first, LANES), :] = jnp.transpose(plane)
            return carry

        lax.fori_loop(0, D_BLOCK, one, 0, unroll=10)

    @pl.when(step >= turn_steps)
    def _():
        pad = jnp.zeros((LANES - nd, LANES), F32)

        def one_q(i, carry):
            q = (step - turn_steps) * Q_BLOCK + i
            real = rows[pl.ds(q, nd, stride=D_STRIDE), :]
            imag = rows[pl.ds(nd * D_STRIDE + q, nd, stride=D_STRIDE), :]
            out_ref[i, :, 0:LANES] = jnp.concatenate([real, pad], axis=0).astype(BF16)
            out_ref[i, :, LANES:] = jnp.concatenate([imag, pad], axis=0).astype(BF16)
            return carry

        lax.fori_loop(0, Q_BLOCK, one_q, 0, unroll=4)


def modes(pol):
    planes, nu, n_q = pol.shape
    nd = planes // 2
    turn_steps = planes // D_BLOCK
    return pl.pallas_call(
        functools.partial(modes_kernel, nd, nu, turn_steps),
        grid=(turn_steps + n_q // Q_BLOCK,),
        out_shape=jax.ShapeDtypeStruct((n_q, LANES, 2 * LANES), BF16),
        in_specs=[
            pl.BlockSpec((D_BLOCK, nu, n_q), lambda s: (jnp.minimum(s, turn_steps - 1), 0, 0))
        ],
        out_specs=pl.BlockSpec(
            (Q_BLOCK, LANES, 2 * LANES), lambda s: (jnp.maximum(s - turn_steps, 0), 0, 0)
        ),
        scratch_shapes=[pltpu.VMEM((planes * D_STRIDE, LANES), F32)],
        compiler_params=params(),
        cost_estimate=cost(1e5, 1e5),
        name="modes",
    )(pol)


def lookup_kernel(ids_ref, *refs):
    out = refs[-1]
    n_rows = refs[0].shape[-1]
    me = lax.axis_index("bte")
    half, x, core = me // (2 * NX), me // 2 % NX, me % 2
    ids = ids_ref[...]
    wanted = ids.shape[1]
    row = lax.broadcasted_iota(jnp.int32, (n_rows, wanted), 0)
    total = None
    for ref, dx in zip(refs[:-1], (0, 1, -1, 2)):
        for dc in range(2):
            owner = (half * NX + (x - dx + NX) % NX) * 2 + (core + dc) % 2
            table = ref[dc]
            high = table.astype(BF16)
            rest = table - high.astype(F32)
            middle = rest.astype(BF16)
            low = (rest - middle.astype(F32)).astype(BF16)
            pick = jnp.where(row == ids - owner * n_rows, 1.0, 0.0).astype(BF16)
            got = jnp.dot(
                jnp.concatenate([high, middle, low], axis=0), pick, preferred_element_type=F32
            )
            total = got if total is None else total + got
    n = refs[0].shape[1]
    found = (total[2 * n :] + total[n : 2 * n]) + total[:n]
    out[0] = found[:, : wanted // 2]
    out[1] = found[:, wanted // 2 :]


def lookup(ids, tables):
    n = tables[0].shape[1]
    return pl.pallas_call(
        lookup_kernel,
        out_shape=jax.ShapeDtypeStruct((2, n, ids.shape[1] // 2), F32),
        in_specs=[whole()] * (1 + len(tables)),
        out_specs=whole(),
        compiler_params=params(),
        cost_estimate=cost(1e5, 1e5),
        name="lookup",
    )(ids, *tables)


def columns_kernel(segments, n_q, *refs):
    refs = list(refs)
    taken = []
    for _, _, n in segments:
        taken.append((refs[0], refs[1 : 1 + n]))
        refs = refs[1 + n :]
    mode_ref, near_ref, mine_ref, theirs_ref, freq_ref, out_ref, field, far_rows = refs
    columns = out_ref.shape[0]
    first_group = segments[0][0]
    step = pl.program_id(0)

    @pl.when(step == 0)
    def _():
        start = 0
        for (_, groups, _), (phase_ref, blocks) in zip(segments, taken):

            def two_pairs(p, carry, start=start, phase_ref=phase_ref, blocks=blocks):
                sides = []
                for side in range(2):
                    sides.append(
                        jnp.concatenate(
                            [b[:, 2 * p + side].reshape(b.shape[0] * 16, LANES) for b in blocks],
                            axis=0,
                        )
                    )
                both = jnp.concatenate(sides, axis=1)
                for parity in range(2):
                    got = jnp.dot(
                        phase_ref[2 * n_q * parity : 2 * n_q * (parity + 1), :],
                        both,
                        preferred_element_type=F32,
                    )
                    for side in range(2):
                        column = start + 4 * p + 2 * side + parity
                        field[pl.ds(pl.multiple_of(column * COL_STRIDE, SUB), 2 * n_q), :] = got[
                            :, side * LANES : (side + 1) * LANES
                        ]
                return carry

            lax.fori_loop(0, groups * SUB // 4, two_pairs, 0, unroll=PHASE_UNROLL)
            start += groups * SUB
        far = (mine_ref[0, 0:16, :] + theirs_ref[0, 0:16, :]) * SCALE
        for unit in range(columns // (N_THIRD * SUB)):
            k, m_half = divmod(first_group // N_THIRD + unit, M_HALF)
            for side in range(2):
                m = 2 * m_half + side
                line = far[m : m + 1, k * LANES : (k + 1) * LANES]
                turned = jnp.transpose(jnp.broadcast_to(line, (LANES, LANES)))
                for j in range(4):
                    row = unit * SUB + side * 4 + j
                    far_rows[pl.ds(row * D_STRIDE, LANES), :] = turned

    lane = lax.broadcasted_iota(jnp.int32, (columns, LANES), 1)
    units = columns // (N_THIRD * SUB)
    nears = []
    for unit in range(units):
        k = (first_group // N_THIRD + unit) // M_HALF
        nears.append(near_ref[k * N_THIRD * SUB : (k + 1) * N_THIRD * SUB, :])
    near = jnp.concatenate(nears, axis=0).reshape(units, N_THIRD, SUB, LANES)

    def some_q(i, carry):
        rotated = []
        for j in range(UNROLL):
            q = step * Q_BLOCK + i * UNROLL + j
            real = field[pl.ds(q, columns, stride=COL_STRIDE), :].astype(BF16)
            imag = field[pl.ds(q + n_q, columns, stride=COL_STRIDE), :].astype(BF16)
            mode = mode_ref[i * UNROLL + j]
            turn = jnp.concatenate([-mode[:, LANES:], mode[:, :LANES]], axis=1)
            rotated.append(
                jnp.dot(
                    jnp.concatenate([real, imag], axis=1),
                    jnp.concatenate([mode, turn], axis=0),
                    preferred_element_type=F32,
                )
            )
        out = out_ref[...]
        for j in range(UNROLL):
            q = step * Q_BLOCK + i * UNROLL + j
            far = far_rows[pl.ds(q, units * SUB, stride=D_STRIDE), :]
            gap = (near - far.reshape(units, 1, SUB, LANES)).reshape(columns, LANES)
            w = freq_ref[pl.ds(q, 1), :]
            plus, minus = gap + w, gap - w
            weight = jnp.exp2(freq_ref[pl.ds(n_q + q, 1), :] - plus * plus) + jnp.exp2(
                freq_ref[pl.ds(2 * n_q + q, 1), :] - minus * minus
            )
            real, imag = rotated[j][:, :LANES], rotated[j][:, LANES:]
            terms = (real * real + imag * imag) * weight
            out = jnp.where(lane == q, jnp.sum(terms, axis=1, keepdims=True), out)
        out_ref[...] = out
        return carry

    lax.fori_loop(0, Q_BLOCK // UNROLL, some_q, 0)


def columns_of(parts, mode, near, mine, theirs, freq):
    n_q = mode.shape[0]
    columns = SUB * sum(PARTS[index][1] for index, _, _ in parts)
    fixed = lambda shape: pl.BlockSpec(shape, lambda s: (0,) * len(shape))
    operands = []
    for _, phase, blocks in parts:
        operands += [phase, *blocks]
    rest = [near, mine, theirs, freq]
    return pl.pallas_call(
        functools.partial(
            columns_kernel, tuple(PARTS[index] + (len(blocks),) for index, _, blocks in parts), n_q
        ),
        grid=(n_q // Q_BLOCK,),
        out_shape=jax.ShapeDtypeStruct((columns, LANES), F32),
        in_specs=[fixed(o.shape) for o in operands]
        + [pl.BlockSpec((Q_BLOCK, LANES, 2 * LANES), lambda s: (s, 0, 0))]
        + [fixed(o.shape) for o in rest],
        out_specs=fixed((columns, LANES)),
        scratch_shapes=[
            pltpu.VMEM((columns * COL_STRIDE, LANES), F32),
            pltpu.VMEM((columns // N_THIRD * D_STRIDE, LANES), F32),
        ],
        compiler_params=params(),
        cost_estimate=cost(1e5, 1e5),
        name="columns",
    )(*operands, mode, *rest)


def totals_kernel(mine_ref, theirs_ref, *refs):
    parts, out = refs[:-1], refs[-1]
    got = mine_ref[0] + theirs_ref[0]
    upper = lax.broadcasted_iota(jnp.int32, (SUB, LANES), 0) < 4
    totals = {}
    g = 0
    for part in parts:
        for at in range(part.shape[0] // SUB):
            k, rest = divmod(g, M_HALF * N_THIRD)
            m_half, n_third = divmod(rest, N_THIRD)
            kernel = part[at * SUB : (at + 1) * SUB, :]
            for j in range(4):
                term = kernel
                if j:
                    line = j * 12 + 2 * m_half
                    lanes = slice(k * LANES, (k + 1) * LANES)
                    term = kernel * jnp.where(
                        upper,
                        jnp.broadcast_to(got[line : line + 1, lanes], (SUB, LANES)),
                        jnp.broadcast_to(got[line + 1 : line + 2, lanes], (SUB, LANES)),
                    )
                key = (j, k, n_third)
                totals[key] = totals[key] + term if key in totals else term
            g += 1
    stacked = jnp.concatenate([totals[key] for key in sorted(totals)], axis=0)
    pad = jnp.zeros((2 * LANES - stacked.shape[0], LANES), F32)
    sums = lax.dot_general(
        jnp.ones((SUB, LANES), F32),
        jnp.concatenate([stacked, pad], axis=0),
        (((1,), (1,)), ((), ())),
        preferred_element_type=F32,
        precision=lax.Precision.HIGHEST,
    )
    out[...] = sums[0:1]


def totals_of(mine, theirs, parts):
    return pl.pallas_call(
        totals_kernel,
        out_shape=jax.ShapeDtypeStruct((1, 2 * LANES), F32),
        in_specs=[whole()] * (2 + len(parts)),
        out_specs=whole(),
        compiler_params=params(),
        cost_estimate=cost(1e5, 1e5),
        name="totals",
    )(mine, theirs, *parts)


def interp_pairs(dz, dy):
    return [
        (z * NY + y, (z + dz) % NZ * NY + (y + dy) % NY) for z in range(NZ) for y in range(NY)
    ]


def bte_pairs(dh, dx, dc):
    return [
        ((h * NX + x) * 2 + c, ((h + dh) % 2 * NX + (x + dx) % NX) * 2 + (c + dc) % 2)
        for h in range(2)
        for x in range(NX)
        for c in range(2)
    ]


def along_interp(value, dz, dy):
    return lax.ppermute(value, "interp", interp_pairs(dz, dy))


def along_bte(value, dh, dx, dc):
    return lax.ppermute(value, "bte", bte_pairs(dh, dx, dc))


def after(value, *others):
    return lax.optimization_barrier((value, *others))[0]


def ring_of(own, *before):
    one, three = along_interp(own, 1, 0), along_interp(own, -1, 0)
    return own, one, along_interp(after(one, *before) if before else one, 1, 0), three


def both_ways(own):
    return along_interp(own, 0, 1), along_interp(own, 0, -1)


def local(
    coupling,
    rvectors,
    qpoints,
    polarization,
    frequencies,
    kbatch,
    kq_owner,
    kq_row,
    energy,
    band_mask,
    deviation,
    velocity,
    impurity,
):
    n_q = qpoints.shape[0]
    nbands = energy.shape[1]
    nmodes = frequencies.shape[1]
    q_total = n_q * lax.axis_size("interp")
    columns = coupling.shape[3]

    planes = jnp.swapaxes(coupling, 2, 3).reshape(-1, columns, nmodes)
    *own_parts, own_table, ids, near = prepare(
        kbatch,
        planes,
        energy.T,
        band_mask.T,
        jnp.transpose(deviation, (1, 2, 0)),
        kq_owner.reshape(1, -1),
        kq_row.reshape(1, -1),
    )
    own_first, own_second, own_last = own_parts

    other_ids = along_bte(ids, 1, 0, 0)
    phase_z, phase_y, freq = tables(
        q_total, *after((qpoints.T, rvectors.T, frequencies.T), other_ids)
    )
    first = ring_of(own_first, freq)
    up, down = both_ways(own_last)
    other_table = along_bte(own_table, 0, 0, 1)

    second = ring_of(after(own_second, freq))
    half = own_last.shape[0] // 2
    far_up, far_down = along_interp(up[:half], 0, 1), along_interp(down[half:], 0, -1)
    chip_table = jnp.stack([own_table, other_table])
    near_tables = [along_bte(chip_table, 0, dx, 0) for dx in (1, -1, 2)]

    first_mine = jnp.stack(first)
    first_up, first_down = both_ways(after(first_mine, far_up, far_down))

    last_mine = jnp.stack([own_last, up, down, jnp.concatenate([far_up, far_down])])

    pol = jnp.transpose(polarization, (1, 2, 3, 0)).reshape(2 * nmodes, nmodes, n_q)
    mode = modes(after(pol, first_mine, last_mine, second[3], *near_tables))

    all_ids = jnp.concatenate([ids, other_ids], axis=1)
    last_one = along_interp(after(last_mine, second[1], second[3]), 1, 0)
    found = lookup(
        after(all_ids, mode, first_up, first_down, last_one), [chip_table] + near_tables
    )
    last = (
        last_mine,
        last_one,
        along_interp(after(last_one, found), 1, 0),
        along_interp(after(last_mine, found), -1, 0),
    )
    mine, theirs = found, along_bte(found[1:], 1, 0, 0)

    first_far = along_interp(first_up[:2], 0, 1), along_interp(first_down[2:], 0, -1)
    second_mine = after(jnp.stack(second), found)
    second_up, second_down = both_ways(second_mine)
    second_far = (
        along_interp(after(second_up, *first_far, theirs)[:2], 0, 1),
        along_interp(after(second_down, *first_far, theirs)[2:], 0, -1),
    )

    first = (first_mine, first_up, first_down, *first_far)
    second = (second_mine, second_up, second_down, *second_far)
    y_first = last
    rest = (mode, near, mine, theirs, freq)
    parts = [
        columns_of([(0, phase_z, first)], *rest),
        columns_of([(1, phase_z, second), (2, phase_y, y_first)], *rest),
    ]
    total = totals_of(mine, theirs, parts)
    near_mask = band_mask[kbatch].astype(F32)

    total = total + along_interp(total, 0, 1) + along_interp(total, 0, -1) + along_interp(total, 0, 2)
    flip = lambda v, bits: lax.ppermute(v, "interp", [(i, i ^ bits) for i in range(NZ * NY)])
    total = total + flip(total, 4) + flip(total, 8) + flip(total, 12)

    total = total[0, : 4 * 48].reshape(4, 2, N_THIRD, 2, 4).sum(axis=3).reshape(4, 2, nbands)
    scatter_rate = total[0]
    inflow = jnp.transpose(total[1:], (1, 0, 2))
    return near_mask[:, None, :] * (velocity + inflow) / (scatter_rate + impurity)[:, None, :]


def solution(mesh):
    in_specs = (
        P(None, "interp", None, "bte"),
        P(),
        P("interp", None),
        P("interp", None, None, None),
        P("interp", None),
        P("bte"),
        P(("interp", "bte"), None),
        P(("interp", "bte")),
        P("bte", None),
        P("bte", None),
        P("bte", None, None),
        P("bte", None, None),
        P("bte", None),
    )
    out_specs = P("bte", None, None)
    return jax.shard_map(local, mesh=mesh, in_specs=in_specs, out_specs=out_specs, check_vma=False)
```

```python
import functools

import jax
import jax.numpy as jnp
from jax import lax
from jax.experimental import pallas as pl
from jax.experimental.pallas import tpu as pltpu
from jax.sharding import PartitionSpec as P

GRID = 160
SMEARING = 0.5
THERMAL = 0.3
LOG2_E = 1.4426950408889634
SCALE = (LOG2_E / (2.0 * SMEARING**2)) ** 0.5

BF16 = jnp.bfloat16
F32 = jnp.float32
LANES = 128
SUB = 8
VMEM_LIMIT = 58 * 1024 * 1024

NZ, NY, NX = 4, 4, 4
N_INTERP = NZ * NY

M_HALF, N_THIRD = 6, 3
GROUPS = 2 * M_HALF * N_THIRD
PARTS = ((0, 12), (12, 24))

Q_BLOCK = 16
COL_STRIDE = 264
D_STRIDE = 136
D_BLOCK = 30
UNROLL = 16
PHASE_UNROLL = 3


def params():
    return pltpu.CompilerParams(vmem_limit_bytes=VMEM_LIMIT)


def whole(memory_space=pltpu.VMEM):
    return pl.BlockSpec(memory_space=memory_space)


def cost(flops, bytes_accessed, transcendentals=0):
    return pl.CostEstimate(
        flops=int(flops), bytes_accessed=int(bytes_accessed), transcendentals=int(transcendentals)
    )


def prepare_kernel(kbatch_ref, x_ref, energy_ref, mask_ref, dev_ref, owner_ref, row_ref, *refs):
    outs, (table, ids, near, rows) = refs[:-4], refs[-4:]
    planes, columns, nd = x_ref.shape
    bands, rows_own = energy_ref.shape
    stride = columns + SUB
    for j in range(planes):
        rows[pl.ds(j * stride, columns), 0:nd] = x_ref[j].astype(F32)
    keep = lax.broadcasted_iota(jnp.int32, (2 * SUB, LANES), 1) < nd
    for out, (first, count) in zip(outs, PARTS):
        for g in range(count):
            k, rest = divmod(first + g, M_HALF * N_THIRD)
            m_half, n_third = divmod(rest, N_THIRD)
            for pair in range(4):
                m = 2 * m_half + pair // 2
                n = 4 * n_third + 2 * (pair % 2)
                old = k * 144 + m * 12 + n
                one = rows[pl.ds(old, SUB, stride=stride), :]
                two = rows[pl.ds(old + 1, SUB, stride=stride), :]
                both = jnp.where(keep, jnp.concatenate([one, two], axis=0), 0.0)
                out[4 * g + pair] = both.astype(BF16)
    energies = energy_ref[...]
    mask = mask_ref[...].astype(F32)
    table[0:bands, :] = energies
    for c in range(3):
        table[(c + 1) * bands : (c + 2) * bands, :] = dev_ref[c] * mask
    ids[...] = owner_ref[...] * rows_own + row_ref[...]
    lane = lax.broadcasted_iota(jnp.int32, (bands, rows_own), 1)
    for k in range(2):
        line = jnp.sum(jnp.where(lane == kbatch_ref[k], energies, 0.0), axis=1, keepdims=True)
        line = jnp.broadcast_to(line * SCALE, (bands, LANES))
        for n_third in range(N_THIRD):
            some = line[4 * n_third : 4 * n_third + 4]
            first = (k * N_THIRD + n_third) * SUB
            near[first : first + SUB, :] = jnp.concatenate([some, some], axis=0)


def prepare(kbatch, planes, energy, mask, dev, owner, row):
    n, columns, _ = planes.shape
    bands, rows_own = energy.shape
    return pl.pallas_call(
        prepare_kernel,
        out_shape=[jax.ShapeDtypeStruct((4 * c, 16, LANES), BF16) for _, c in PARTS]
        + [
            jax.ShapeDtypeStruct((4 * bands, rows_own), F32),
            jax.ShapeDtypeStruct(owner.shape, jnp.int32),
            jax.ShapeDtypeStruct((2 * N_THIRD * SUB, LANES), F32),
        ],
        in_specs=[whole(pltpu.SMEM)] + [whole()] * 6,
        out_specs=[whole()] * (len(PARTS) + 3),
        scratch_shapes=[pltpu.VMEM((n * (columns + SUB), LANES), F32)],
        compiler_params=params(),
        cost_estimate=cost(1e5, 1e5),
        name="prepare",
    )(kbatch, planes, energy, mask, dev, owner, row)


def tables_kernel(n_q_total, q_ref, vec_ref, freq_ref, out, freq_out):
    n_q = q_ref.shape[1]
    own = lax.axis_index("interp")
    z, y = own // NY, own % NY
    points = [
        jnp.transpose(jnp.broadcast_to(q_ref[c : c + 1, :].astype(F32), (LANES, n_q)))
        for c in range(3)
    ]
    points = [jnp.concatenate([p, p], axis=1) for p in points]
    vectors = vec_ref[...].astype(F32).astype(BF16)
    lane = lax.broadcasted_iota(jnp.int32, (1, 2 * LANES), 1)
    block, parity, part, vector = lane // 16, lane // 8 % 2, lane // 4 % 2, lane % 4
    number = lax.broadcasted_iota(jnp.int32, (vec_ref.shape[1], 2 * LANES), 0)
    dz, turn = block % 4, block // 4
    dy = jnp.where(turn == 2, 3, jnp.where(turn == 3, 2, turn))
    source = (z - dz + NZ) % NZ * NY + (y - dy + NY) % NY
    pick = jnp.where(number == source * 4 + vector, 1.0, 0.0).astype(BF16)
    chosen = jnp.dot(vectors, pick, preferred_element_type=F32)
    product = sum(points[c] * chosen[c : c + 1, :] for c in range(3))
    product = product + (part * (GRID // 4)).astype(F32)
    for row, turned in enumerate((product, product - GRID // 4)):
        turned = turned - GRID * jnp.floor((turned + 0.5) * (1.0 / GRID))
        value = jnp.cos((2.0 * jnp.pi / GRID) * turned)
        for side in range(2):
            first = (2 * side + row) * n_q
            out[first : first + n_q, :] = jnp.where(parity == side, value, 0.0).astype(BF16)
    modes = freq_ref.shape[0]
    w = jnp.concatenate([freq_ref[...], jnp.ones((LANES - modes, n_q), F32)], axis=0)
    w = jnp.transpose(w)
    occupy = 1.0 / (jnp.exp(w / THERMAL) - 1.0)
    share = 1.0 / (w * n_q_total)
    freq_out[0:n_q, :] = w * SCALE
    freq_out[n_q : 2 * n_q, :] = jnp.log(occupy * share) * LOG2_E
    freq_out[2 * n_q : 3 * n_q, :] = jnp.log((occupy + 1.0) * share) * LOG2_E


def tables(n_q_total, points, vectors, freq):
    n_q = points.shape[1]
    return pl.pallas_call(
        functools.partial(tables_kernel, n_q_total),
        out_shape=[
            jax.ShapeDtypeStruct((4 * n_q, 2 * LANES), BF16),
            jax.ShapeDtypeStruct((3 * n_q, LANES), F32),
        ],
        in_specs=[whole()] * 3,
        out_specs=[whole()] * 2,
        compiler_params=params(),
        cost_estimate=cost(1e5, 1e5),
        name="tables",
    )(points, vectors, freq)


def modes_kernel(nd, nu, turn_steps, pol_ref, out_ref, rows):
    step = pl.program_id(0)

    @pl.when(step < turn_steps)
    def _():
        pad = jnp.zeros((LANES - nu, LANES), F32)

        def one(t, carry):
            plane = jnp.concatenate([pol_ref[t].astype(F32), pad], axis=0)
            first = pl.multiple_of((step * D_BLOCK + t) * D_STRIDE, SUB)
            rows[pl.ds(first, LANES), :] = jnp.transpose(plane)
            return carry

        lax.fori_loop(0, D_BLOCK, one, 0, unroll=10)

    @pl.when(step >= turn_steps)
    def _():
        pad = jnp.zeros((LANES - nd, LANES), F32)

        def one_q(i, carry):
            q = (step - turn_steps) * Q_BLOCK + i
            real = rows[pl.ds(q, nd, stride=D_STRIDE), :]
            imag = rows[pl.ds(nd * D_STRIDE + q, nd, stride=D_STRIDE), :]
            out_ref[i, :, 0:LANES] = jnp.concatenate([real, pad], axis=0).astype(BF16)
            out_ref[i, :, LANES:] = jnp.concatenate([imag, pad], axis=0).astype(BF16)
            return carry

        lax.fori_loop(0, Q_BLOCK, one_q, 0, unroll=4)


def modes(pol):
    planes, nu, n_q = pol.shape
    nd = planes // 2
    turn_steps = planes // D_BLOCK
    return pl.pallas_call(
        functools.partial(modes_kernel, nd, nu, turn_steps),
        grid=(turn_steps + n_q // Q_BLOCK,),
        out_shape=jax.ShapeDtypeStruct((n_q, LANES, 2 * LANES), BF16),
        in_specs=[
            pl.BlockSpec((D_BLOCK, nu, n_q), lambda s: (jnp.minimum(s, turn_steps - 1), 0, 0))
        ],
        out_specs=pl.BlockSpec(
            (Q_BLOCK, LANES, 2 * LANES), lambda s: (jnp.maximum(s - turn_steps, 0), 0, 0)
        ),
        scratch_shapes=[pltpu.VMEM((planes * D_STRIDE, LANES), F32)],
        compiler_params=params(),
        cost_estimate=cost(1e5, 1e5),
        name="modes",
    )(pol)


def lookup_kernel(ids_ref, *refs):
    out = refs[-1]
    n_rows = refs[0].shape[-1]
    me = lax.axis_index("bte")
    half, x, core = me // (2 * NX), me // 2 % NX, me % 2
    ids = ids_ref[...]
    wanted = ids.shape[1]
    row = lax.broadcasted_iota(jnp.int32, (n_rows, wanted), 0)
    total = None
    for ref, dx in zip(refs[:-1], (0, 1, -1, 2)):
        for dc in range(2):
            owner = (half * NX + (x - dx + NX) % NX) * 2 + (core + dc) % 2
            table = ref[dc]
            high = table.astype(BF16)
            rest = table - high.astype(F32)
            middle = rest.astype(BF16)
            low = (rest - middle.astype(F32)).astype(BF16)
            pick = jnp.where(row == ids - owner * n_rows, 1.0, 0.0).astype(BF16)
            got = jnp.dot(
                jnp.concatenate([high, middle, low], axis=0), pick, preferred_element_type=F32
            )
            total = got if total is None else total + got
    n = refs[0].shape[1]
    found = (total[2 * n :] + total[n : 2 * n]) + total[:n]
    out[0] = found[:, : wanted // 2]
    out[1] = found[:, wanted // 2 :]


def lookup(ids, tables):
    n = tables[0].shape[1]
    return pl.pallas_call(
        lookup_kernel,
        out_shape=jax.ShapeDtypeStruct((2, n, ids.shape[1] // 2), F32),
        in_specs=[whole()] * (1 + len(tables)),
        out_specs=whole(),
        compiler_params=params(),
        cost_estimate=cost(1e5, 1e5),
        name="lookup",
    )(ids, *tables)


def totals(got, parts, shape):
    upper = lax.broadcasted_iota(jnp.int32, (SUB, LANES), 0) < 4
    sums = {}
    g = 0
    for part in parts:
        for at in range(part.shape[0] // SUB):
            k, rest = divmod(g, M_HALF * N_THIRD)
            m_half, n_third = divmod(rest, N_THIRD)
            kernel = part[at * SUB : (at + 1) * SUB, :]
            for j in range(4):
                term = kernel
                if j:
                    line = j * 12 + 2 * m_half
                    lanes = slice(k * LANES, (k + 1) * LANES)
                    term = kernel * jnp.where(
                        upper,
                        jnp.broadcast_to(got[line : line + 1, lanes], (SUB, LANES)),
                        jnp.broadcast_to(got[line + 1 : line + 2, lanes], (SUB, LANES)),
                    )
                key = (j, k, n_third)
                sums[key] = sums[key] + term if key in sums else term
            g += 1
    stacked = jnp.concatenate([sums[key] for key in sorted(sums)], axis=0)
    pad = jnp.zeros((shape[1] - stacked.shape[0], LANES), F32)
    return lax.dot_general(
        jnp.ones((shape[0], LANES), F32),
        jnp.concatenate([stacked, pad], axis=0),
        (((1,), (1,)), ((), ())),
        preferred_element_type=F32,
        precision=lax.Precision.HIGHEST,
    )


def columns_kernel(first_group, n_blocks, n_q, earlier, *refs):
    phase_ref, blocks, refs = refs[0], refs[1 : 1 + n_blocks], refs[1 + n_blocks :]
    mode_ref, near_ref, mine_ref, theirs_ref, freq_ref = refs[:5]
    if earlier is None:
        out_ref, field, far_rows = refs[5:]
    else:
        others, (total_ref, field, far_rows, out_ref) = refs[5 : 5 + earlier], refs[5 + earlier :]
    columns = out_ref.shape[0]
    step = pl.program_id(0)

    @pl.when(step == 0)
    def _():
        def two_pairs(p, carry):
            sides = []
            for side in range(2):
                sides.append(
                    jnp.concatenate(
                        [b[:, 2 * p + side].reshape(b.shape[0] * 16, LANES) for b in blocks], axis=0
                    )
                )
            both = jnp.concatenate(sides, axis=1)
            for parity in range(2):
                got = jnp.dot(
                    phase_ref[2 * n_q * parity : 2 * n_q * (parity + 1), :],
                    both,
                    preferred_element_type=F32,
                )
                for side in range(2):
                    column = 4 * p + 2 * side + parity
                    field[pl.ds(pl.multiple_of(column * COL_STRIDE, SUB), 2 * n_q), :] = got[
                        :, side * LANES : (side + 1) * LANES
                    ]
            return carry

        lax.fori_loop(0, columns // 4, two_pairs, 0, unroll=PHASE_UNROLL)
        far = (mine_ref[0, 0:16, :] + theirs_ref[0, 0:16, :]) * SCALE
        for unit in range(columns // (N_THIRD * SUB)):
            k, m_half = divmod(first_group // N_THIRD + unit, M_HALF)
            for side in range(2):
                m = 2 * m_half + side
                line = far[m : m + 1, k * LANES : (k + 1) * LANES]
                turned = jnp.transpose(jnp.broadcast_to(line, (LANES, LANES)))
                for j in range(4):
                    row = unit * SUB + side * 4 + j
                    far_rows[pl.ds(row * D_STRIDE, LANES), :] = turned

    lane = lax.broadcasted_iota(jnp.int32, (columns, LANES), 1)
    units = columns // (N_THIRD * SUB)
    nears = []
    for unit in range(units):
        k = (first_group // N_THIRD + unit) // M_HALF
        nears.append(near_ref[k * N_THIRD * SUB : (k + 1) * N_THIRD * SUB, :])
    near = jnp.concatenate(nears, axis=0).reshape(units, N_THIRD, SUB, LANES)

    def some_q(i, carry):
        rotated = []
        for j in range(UNROLL):
            q = step * Q_BLOCK + i * UNROLL + j
            real = field[pl.ds(q, columns, stride=COL_STRIDE), :].astype(BF16)
            imag = field[pl.ds(q + n_q, columns, stride=COL_STRIDE), :].astype(BF16)
            mode = mode_ref[i * UNROLL + j]
            turn = jnp.concatenate([-mode[:, LANES:], mode[:, :LANES]], axis=1)
            rotated.append(
                jnp.dot(
                    jnp.concatenate([real, imag], axis=1),
                    jnp.concatenate([mode, turn], axis=0),
                    preferred_element_type=F32,
                )
            )
        out = out_ref[...]
        for j in range(UNROLL):
            q = step * Q_BLOCK + i * UNROLL + j
            far = far_rows[pl.ds(q, units * SUB, stride=D_STRIDE), :]
            gap = (near - far.reshape(units, 1, SUB, LANES)).reshape(columns, LANES)
            w = freq_ref[pl.ds(q, 1), :]
            plus, minus = gap + w, gap - w
            weight = jnp.exp2(freq_ref[pl.ds(n_q + q, 1), :] - plus * plus) + jnp.exp2(
                freq_ref[pl.ds(2 * n_q + q, 1), :] - minus * minus
            )
            real, imag = rotated[j][:, :LANES], rotated[j][:, LANES:]
            terms = (real * real + imag * imag) * weight
            out = jnp.where(lane == q, jnp.sum(terms, axis=1, keepdims=True), out)
        out_ref[...] = out
        return carry

    lax.fori_loop(0, Q_BLOCK // UNROLL, some_q, 0)

    if earlier is not None:

        @pl.when(step == pl.num_programs(0) - 1)
        def _():
            total_ref[...] = totals(mine_ref[0] + theirs_ref[0], [*others, out_ref], total_ref.shape)


def columns_of(index, phase, blocks, mode, near, mine, theirs, freq, others=None):
    n_q = mode.shape[0]
    first, groups = PARTS[index]
    columns = SUB * groups
    fixed = lambda shape: pl.BlockSpec(shape, lambda s: (0,) * len(shape))
    operands = [phase, *blocks]
    rest = [near, mine, theirs, freq, *(others or [])]
    sums = (columns, LANES)
    out = sums if others is None else (N_INTERP, 2 * LANES)
    return pl.pallas_call(
        functools.partial(
            columns_kernel, first, len(blocks), n_q, None if others is None else len(others)
        ),
        grid=(n_q // Q_BLOCK,),
        out_shape=jax.ShapeDtypeStruct(out, F32),
        in_specs=[fixed(o.shape) for o in operands]
        + [pl.BlockSpec((Q_BLOCK, LANES, 2 * LANES), lambda s: (s, 0, 0))]
        + [fixed(o.shape) for o in rest],
        out_specs=fixed(out),
        scratch_shapes=[
            pltpu.VMEM((columns * COL_STRIDE, LANES), F32),
            pltpu.VMEM((columns // N_THIRD * D_STRIDE, LANES), F32),
        ]
        + ([] if others is None else [pltpu.VMEM(sums, F32)]),
        compiler_params=params(),
        cost_estimate=cost(1e5, 1e5),
        name="columns",
    )(*operands, mode, *rest)


def interp_pairs(dz, dy):
    return [
        (z * NY + y, (z + dz) % NZ * NY + (y + dy) % NY) for z in range(NZ) for y in range(NY)
    ]


def bte_pairs(dh, dx, dc):
    return [
        ((h * NX + x) * 2 + c, ((h + dh) % 2 * NX + (x + dx) % NX) * 2 + (c + dc) % 2)
        for h in range(2)
        for x in range(NX)
        for c in range(2)
    ]


def along_interp(value, dz, dy):
    return lax.ppermute(value, "interp", interp_pairs(dz, dy))


def along_bte(value, dh, dx, dc):
    return lax.ppermute(value, "bte", bte_pairs(dh, dx, dc))


def after(value, *others):
    return lax.optimization_barrier((value, *others))[0]


def ring_of(own, *before):
    one, three = along_interp(own, 1, 0), along_interp(own, -1, 0)
    return own, one, along_interp(after(one, *before) if before else one, 1, 0), three


def both_ways(own):
    return along_interp(own, 0, 1), along_interp(own, 0, -1)


def local(
    coupling,
    rvectors,
    qpoints,
    polarization,
    frequencies,
    kbatch,
    kq_owner,
    kq_row,
    energy,
    band_mask,
    deviation,
    velocity,
    impurity,
):
    n_q = qpoints.shape[0]
    nbands = energy.shape[1]
    nmodes = frequencies.shape[1]
    q_total = n_q * lax.axis_size("interp")
    columns = coupling.shape[3]

    planes = jnp.swapaxes(coupling, 2, 3).reshape(-1, columns, nmodes)
    *own_parts, own_table, ids, near = prepare(
        kbatch,
        planes,
        energy.T,
        band_mask.T,
        jnp.transpose(deviation, (1, 2, 0)),
        kq_owner.reshape(1, -1),
        kq_row.reshape(1, -1),
    )
    own_first, own_second = own_parts

    other_ids = along_bte(ids, 1, 0, 0)
    phase, freq = tables(q_total, *after((qpoints.T, rvectors.T, frequencies.T), ids))
    first = ring_of(own_first, freq, other_ids)
    other_table = along_bte(own_table, 0, 0, 1)
    second = ring_of(after(own_second, freq))
    chip_table = jnp.stack([own_table, other_table])
    near_tables = [along_bte(chip_table, 0, dx, 0) for dx in (1, -1, 2)]

    first_mine = jnp.stack(first)
    first_up, first_down = both_ways(first_mine)

    pol = jnp.transpose(polarization, (1, 2, 3, 0)).reshape(2 * nmodes, nmodes, n_q)
    mode = modes(after(pol, first_mine, *near_tables))

    all_ids = jnp.concatenate([ids, other_ids], axis=1)
    found = lookup(after(all_ids, mode, first_up, first_down), [chip_table] + near_tables)
    mine, theirs = found, along_bte(found[1:], 1, 0, 0)

    first_far = along_interp(first_up[:2], 0, 1), along_interp(first_down[2:], 0, -1)
    second_mine = after(jnp.stack(second), found)
    second_up, second_down = both_ways(second_mine)
    second_far = (
        along_interp(after(second_up, *first_far, theirs)[:2], 0, 1),
        along_interp(after(second_down, *first_far, theirs)[2:], 0, -1),
    )

    rest = (mode, near, mine, theirs, freq)
    sums = columns_of(0, phase, (first_mine, first_up, first_down, *first_far), *rest)
    total = columns_of(
        1, phase, (second_mine, second_up, second_down, *second_far), *rest, others=[sums]
    )
    near_mask = band_mask[kbatch].astype(F32)

    total = lax.all_to_all(total, "interp", 0, 0, tiled=True).sum(axis=0)
    total = total[: 4 * 48].reshape(4, 2, N_THIRD, 2, 4).sum(axis=3).reshape(4, 2, nbands)
    scatter_rate = total[0]
    inflow = jnp.transpose(total[1:], (1, 0, 2))
    return near_mask[:, None, :] * (velocity + inflow) / (scatter_rate + impurity)[:, None, :]


def solution(mesh):
    in_specs = (
        P(None, "interp", None, "bte"),
        P(),
        P("interp", None),
        P("interp", None, None, None),
        P("interp", None),
        P("bte"),
        P(("interp", "bte"), None),
        P(("interp", "bte")),
        P("bte", None),
        P("bte", None),
        P("bte", None, None),
        P("bte", None, None),
        P("bte", None),
    )
    out_specs = P("bte", None, None)
    return jax.shard_map(local, mesh=mesh, in_specs=in_specs, out_specs=out_specs, check_vma=False)
```

```python
import functools

import jax
import jax.numpy as jnp
from jax import lax
from jax.experimental import pallas as pl
from jax.experimental.pallas import tpu as pltpu
from jax.sharding import PartitionSpec as P

GRID = 160
SMEARING = 0.5
THERMAL = 0.3
LOG2_E = 1.4426950408889634
SCALE = (LOG2_E / (2.0 * SMEARING**2)) ** 0.5

BF16 = jnp.bfloat16
F32 = jnp.float32
LANES = 128
SUB = 8
VMEM_LIMIT = 58 * 1024 * 1024

NZ, NY, NX = 4, 4, 4
N_INTERP = NZ * NY

M_HALF, N_THIRD = 6, 3
GROUPS = 2 * M_HALF * N_THIRD
PARTS = ((0, 12), (12, 24))

Q_BLOCK = 16
COL_STRIDE = 264
D_STRIDE = 136
D_BLOCK = 30
UNROLL = 16
PHASE_UNROLL = 3


def params():
    return pltpu.CompilerParams(vmem_limit_bytes=VMEM_LIMIT)


def whole(memory_space=pltpu.VMEM):
    return pl.BlockSpec(memory_space=memory_space)


def cost(flops, bytes_accessed, transcendentals=0):
    return pl.CostEstimate(
        flops=int(flops), bytes_accessed=int(bytes_accessed), transcendentals=int(transcendentals)
    )


def prepare_kernel(kbatch_ref, x_ref, energy_ref, mask_ref, dev_ref, owner_ref, row_ref, *refs):
    outs, (table, ids, near, rows) = refs[:-4], refs[-4:]
    planes, columns, nd = x_ref.shape
    bands, rows_own = energy_ref.shape
    stride = columns + SUB
    for j in range(planes):
        rows[pl.ds(j * stride, columns), 0:nd] = x_ref[j].astype(F32)
    keep = lax.broadcasted_iota(jnp.int32, (2 * SUB, LANES), 1) < nd
    for out, (first, count) in zip(outs, PARTS):
        for g in range(count):
            k, rest = divmod(first + g, M_HALF * N_THIRD)
            m_half, n_third = divmod(rest, N_THIRD)
            for pair in range(4):
                m = 2 * m_half + pair // 2
                n = 4 * n_third + 2 * (pair % 2)
                old = k * 144 + m * 12 + n
                one = rows[pl.ds(old, SUB, stride=stride), :]
                two = rows[pl.ds(old + 1, SUB, stride=stride), :]
                both = jnp.where(keep, jnp.concatenate([one, two], axis=0), 0.0)
                out[4 * g + pair] = both.astype(BF16)
    energies = energy_ref[...]
    mask = mask_ref[...].astype(F32)
    table[0:bands, :] = energies
    for c in range(3):
        table[(c + 1) * bands : (c + 2) * bands, :] = dev_ref[c] * mask
    ids[...] = owner_ref[...] * rows_own + row_ref[...]
    lane = lax.broadcasted_iota(jnp.int32, (bands, rows_own), 1)
    for k in range(2):
        line = jnp.sum(jnp.where(lane == kbatch_ref[k], energies, 0.0), axis=1, keepdims=True)
        line = jnp.broadcast_to(line * SCALE, (bands, LANES))
        for n_third in range(N_THIRD):
            some = line[4 * n_third : 4 * n_third + 4]
            first = (k * N_THIRD + n_third) * SUB
            near[first : first + SUB, :] = jnp.concatenate([some, some], axis=0)


def prepare(kbatch, planes, energy, mask, dev, owner, row):
    n, columns, _ = planes.shape
    bands, rows_own = energy.shape
    return pl.pallas_call(
        prepare_kernel,
        out_shape=[jax.ShapeDtypeStruct((4 * c, 16, LANES), BF16) for _, c in PARTS]
        + [
            jax.ShapeDtypeStruct((4 * bands, rows_own), F32),
            jax.ShapeDtypeStruct(owner.shape, jnp.int32),
            jax.ShapeDtypeStruct((2 * N_THIRD * SUB, LANES), F32),
        ],
        in_specs=[whole(pltpu.SMEM)] + [whole()] * 6,
        out_specs=[whole()] * (len(PARTS) + 3),
        scratch_shapes=[pltpu.VMEM((n * (columns + SUB), LANES), F32)],
        compiler_params=params(),
        cost_estimate=cost(1e5, 1e5),
        name="prepare",
    )(kbatch, planes, energy, mask, dev, owner, row)


def tables_kernel(n_q_total, q_ref, vec_ref, freq_ref, out, freq_out):
    n_q = q_ref.shape[1]
    own = lax.axis_index("interp")
    z, y = own // NY, own % NY
    points = [
        jnp.transpose(jnp.broadcast_to(q_ref[c : c + 1, :].astype(F32), (LANES, n_q)))
        for c in range(3)
    ]
    points = [jnp.concatenate([p, p], axis=1) for p in points]
    vectors = vec_ref[...].astype(F32).astype(BF16)
    lane = lax.broadcasted_iota(jnp.int32, (1, 2 * LANES), 1)
    block, parity, part, vector = lane // 16, lane // 8 % 2, lane // 4 % 2, lane % 4
    number = lax.broadcasted_iota(jnp.int32, (vec_ref.shape[1], 2 * LANES), 0)
    dz, turn = block % 4, block // 4
    dy = jnp.where(turn == 2, 3, jnp.where(turn == 3, 2, turn))
    source = (z - dz + NZ) % NZ * NY + (y - dy + NY) % NY
    pick = jnp.where(number == source * 4 + vector, 1.0, 0.0).astype(BF16)
    chosen = jnp.dot(vectors, pick, preferred_element_type=F32)
    product = sum(points[c] * chosen[c : c + 1, :] for c in range(3))
    product = product + (part * (GRID // 4)).astype(F32)
    for row, turned in enumerate((product, product - GRID // 4)):
        turned = turned - GRID * jnp.floor((turned + 0.5) * (1.0 / GRID))
        value = jnp.cos((2.0 * jnp.pi / GRID) * turned)
        for side in range(2):
            first = (2 * side + row) * n_q
            out[first : first + n_q, :] = jnp.where(parity == side, value, 0.0).astype(BF16)
    modes = freq_ref.shape[0]
    w = jnp.concatenate([freq_ref[...], jnp.ones((LANES - modes, n_q), F32)], axis=0)
    w = jnp.transpose(w)
    occupy = 1.0 / (jnp.exp(w / THERMAL) - 1.0)
    share = 1.0 / (w * n_q_total)
    freq_out[0:n_q, :] = w * SCALE
    freq_out[n_q : 2 * n_q, :] = jnp.log(occupy * share) * LOG2_E
    freq_out[2 * n_q : 3 * n_q, :] = jnp.log((occupy + 1.0) * share) * LOG2_E


def tables(n_q_total, points, vectors, freq):
    n_q = points.shape[1]
    return pl.pallas_call(
        functools.partial(tables_kernel, n_q_total),
        out_shape=[
            jax.ShapeDtypeStruct((4 * n_q, 2 * LANES), BF16),
            jax.ShapeDtypeStruct((3 * n_q, LANES), F32),
        ],
        in_specs=[whole()] * 3,
        out_specs=[whole()] * 2,
        compiler_params=params(),
        cost_estimate=cost(1e5, 1e5),
        name="tables",
    )(points, vectors, freq)


def modes_kernel(nd, nu, turn_steps, pol_ref, out_ref, rows):
    step = pl.program_id(0)

    @pl.when(step < turn_steps)
    def _():
        pad = jnp.zeros((LANES - nu, LANES), F32)

        def one(t, carry):
            plane = jnp.concatenate([pol_ref[t].astype(F32), pad], axis=0)
            first = pl.multiple_of((step * D_BLOCK + t) * D_STRIDE, SUB)
            rows[pl.ds(first, LANES), :] = jnp.transpose(plane)
            return carry

        lax.fori_loop(0, D_BLOCK, one, 0, unroll=10)

    @pl.when(step >= turn_steps)
    def _():
        pad = jnp.zeros((LANES - nd, LANES), F32)

        def one_q(i, carry):
            q = (step - turn_steps) * Q_BLOCK + i
            real = rows[pl.ds(q, nd, stride=D_STRIDE), :]
            imag = rows[pl.ds(nd * D_STRIDE + q, nd, stride=D_STRIDE), :]
            out_ref[i, :, 0:LANES] = jnp.concatenate([real, pad], axis=0).astype(BF16)
            out_ref[i, :, LANES:] = jnp.concatenate([imag, pad], axis=0).astype(BF16)
            return carry

        lax.fori_loop(0, Q_BLOCK, one_q, 0, unroll=4)


def modes(pol):
    planes, nu, n_q = pol.shape
    nd = planes // 2
    turn_steps = planes // D_BLOCK
    return pl.pallas_call(
        functools.partial(modes_kernel, nd, nu, turn_steps),
        grid=(turn_steps + n_q // Q_BLOCK,),
        out_shape=jax.ShapeDtypeStruct((n_q, LANES, 2 * LANES), BF16),
        in_specs=[
            pl.BlockSpec((D_BLOCK, nu, n_q), lambda s: (jnp.minimum(s, turn_steps - 1), 0, 0))
        ],
        out_specs=pl.BlockSpec(
            (Q_BLOCK, LANES, 2 * LANES), lambda s: (jnp.maximum(s - turn_steps, 0), 0, 0)
        ),
        scratch_shapes=[pltpu.VMEM((planes * D_STRIDE, LANES), F32)],
        compiler_params=params(),
        cost_estimate=cost(1e5, 1e5),
        name="modes",
    )(pol)


def lookup_kernel(ids_ref, *refs):
    out = refs[-1]
    n_rows = refs[0].shape[-1]
    me = lax.axis_index("bte")
    half, x, core = me // (2 * NX), me // 2 % NX, me % 2
    ids = ids_ref[...]
    wanted = ids.shape[1]
    row = lax.broadcasted_iota(jnp.int32, (n_rows, wanted), 0)
    total = None
    for ref, dx in zip(refs[:-1], (0, 1, -1, 2)):
        for dc in range(2):
            owner = (half * NX + (x - dx + NX) % NX) * 2 + (core + dc) % 2
            table = ref[dc]
            high = table.astype(BF16)
            rest = table - high.astype(F32)
            middle = rest.astype(BF16)
            low = (rest - middle.astype(F32)).astype(BF16)
            pick = jnp.where(row == ids - owner * n_rows, 1.0, 0.0).astype(BF16)
            got = jnp.dot(
                jnp.concatenate([high, middle, low], axis=0), pick, preferred_element_type=F32
            )
            total = got if total is None else total + got
    n = refs[0].shape[1]
    found = (total[2 * n :] + total[n : 2 * n]) + total[:n]
    out[0] = found[:, : wanted // 2]
    out[1] = found[:, wanted // 2 :]


def lookup(ids, tables):
    n = tables[0].shape[1]
    return pl.pallas_call(
        lookup_kernel,
        out_shape=jax.ShapeDtypeStruct((2, n, ids.shape[1] // 2), F32),
        in_specs=[whole()] * (1 + len(tables)),
        out_specs=whole(),
        compiler_params=params(),
        cost_estimate=cost(1e5, 1e5),
        name="lookup",
    )(ids, *tables)


def totals(got, parts, shape):
    upper = lax.broadcasted_iota(jnp.int32, (SUB, LANES), 0) < 4
    sums = {}
    g = 0
    for part in parts:
        for at in range(part.shape[0] // SUB):
            k, rest = divmod(g, M_HALF * N_THIRD)
            m_half, n_third = divmod(rest, N_THIRD)
            kernel = part[at * SUB : (at + 1) * SUB, :]
            for j in range(4):
                term = kernel
                if j:
                    line = j * 12 + 2 * m_half
                    lanes = slice(k * LANES, (k + 1) * LANES)
                    term = kernel * jnp.where(
                        upper,
                        jnp.broadcast_to(got[line : line + 1, lanes], (SUB, LANES)),
                        jnp.broadcast_to(got[line + 1 : line + 2, lanes], (SUB, LANES)),
                    )
                key = (j, k, n_third)
                sums[key] = sums[key] + term if key in sums else term
            g += 1
    stacked = jnp.concatenate([sums[key] for key in sorted(sums)], axis=0)
    pad = jnp.zeros((shape[1] - stacked.shape[0], LANES), F32)
    return lax.dot_general(
        jnp.ones((shape[0], LANES), F32),
        jnp.concatenate([stacked, pad], axis=0),
        (((1,), (1,)), ((), ())),
        preferred_element_type=F32,
        precision=lax.Precision.HIGHEST,
    )


def columns_kernel(first_group, n_blocks, n_q, earlier, *refs):
    phase_ref, blocks, refs = refs[0], refs[1 : 1 + n_blocks], refs[1 + n_blocks :]
    mode_ref, near_ref, mine_ref, theirs_ref, freq_ref = refs[:5]
    if earlier is None:
        out_ref, field, far_rows = refs[5:]
    else:
        others, (total_ref, field, far_rows, out_ref) = refs[5 : 5 + earlier], refs[5 + earlier :]
    columns = out_ref.shape[0]
    step = pl.program_id(0)

    @pl.when(step == 0)
    def _():
        def two_pairs(p, carry):
            sides = []
            for side in range(2):
                sides.append(
                    jnp.concatenate(
                        [b[:, 2 * p + side].reshape(b.shape[0] * 16, LANES) for b in blocks], axis=0
                    )
                )
            both = jnp.concatenate(sides, axis=1)
            for parity in range(2):
                got = jnp.dot(
                    phase_ref[2 * n_q * parity : 2 * n_q * (parity + 1), :],
                    both,
                    preferred_element_type=F32,
                )
                for side in range(2):
                    column = 4 * p + 2 * side + parity
                    field[pl.ds(pl.multiple_of(column * COL_STRIDE, SUB), 2 * n_q), :] = got[
                        :, side * LANES : (side + 1) * LANES
                    ]
            return carry

        lax.fori_loop(0, columns // 4, two_pairs, 0, unroll=PHASE_UNROLL)
        far = (mine_ref[0, 0:16, :] + theirs_ref[0, 0:16, :]) * SCALE
        for unit in range(columns // (N_THIRD * SUB)):
            k, m_half = divmod(first_group // N_THIRD + unit, M_HALF)
            for side in range(2):
                m = 2 * m_half + side
                line = far[m : m + 1, k * LANES : (k + 1) * LANES]
                turned = jnp.transpose(jnp.broadcast_to(line, (LANES, LANES)))
                for j in range(4):
                    row = unit * SUB + side * 4 + j
                    far_rows[pl.ds(row * D_STRIDE, LANES), :] = turned

    lane = lax.broadcasted_iota(jnp.int32, (columns, LANES), 1)
    units = columns // (N_THIRD * SUB)
    nears = []
    for unit in range(units):
        k = (first_group // N_THIRD + unit) // M_HALF
        nears.append(near_ref[k * N_THIRD * SUB : (k + 1) * N_THIRD * SUB, :])
    near = jnp.concatenate(nears, axis=0).reshape(units, N_THIRD, SUB, LANES)

    def some_q(i, carry):
        rotated = []
        for j in range(UNROLL):
            q = step * Q_BLOCK + i * UNROLL + j
            real = field[pl.ds(q, columns, stride=COL_STRIDE), :].astype(BF16)
            imag = field[pl.ds(q + n_q, columns, stride=COL_STRIDE), :].astype(BF16)
            mode = mode_ref[i * UNROLL + j]
            turn = jnp.concatenate([-mode[:, LANES:], mode[:, :LANES]], axis=1)
            rotated.append(
                jnp.dot(
                    jnp.concatenate([real, imag], axis=1),
                    jnp.concatenate([mode, turn], axis=0),
                    preferred_element_type=F32,
                )
            )
        out = out_ref[...]
        for j in range(UNROLL):
            q = step * Q_BLOCK + i * UNROLL + j
            far = far_rows[pl.ds(q, units * SUB, stride=D_STRIDE), :]
            gap = (near - far.reshape(units, 1, SUB, LANES)).reshape(columns, LANES)
            w = freq_ref[pl.ds(q, 1), :]
            plus, minus = gap + w, gap - w
            weight = jnp.exp2(freq_ref[pl.ds(n_q + q, 1), :] - plus * plus) + jnp.exp2(
                freq_ref[pl.ds(2 * n_q + q, 1), :] - minus * minus
            )
            real, imag = rotated[j][:, :LANES], rotated[j][:, LANES:]
            terms = (real * real + imag * imag) * weight
            out = jnp.where(lane == q, jnp.sum(terms, axis=1, keepdims=True), out)
        out_ref[...] = out
        return carry

    lax.fori_loop(0, Q_BLOCK // UNROLL, some_q, 0)

    if earlier is not None:

        @pl.when(step == pl.num_programs(0) - 1)
        def _():
            got = totals(mine_ref[0] + theirs_ref[0], [*others, out_ref], total_ref.shape[1:])
            for i in range(total_ref.shape[0]):
                total_ref[i] = got


def columns_of(index, phase, blocks, mode, near, mine, theirs, freq, others=None):
    n_q = mode.shape[0]
    first, groups = PARTS[index]
    columns = SUB * groups
    fixed = lambda shape: pl.BlockSpec(shape, lambda s: (0,) * len(shape))
    operands = [phase, *blocks]
    rest = [near, mine, theirs, freq, *(others or [])]
    sums = (columns, LANES)
    out = sums if others is None else (N_INTERP, SUB, 2 * LANES)
    return pl.pallas_call(
        functools.partial(
            columns_kernel, first, len(blocks), n_q, None if others is None else len(others)
        ),
        grid=(n_q // Q_BLOCK,),
        out_shape=jax.ShapeDtypeStruct(out, F32),
        in_specs=[fixed(o.shape) for o in operands]
        + [pl.BlockSpec((Q_BLOCK, LANES, 2 * LANES), lambda s: (s, 0, 0))]
        + [fixed(o.shape) for o in rest],
        out_specs=fixed(out),
        scratch_shapes=[
            pltpu.VMEM((columns * COL_STRIDE, LANES), F32),
            pltpu.VMEM((columns // N_THIRD * D_STRIDE, LANES), F32),
        ]
        + ([] if others is None else [pltpu.VMEM(sums, F32)]),
        compiler_params=params(),
        cost_estimate=cost(1e5, 1e5),
        name="columns",
    )(*operands, mode, *rest)


def interp_pairs(dz, dy):
    return [
        (z * NY + y, (z + dz) % NZ * NY + (y + dy) % NY) for z in range(NZ) for y in range(NY)
    ]


def bte_pairs(dh, dx, dc):
    return [
        ((h * NX + x) * 2 + c, ((h + dh) % 2 * NX + (x + dx) % NX) * 2 + (c + dc) % 2)
        for h in range(2)
        for x in range(NX)
        for c in range(2)
    ]


def along_interp(value, dz, dy):
    return lax.ppermute(value, "interp", interp_pairs(dz, dy))


def along_bte(value, dh, dx, dc):
    return lax.ppermute(value, "bte", bte_pairs(dh, dx, dc))


def after(value, *others):
    return lax.optimization_barrier((value, *others))[0]


def ring_of(own, *before):
    one, three = along_interp(own, 1, 0), along_interp(own, -1, 0)
    return own, one, along_interp(after(one, *before) if before else one, 1, 0), three


def both_ways(own):
    return along_interp(own, 0, 1), along_interp(own, 0, -1)


def local(
    coupling,
    rvectors,
    qpoints,
    polarization,
    frequencies,
    kbatch,
    kq_owner,
    kq_row,
    energy,
    band_mask,
    deviation,
    velocity,
    impurity,
):
    n_q = qpoints.shape[0]
    nbands = energy.shape[1]
    nmodes = frequencies.shape[1]
    q_total = n_q * lax.axis_size("interp")
    columns = coupling.shape[3]

    planes = jnp.swapaxes(coupling, 2, 3).reshape(-1, columns, nmodes)
    *own_parts, own_table, ids, near = prepare(
        kbatch,
        planes,
        energy.T,
        band_mask.T,
        jnp.transpose(deviation, (1, 2, 0)),
        kq_owner.reshape(1, -1),
        kq_row.reshape(1, -1),
    )
    own_first, own_second = own_parts

    other_ids = along_bte(ids, 1, 0, 0)
    phase, freq = tables(q_total, *after((qpoints.T, rvectors.T, frequencies.T), ids))
    first = ring_of(own_first, freq, other_ids)
    other_table = along_bte(own_table, 0, 0, 1)
    second = ring_of(after(own_second, freq))
    chip_table = jnp.stack([own_table, other_table])
    chip_table = after(chip_table, second[3])
    near_tables = [along_bte(chip_table, 0, dx, 0) for dx in (1, -1, 2)]

    first_mine = jnp.stack(first)
    first_up, first_down = both_ways(first_mine)

    pol = jnp.transpose(polarization, (1, 2, 3, 0)).reshape(2 * nmodes, nmodes, n_q)
    second_mine = after(jnp.stack(second), first_up, first_down, *near_tables)
    mode = modes(after(pol, second_mine))

    all_ids = jnp.concatenate([ids, other_ids], axis=1)
    found = lookup(after(all_ids, mode), [chip_table] + near_tables)
    mine, theirs = found, along_bte(found[1:], 1, 0, 0)

    first_far = along_interp(first_up[:2], 0, 1), along_interp(first_down[2:], 0, -1)
    second_up, second_down = both_ways(second_mine)
    second_far = (
        along_interp(after(second_up, *first_far, theirs)[:2], 0, 1),
        along_interp(after(second_down, *first_far, theirs)[2:], 0, -1),
    )

    rest = (mode, near, mine, theirs, freq)
    sums = columns_of(0, phase, (first_mine, first_up, first_down, *first_far), *rest)
    total = columns_of(
        1, phase, (second_mine, second_up, second_down, *second_far), *rest, others=[sums]
    )
    near_mask = band_mask[kbatch].astype(F32)

    total = lax.all_to_all(total, "interp", 0, 0, tiled=True)[:, 0].sum(axis=0)
    total = total[: 4 * 48].reshape(4, 2, N_THIRD, 2, 4).sum(axis=3).reshape(4, 2, nbands)
    scatter_rate = total[0]
    inflow = jnp.transpose(total[1:], (1, 0, 2))
    return near_mask[:, None, :] * (velocity + inflow) / (scatter_rate + impurity)[:, None, :]


def solution(mesh):
    in_specs = (
        P(None, "interp", None, "bte"),
        P(),
        P("interp", None),
        P("interp", None, None, None),
        P("interp", None),
        P("bte"),
        P(("interp", "bte"), None),
        P(("interp", "bte")),
        P("bte", None),
        P("bte", None),
        P("bte", None, None),
        P("bte", None, None),
        P("bte", None),
    )
    out_specs = P("bte", None, None)
    return jax.shard_map(local, mesh=mesh, in_specs=in_specs, out_specs=out_specs, check_vma=False)
```

```python
import functools

import jax
import jax.numpy as jnp
from jax import lax
from jax.experimental import pallas as pl
from jax.experimental.pallas import tpu as pltpu
from jax.sharding import PartitionSpec as P

GRID = 160
SMEARING = 0.5
THERMAL = 0.3
LOG2_E = 1.4426950408889634
SCALE = (LOG2_E / (2.0 * SMEARING**2)) ** 0.5

BF16 = jnp.bfloat16
F32 = jnp.float32
LANES = 128
SUB = 8
VMEM_LIMIT = 58 * 1024 * 1024

NZ, NY, NX = 4, 4, 4
N_INTERP = NZ * NY

M_HALF, N_THIRD = 6, 3
GROUPS = 2 * M_HALF * N_THIRD
PARTS = ((0, 12), (12, 24))

Q_BLOCK = 16
COL_STRIDE = 264
D_STRIDE = 136
D_BLOCK = 30
UNROLL = 16
PHASE_UNROLL = 3


def params():
    return pltpu.CompilerParams(vmem_limit_bytes=VMEM_LIMIT)


def whole(memory_space=pltpu.VMEM):
    return pl.BlockSpec(memory_space=memory_space)


def cost(flops, bytes_accessed, transcendentals=0):
    return pl.CostEstimate(
        flops=int(flops), bytes_accessed=int(bytes_accessed), transcendentals=int(transcendentals)
    )


def prepare_kernel(kbatch_ref, x_ref, energy_ref, mask_ref, dev_ref, owner_ref, row_ref, *refs):
    outs, (table, ids, near, rows) = refs[:-4], refs[-4:]
    planes, columns, nd = x_ref.shape
    bands, rows_own = energy_ref.shape
    stride = columns + SUB
    for j in range(planes):
        rows[pl.ds(j * stride, columns), 0:nd] = x_ref[j].astype(F32)
    keep = lax.broadcasted_iota(jnp.int32, (2 * SUB, LANES), 1) < nd
    for out, (first, count) in zip(outs, PARTS):
        for g in range(count):
            k, rest = divmod(first + g, M_HALF * N_THIRD)
            m_half, n_third = divmod(rest, N_THIRD)
            for pair in range(4):
                m = 2 * m_half + pair // 2
                n = 4 * n_third + 2 * (pair % 2)
                old = k * 144 + m * 12 + n
                one = rows[pl.ds(old, SUB, stride=stride), :]
                two = rows[pl.ds(old + 1, SUB, stride=stride), :]
                both = jnp.where(keep, jnp.concatenate([one, two], axis=0), 0.0)
                out[4 * g + pair] = both.astype(BF16)
    energies = energy_ref[...]
    mask = mask_ref[...].astype(F32)
    table[0:bands, :] = energies
    for c in range(3):
        table[(c + 1) * bands : (c + 2) * bands, :] = dev_ref[c] * mask
    ids[...] = owner_ref[...] * rows_own + row_ref[...]
    lane = lax.broadcasted_iota(jnp.int32, (bands, rows_own), 1)
    for k in range(2):
        line = jnp.sum(jnp.where(lane == kbatch_ref[k], energies, 0.0), axis=1, keepdims=True)
        line = jnp.broadcast_to(line * SCALE, (bands, LANES))
        for n_third in range(N_THIRD):
            some = line[4 * n_third : 4 * n_third + 4]
            first = (k * N_THIRD + n_third) * SUB
            near[first : first + SUB, :] = jnp.concatenate([some, some], axis=0)


def prepare(kbatch, planes, energy, mask, dev, owner, row):
    n, columns, _ = planes.shape
    bands, rows_own = energy.shape
    return pl.pallas_call(
        prepare_kernel,
        out_shape=[jax.ShapeDtypeStruct((4 * c, 16, LANES), BF16) for _, c in PARTS]
        + [
            jax.ShapeDtypeStruct((4 * bands, rows_own), F32),
            jax.ShapeDtypeStruct(owner.shape, jnp.int32),
            jax.ShapeDtypeStruct((2 * N_THIRD * SUB, LANES), F32),
        ],
        in_specs=[whole(pltpu.SMEM)] + [whole()] * 6,
        out_specs=[whole()] * (len(PARTS) + 3),
        scratch_shapes=[pltpu.VMEM((n * (columns + SUB), LANES), F32)],
        compiler_params=params(),
        cost_estimate=cost(1e5, 1e5),
        name="prepare",
    )(kbatch, planes, energy, mask, dev, owner, row)


def tables_kernel(n_q_total, q_ref, vec_ref, freq_ref, out, freq_out):
    n_q = q_ref.shape[1]
    own = lax.axis_index("interp")
    z, y = own // NY, own % NY
    points = [
        jnp.transpose(jnp.broadcast_to(q_ref[c : c + 1, :].astype(F32), (LANES, n_q)))
        for c in range(3)
    ]
    points = [jnp.concatenate([p, p], axis=1) for p in points]
    vectors = vec_ref[...].astype(F32).astype(BF16)
    lane = lax.broadcasted_iota(jnp.int32, (1, 2 * LANES), 1)
    block, parity, part, vector = lane // 16, lane // 8 % 2, lane // 4 % 2, lane % 4
    number = lax.broadcasted_iota(jnp.int32, (vec_ref.shape[1], 2 * LANES), 0)
    dz, turn = block % 4, block // 4
    dy = jnp.where(turn == 2, 3, jnp.where(turn == 3, 2, turn))
    source = (z - dz + NZ) % NZ * NY + (y - dy + NY) % NY
    pick = jnp.where(number == source * 4 + vector, 1.0, 0.0).astype(BF16)
    chosen = jnp.dot(vectors, pick, preferred_element_type=F32)
    product = sum(points[c] * chosen[c : c + 1, :] for c in range(3))
    product = product + (part * (GRID // 4)).astype(F32)
    for row, turned in enumerate((product, product - GRID // 4)):
        turned = turned - GRID * jnp.floor((turned + 0.5) * (1.0 / GRID))
        value = jnp.cos((2.0 * jnp.pi / GRID) * turned)
        for side in range(2):
            first = (2 * side + row) * n_q
            out[first : first + n_q, :] = jnp.where(parity == side, value, 0.0).astype(BF16)
    modes = freq_ref.shape[0]
    w = jnp.concatenate([freq_ref[...], jnp.ones((LANES - modes, n_q), F32)], axis=0)
    w = jnp.transpose(w)
    occupy = 1.0 / (jnp.exp(w / THERMAL) - 1.0)
    share = 1.0 / (w * n_q_total)
    freq_out[0:n_q, :] = w * SCALE
    freq_out[n_q : 2 * n_q, :] = jnp.log(occupy * share) * LOG2_E
    freq_out[2 * n_q : 3 * n_q, :] = jnp.log((occupy + 1.0) * share) * LOG2_E


def tables(n_q_total, points, vectors, freq):
    n_q = points.shape[1]
    return pl.pallas_call(
        functools.partial(tables_kernel, n_q_total),
        out_shape=[
            jax.ShapeDtypeStruct((4 * n_q, 2 * LANES), BF16),
            jax.ShapeDtypeStruct((3 * n_q, LANES), F32),
        ],
        in_specs=[whole()] * 3,
        out_specs=[whole()] * 2,
        compiler_params=params(),
        cost_estimate=cost(1e5, 1e5),
        name="tables",
    )(points, vectors, freq)


def modes_kernel(nd, nu, turn_steps, pol_ref, out_ref, rows):
    step = pl.program_id(0)

    @pl.when(step < turn_steps)
    def _():
        pad = jnp.zeros((LANES - nu, LANES), F32)

        def one(t, carry):
            plane = jnp.concatenate([pol_ref[t].astype(F32), pad], axis=0)
            first = pl.multiple_of((step * D_BLOCK + t) * D_STRIDE, SUB)
            rows[pl.ds(first, LANES), :] = jnp.transpose(plane)
            return carry

        lax.fori_loop(0, D_BLOCK, one, 0, unroll=10)

    @pl.when(step >= turn_steps)
    def _():
        pad = jnp.zeros((LANES - nd, LANES), F32)

        def one_q(i, carry):
            q = (step - turn_steps) * Q_BLOCK + i
            real = rows[pl.ds(q, nd, stride=D_STRIDE), :]
            imag = rows[pl.ds(nd * D_STRIDE + q, nd, stride=D_STRIDE), :]
            out_ref[i, :, 0:LANES] = jnp.concatenate([real, pad], axis=0).astype(BF16)
            out_ref[i, :, LANES:] = jnp.concatenate([imag, pad], axis=0).astype(BF16)
            return carry

        lax.fori_loop(0, Q_BLOCK, one_q, 0, unroll=4)


def modes(pol):
    planes, nu, n_q = pol.shape
    nd = planes // 2
    turn_steps = planes // D_BLOCK
    return pl.pallas_call(
        functools.partial(modes_kernel, nd, nu, turn_steps),
        grid=(turn_steps + n_q // Q_BLOCK,),
        out_shape=jax.ShapeDtypeStruct((n_q, LANES, 2 * LANES), BF16),
        in_specs=[
            pl.BlockSpec((D_BLOCK, nu, n_q), lambda s: (jnp.minimum(s, turn_steps - 1), 0, 0))
        ],
        out_specs=pl.BlockSpec(
            (Q_BLOCK, LANES, 2 * LANES), lambda s: (jnp.maximum(s - turn_steps, 0), 0, 0)
        ),
        scratch_shapes=[pltpu.VMEM((planes * D_STRIDE, LANES), F32)],
        compiler_params=params(),
        cost_estimate=cost(1e5, 1e5),
        name="modes",
    )(pol)


def lookup_kernel(ids_ref, *refs):
    out = refs[-1]
    n_rows = refs[0].shape[-1]
    me = lax.axis_index("bte")
    half, x, core = me // (2 * NX), me // 2 % NX, me % 2
    ids = ids_ref[...]
    wanted = ids.shape[1]
    row = lax.broadcasted_iota(jnp.int32, (n_rows, wanted), 0)
    total = None
    for ref, dx in zip(refs[:-1], (0, 1, -1, 2)):
        for dc in range(2):
            owner = (half * NX + (x - dx + NX) % NX) * 2 + (core + dc) % 2
            table = ref[dc]
            high = table.astype(BF16)
            rest = table - high.astype(F32)
            middle = rest.astype(BF16)
            low = (rest - middle.astype(F32)).astype(BF16)
            pick = jnp.where(row == ids - owner * n_rows, 1.0, 0.0).astype(BF16)
            got = jnp.dot(
                jnp.concatenate([high, middle, low], axis=0), pick, preferred_element_type=F32
            )
            total = got if total is None else total + got
    n = refs[0].shape[1]
    found = (total[2 * n :] + total[n : 2 * n]) + total[:n]
    out[0] = found[:, : wanted // 2]
    out[1] = found[:, wanted // 2 :]


def lookup(ids, tables):
    n = tables[0].shape[1]
    return pl.pallas_call(
        lookup_kernel,
        out_shape=jax.ShapeDtypeStruct((2, n, ids.shape[1] // 2), F32),
        in_specs=[whole()] * (1 + len(tables)),
        out_specs=whole(),
        compiler_params=params(),
        cost_estimate=cost(1e5, 1e5),
        name="lookup",
    )(ids, *tables)


def totals(got, parts, shape):
    upper = lax.broadcasted_iota(jnp.int32, (SUB, LANES), 0) < 4
    sums = {}
    g = 0
    for part in parts:
        for at in range(part.shape[0] // SUB):
            k, rest = divmod(g, M_HALF * N_THIRD)
            m_half, n_third = divmod(rest, N_THIRD)
            kernel = part[at * SUB : (at + 1) * SUB, :]
            for j in range(4):
                term = kernel
                if j:
                    line = j * 12 + 2 * m_half
                    lanes = slice(k * LANES, (k + 1) * LANES)
                    term = kernel * jnp.where(
                        upper,
                        jnp.broadcast_to(got[line : line + 1, lanes], (SUB, LANES)),
                        jnp.broadcast_to(got[line + 1 : line + 2, lanes], (SUB, LANES)),
                    )
                key = (j, k, n_third)
                sums[key] = sums[key] + term if key in sums else term
            g += 1
    stacked = jnp.concatenate([sums[key] for key in sorted(sums)], axis=0)
    pad = jnp.zeros((shape[1] - stacked.shape[0], LANES), F32)
    return lax.dot_general(
        jnp.ones((shape[0], LANES), F32),
        jnp.concatenate([stacked, pad], axis=0),
        (((1,), (1,)), ((), ())),
        preferred_element_type=F32,
        precision=lax.Precision.HIGHEST,
    )


def columns_kernel(first_group, n_blocks, n_q, earlier, *refs):
    phase_ref, blocks, refs = refs[0], refs[1 : 1 + n_blocks], refs[1 + n_blocks :]
    mode_ref, near_ref, mine_ref, theirs_ref, freq_ref = refs[:5]
    if earlier is None:
        out_ref, field, far_rows = refs[5:]
    else:
        others, (total_ref, field, far_rows, out_ref) = refs[5 : 5 + earlier], refs[5 + earlier :]
    columns = out_ref.shape[0]
    step = pl.program_id(0)

    @pl.when(step == 0)
    def _():
        def two_pairs(p, carry):
            sides = []
            for side in range(2):
                sides.append(
                    jnp.concatenate(
                        [b[:, 2 * p + side].reshape(b.shape[0] * 16, LANES) for b in blocks], axis=0
                    )
                )
            both = jnp.concatenate(sides, axis=1)
            for parity in range(2):
                got = jnp.dot(
                    phase_ref[2 * n_q * parity : 2 * n_q * (parity + 1), :],
                    both,
                    preferred_element_type=F32,
                )
                for side in range(2):
                    column = 4 * p + 2 * side + parity
                    field[pl.ds(pl.multiple_of(column * COL_STRIDE, SUB), 2 * n_q), :] = got[
                        :, side * LANES : (side + 1) * LANES
                    ]
            return carry

        lax.fori_loop(0, columns // 4, two_pairs, 0, unroll=PHASE_UNROLL)
        far = (mine_ref[0, 0:16, :] + theirs_ref[0, 0:16, :]) * SCALE
        for unit in range(columns // (N_THIRD * SUB)):
            k, m_half = divmod(first_group // N_THIRD + unit, M_HALF)
            for side in range(2):
                m = 2 * m_half + side
                line = far[m : m + 1, k * LANES : (k + 1) * LANES]
                turned = jnp.transpose(jnp.broadcast_to(line, (LANES, LANES)))
                for j in range(4):
                    row = unit * SUB + side * 4 + j
                    far_rows[pl.ds(row * D_STRIDE, LANES), :] = turned

    lane = lax.broadcasted_iota(jnp.int32, (columns, LANES), 1)
    units = columns // (N_THIRD * SUB)
    nears = []
    for unit in range(units):
        k = (first_group // N_THIRD + unit) // M_HALF
        nears.append(near_ref[k * N_THIRD * SUB : (k + 1) * N_THIRD * SUB, :])
    near = jnp.concatenate(nears, axis=0).reshape(units, N_THIRD, SUB, LANES)

    def some_q(i, carry):
        rotated = []
        for j in range(UNROLL):
            q = step * Q_BLOCK + i * UNROLL + j
            real = field[pl.ds(q, columns, stride=COL_STRIDE), :].astype(BF16)
            imag = field[pl.ds(q + n_q, columns, stride=COL_STRIDE), :].astype(BF16)
            mode = mode_ref[i * UNROLL + j]
            turn = jnp.concatenate([-mode[:, LANES:], mode[:, :LANES]], axis=1)
            rotated.append(
                jnp.dot(
                    jnp.concatenate([real, imag], axis=1),
                    jnp.concatenate([mode, turn], axis=0),
                    preferred_element_type=F32,
                )
            )
        out = out_ref[...]
        for j in range(UNROLL):
            q = step * Q_BLOCK + i * UNROLL + j
            far = far_rows[pl.ds(q, units * SUB, stride=D_STRIDE), :]
            gap = (near - far.reshape(units, 1, SUB, LANES)).reshape(columns, LANES)
            w = freq_ref[pl.ds(q, 1), :]
            plus, minus = gap + w, gap - w
            weight = jnp.exp2(freq_ref[pl.ds(n_q + q, 1), :] - plus * plus) + jnp.exp2(
                freq_ref[pl.ds(2 * n_q + q, 1), :] - minus * minus
            )
            real, imag = rotated[j][:, :LANES], rotated[j][:, LANES:]
            terms = (real * real + imag * imag) * weight
            out = jnp.where(lane == q, jnp.sum(terms, axis=1, keepdims=True), out)
        out_ref[...] = out
        return carry

    lax.fori_loop(0, Q_BLOCK // UNROLL, some_q, 0)

    if earlier is not None:

        @pl.when(step == pl.num_programs(0) - 1)
        def _():
            got = totals(mine_ref[0] + theirs_ref[0], [*others, out_ref], total_ref.shape[1:])
            for i in range(total_ref.shape[0]):
                total_ref[i] = got


def columns_of(index, phase, blocks, mode, near, mine, theirs, freq, others=None):
    n_q = mode.shape[0]
    first, groups = PARTS[index]
    columns = SUB * groups
    fixed = lambda shape: pl.BlockSpec(shape, lambda s: (0,) * len(shape))
    operands = [phase, *blocks]
    rest = [near, mine, theirs, freq, *(others or [])]
    sums = (columns, LANES)
    out = sums if others is None else (N_INTERP, SUB, 2 * LANES)
    return pl.pallas_call(
        functools.partial(
            columns_kernel, first, len(blocks), n_q, None if others is None else len(others)
        ),
        grid=(n_q // Q_BLOCK,),
        out_shape=jax.ShapeDtypeStruct(out, F32),
        in_specs=[fixed(o.shape) for o in operands]
        + [pl.BlockSpec((Q_BLOCK, LANES, 2 * LANES), lambda s: (s, 0, 0))]
        + [fixed(o.shape) for o in rest],
        out_specs=fixed(out),
        scratch_shapes=[
            pltpu.VMEM((columns * COL_STRIDE, LANES), F32),
            pltpu.VMEM((columns // N_THIRD * D_STRIDE, LANES), F32),
        ]
        + ([] if others is None else [pltpu.VMEM(sums, F32)]),
        compiler_params=params(),
        cost_estimate=cost(1e5, 1e5),
        name="columns",
    )(*operands, mode, *rest)


def interp_pairs(dz, dy):
    return [
        (z * NY + y, (z + dz) % NZ * NY + (y + dy) % NY) for z in range(NZ) for y in range(NY)
    ]


def bte_pairs(dh, dx, dc):
    return [
        ((h * NX + x) * 2 + c, ((h + dh) % 2 * NX + (x + dx) % NX) * 2 + (c + dc) % 2)
        for h in range(2)
        for x in range(NX)
        for c in range(2)
    ]


def along_interp(value, dz, dy):
    return lax.ppermute(value, "interp", interp_pairs(dz, dy))


def along_bte(value, dh, dx, dc):
    return lax.ppermute(value, "bte", bte_pairs(dh, dx, dc))


def after(value, *others):
    return lax.optimization_barrier((value, *others))[0]


def both_ways(own):
    return along_interp(own, 0, 1), along_interp(own, 0, -1)


def local(
    coupling,
    rvectors,
    qpoints,
    polarization,
    frequencies,
    kbatch,
    kq_owner,
    kq_row,
    energy,
    band_mask,
    deviation,
    velocity,
    impurity,
):
    n_q = qpoints.shape[0]
    nbands = energy.shape[1]
    nmodes = frequencies.shape[1]
    q_total = n_q * lax.axis_size("interp")
    columns = coupling.shape[3]

    planes = jnp.swapaxes(coupling, 2, 3).reshape(-1, columns, nmodes)
    *own_parts, own_table, ids, near = prepare(
        kbatch,
        planes,
        energy.T,
        band_mask.T,
        jnp.transpose(deviation, (1, 2, 0)),
        kq_owner.reshape(1, -1),
        kq_row.reshape(1, -1),
    )
    own_first, own_second = own_parts

    other_ids = along_bte(ids, 1, 0, 0)
    phase, freq = tables(q_total, *after((qpoints.T, rvectors.T, frequencies.T), ids))
    other_table = along_bte(own_table, 0, 0, 1)

    def behind(own, *before):
        one, three = along_interp(own, 1, 0), along_interp(own, -1, 0)
        two = along_interp(after(one, *before), 1, 0)
        return jnp.stack([own, one]), jnp.stack([two, three])

    first_near, first_late = behind(own_first, freq, other_ids)
    first_up, first_down = both_ways(first_near)
    second_near, second_late = behind(
        after(own_second, first_late, other_ids), first_up, first_down
    )
    late_up, late_down = both_ways(first_late)
    first_far = along_interp(first_up, 0, 1), along_interp(late_down, 0, -1)
    first = (first_near, first_late, first_up, late_up, first_down, late_down, *first_far)

    second_up, second_down = both_ways(after(second_near, first_late))
    second_late = after(second_late, first_up, first_down, late_up, late_down)
    second_late_up, second_late_down = both_ways(second_late)

    chip_table = after(jnp.stack([own_table, other_table]), second_late)
    near_tables = [along_bte(chip_table, 0, dx, 0) for dx in (1, -1, 2)]
    pol = jnp.transpose(polarization, (1, 2, 3, 0)).reshape(2 * nmodes, nmodes, n_q)
    mode = modes(after(pol, second_late))

    all_ids = jnp.concatenate([ids, other_ids], axis=1)
    found = lookup(
        after(all_ids, mode, second_late_up, second_down, *first_far), [chip_table] + near_tables
    )
    mine, theirs = found, along_bte(found[1:], 1, 0, 0)

    second_far = (
        along_interp(after(second_up, *first_far, found), 0, 1),
        along_interp(after(second_late_down, *first_far, found), 0, -1),
    )
    second = (
        second_near,
        second_late,
        second_up,
        second_late_up,
        second_down,
        second_late_down,
        *second_far,
    )

    rest = (mode, near, mine, theirs, freq)
    sums = columns_of(0, phase, first, *rest)
    total = columns_of(1, phase, second, *rest, others=[sums])
    near_mask = band_mask[kbatch].astype(F32)

    total = lax.all_to_all(total, "interp", 0, 0, tiled=True)[:, 0].sum(axis=0)
    total = total[: 4 * 48].reshape(4, 2, N_THIRD, 2, 4).sum(axis=3).reshape(4, 2, nbands)
    scatter_rate = total[0]
    inflow = jnp.transpose(total[1:], (1, 0, 2))
    return near_mask[:, None, :] * (velocity + inflow) / (scatter_rate + impurity)[:, None, :]


def solution(mesh):
    in_specs = (
        P(None, "interp", None, "bte"),
        P(),
        P("interp", None),
        P("interp", None, None, None),
        P("interp", None),
        P("bte"),
        P(("interp", "bte"), None),
        P(("interp", "bte")),
        P("bte", None),
        P("bte", None),
        P("bte", None, None),
        P("bte", None, None),
        P("bte", None),
    )
    out_specs = P("bte", None, None)
    return jax.shard_map(local, mesh=mesh, in_specs=in_specs, out_specs=out_specs, check_vma=False)
```

```python
import functools

import jax
import jax.numpy as jnp
from jax import lax
from jax.experimental import pallas as pl
from jax.experimental.pallas import tpu as pltpu
from jax.sharding import PartitionSpec as P

GRID = 160
SMEARING = 0.5
THERMAL = 0.3
LOG2_E = 1.4426950408889634
SCALE = (LOG2_E / (2.0 * SMEARING**2)) ** 0.5

BF16 = jnp.bfloat16
F32 = jnp.float32
LANES = 128
SUB = 8
VMEM_LIMIT = 58 * 1024 * 1024

NZ, NY, NX = 4, 4, 4
N_INTERP = NZ * NY

M_HALF, N_THIRD = 6, 3
GROUPS = 2 * M_HALF * N_THIRD
PARTS = ((0, 12), (12, 24))

Q_BLOCK = 16
COL_STRIDE = 264
D_STRIDE = 136
D_BLOCK = 30
UNROLL = 16
PHASE_UNROLL = 3


def params():
    return pltpu.CompilerParams(vmem_limit_bytes=VMEM_LIMIT)


def whole(memory_space=pltpu.VMEM):
    return pl.BlockSpec(memory_space=memory_space)


def cost(flops, bytes_accessed, transcendentals=0):
    return pl.CostEstimate(
        flops=int(flops), bytes_accessed=int(bytes_accessed), transcendentals=int(transcendentals)
    )


def prepare_kernel(kbatch_ref, x_ref, energy_ref, mask_ref, dev_ref, owner_ref, row_ref, *refs):
    outs, (table, ids, near, rows) = refs[:-4], refs[-4:]
    planes, columns, nd = x_ref.shape
    bands, rows_own = energy_ref.shape
    stride = columns + SUB
    for j in range(planes):
        rows[pl.ds(j * stride, columns), 0:nd] = x_ref[j].astype(F32)
    keep = lax.broadcasted_iota(jnp.int32, (2 * SUB, LANES), 1) < nd
    for out, (first, count) in zip(outs, PARTS):
        for g in range(count):
            k, rest = divmod(first + g, M_HALF * N_THIRD)
            m_half, n_third = divmod(rest, N_THIRD)
            for pair in range(4):
                m = 2 * m_half + pair // 2
                n = 4 * n_third + 2 * (pair % 2)
                old = k * 144 + m * 12 + n
                one = rows[pl.ds(old, SUB, stride=stride), :]
                two = rows[pl.ds(old + 1, SUB, stride=stride), :]
                both = jnp.where(keep, jnp.concatenate([one, two], axis=0), 0.0)
                out[4 * g + pair] = both.astype(BF16)
    energies = energy_ref[...]
    mask = mask_ref[...].astype(F32)
    table[0:bands, :] = energies
    for c in range(3):
        table[(c + 1) * bands : (c + 2) * bands, :] = dev_ref[c] * mask
    ids[...] = owner_ref[...] * rows_own + row_ref[...]
    lane = lax.broadcasted_iota(jnp.int32, (bands, rows_own), 1)
    for k in range(2):
        line = jnp.sum(jnp.where(lane == kbatch_ref[k], energies, 0.0), axis=1, keepdims=True)
        line = jnp.broadcast_to(line * SCALE, (bands, LANES))
        for n_third in range(N_THIRD):
            some = line[4 * n_third : 4 * n_third + 4]
            first = (k * N_THIRD + n_third) * SUB
            near[first : first + SUB, :] = jnp.concatenate([some, some], axis=0)


def prepare(kbatch, planes, energy, mask, dev, owner, row):
    n, columns, _ = planes.shape
    bands, rows_own = energy.shape
    return pl.pallas_call(
        prepare_kernel,
        out_shape=[jax.ShapeDtypeStruct((4 * c, 16, LANES), BF16) for _, c in PARTS]
        + [
            jax.ShapeDtypeStruct((4 * bands, rows_own), F32),
            jax.ShapeDtypeStruct(owner.shape, jnp.int32),
            jax.ShapeDtypeStruct((2 * N_THIRD * SUB, LANES), F32),
        ],
        in_specs=[whole(pltpu.SMEM)] + [whole()] * 6,
        out_specs=[whole()] * (len(PARTS) + 3),
        scratch_shapes=[pltpu.VMEM((n * (columns + SUB), LANES), F32)],
        compiler_params=params(),
        cost_estimate=cost(1e5, 1e5),
        name="prepare",
    )(kbatch, planes, energy, mask, dev, owner, row)


def tables_kernel(n_q_total, q_ref, vec_ref, freq_ref, out, freq_out):
    n_q = q_ref.shape[1]
    own = lax.axis_index("interp")
    z, y = own // NY, own % NY
    points = [
        jnp.transpose(jnp.broadcast_to(q_ref[c : c + 1, :].astype(F32), (LANES, n_q)))
        for c in range(3)
    ]
    points = [jnp.concatenate([p, p], axis=1) for p in points]
    vectors = vec_ref[...].astype(F32).astype(BF16)
    lane = lax.broadcasted_iota(jnp.int32, (1, 2 * LANES), 1)
    block, parity, part, vector = lane // 16, lane // 8 % 2, lane // 4 % 2, lane % 4
    number = lax.broadcasted_iota(jnp.int32, (vec_ref.shape[1], 2 * LANES), 0)
    dz, turn = block % 4, block // 4
    dy = jnp.where(turn == 2, 3, jnp.where(turn == 3, 2, turn))
    source = (z - dz + NZ) % NZ * NY + (y - dy + NY) % NY
    pick = jnp.where(number == source * 4 + vector, 1.0, 0.0).astype(BF16)
    chosen = jnp.dot(vectors, pick, preferred_element_type=F32)
    product = sum(points[c] * chosen[c : c + 1, :] for c in range(3))
    product = product + (part * (GRID // 4)).astype(F32)
    for row, turned in enumerate((product, product - GRID // 4)):
        turned = turned - GRID * jnp.floor((turned + 0.5) * (1.0 / GRID))
        value = jnp.cos((2.0 * jnp.pi / GRID) * turned)
        for side in range(2):
            first = (2 * side + row) * n_q
            out[first : first + n_q, :] = jnp.where(parity == side, value, 0.0).astype(BF16)
    modes = freq_ref.shape[0]
    w = jnp.concatenate([freq_ref[...], jnp.ones((LANES - modes, n_q), F32)], axis=0)
    w = jnp.transpose(w)
    occupy = 1.0 / (jnp.exp(w / THERMAL) - 1.0)
    share = 1.0 / (w * n_q_total)
    freq_out[0:n_q, :] = w * SCALE
    freq_out[n_q : 2 * n_q, :] = jnp.log(occupy * share) * LOG2_E
    freq_out[2 * n_q : 3 * n_q, :] = jnp.log((occupy + 1.0) * share) * LOG2_E


def tables(n_q_total, points, vectors, freq):
    n_q = points.shape[1]
    return pl.pallas_call(
        functools.partial(tables_kernel, n_q_total),
        out_shape=[
            jax.ShapeDtypeStruct((4 * n_q, 2 * LANES), BF16),
            jax.ShapeDtypeStruct((3 * n_q, LANES), F32),
        ],
        in_specs=[whole()] * 3,
        out_specs=[whole()] * 2,
        compiler_params=params(),
        cost_estimate=cost(1e5, 1e5),
        name="tables",
    )(points, vectors, freq)


def modes_kernel(nd, nu, turn_steps, pol_ref, out_ref, rows):
    step = pl.program_id(0)

    @pl.when(step < turn_steps)
    def _():
        pad = jnp.zeros((LANES - nu, LANES), F32)

        def one(t, carry):
            plane = jnp.concatenate([pol_ref[t].astype(F32), pad], axis=0)
            first = pl.multiple_of((step * D_BLOCK + t) * D_STRIDE, SUB)
            rows[pl.ds(first, LANES), :] = jnp.transpose(plane)
            return carry

        lax.fori_loop(0, D_BLOCK, one, 0, unroll=10)

    @pl.when(step >= turn_steps)
    def _():
        pad = jnp.zeros((LANES - nd, LANES), F32)

        def one_q(i, carry):
            q = (step - turn_steps) * Q_BLOCK + i
            real = rows[pl.ds(q, nd, stride=D_STRIDE), :]
            imag = rows[pl.ds(nd * D_STRIDE + q, nd, stride=D_STRIDE), :]
            out_ref[i, :, 0:LANES] = jnp.concatenate([real, pad], axis=0).astype(BF16)
            out_ref[i, :, LANES:] = jnp.concatenate([imag, pad], axis=0).astype(BF16)
            return carry

        lax.fori_loop(0, Q_BLOCK, one_q, 0, unroll=4)


def modes(pol):
    planes, nu, n_q = pol.shape
    nd = planes // 2
    turn_steps = planes // D_BLOCK
    return pl.pallas_call(
        functools.partial(modes_kernel, nd, nu, turn_steps),
        grid=(turn_steps + n_q // Q_BLOCK,),
        out_shape=jax.ShapeDtypeStruct((n_q, LANES, 2 * LANES), BF16),
        in_specs=[
            pl.BlockSpec((D_BLOCK, nu, n_q), lambda s: (jnp.minimum(s, turn_steps - 1), 0, 0))
        ],
        out_specs=pl.BlockSpec(
            (Q_BLOCK, LANES, 2 * LANES), lambda s: (jnp.maximum(s - turn_steps, 0), 0, 0)
        ),
        scratch_shapes=[pltpu.VMEM((planes * D_STRIDE, LANES), F32)],
        compiler_params=params(),
        cost_estimate=cost(1e5, 1e5),
        name="modes",
    )(pol)


def lookup_kernel(ids_ref, *refs):
    out = refs[-1]
    n_rows = refs[0].shape[-1]
    me = lax.axis_index("bte")
    half, x, core = me // (2 * NX), me // 2 % NX, me % 2
    ids = ids_ref[...]
    wanted = ids.shape[1]
    row = lax.broadcasted_iota(jnp.int32, (n_rows, wanted), 0)
    total = None
    for ref, dx in zip(refs[:-1], (0, 1, -1, 2)):
        for dc in range(2):
            owner = (half * NX + (x - dx + NX) % NX) * 2 + (core + dc) % 2
            table = ref[dc]
            high = table.astype(BF16)
            rest = table - high.astype(F32)
            middle = rest.astype(BF16)
            low = (rest - middle.astype(F32)).astype(BF16)
            pick = jnp.where(row == ids - owner * n_rows, 1.0, 0.0).astype(BF16)
            got = jnp.dot(
                jnp.concatenate([high, middle, low], axis=0), pick, preferred_element_type=F32
            )
            total = got if total is None else total + got
    n = refs[0].shape[1]
    found = (total[2 * n :] + total[n : 2 * n]) + total[:n]
    out[0] = found[:, : wanted // 2]
    out[1] = found[:, wanted // 2 :]


def lookup(ids, tables):
    n = tables[0].shape[1]
    return pl.pallas_call(
        lookup_kernel,
        out_shape=jax.ShapeDtypeStruct((2, n, ids.shape[1] // 2), F32),
        in_specs=[whole()] * (1 + len(tables)),
        out_specs=whole(),
        compiler_params=params(),
        cost_estimate=cost(1e5, 1e5),
        name="lookup",
    )(ids, *tables)


def totals(got, parts, shape):
    upper = lax.broadcasted_iota(jnp.int32, (SUB, LANES), 0) < 4
    sums = {}
    g = 0
    for part in parts:
        for at in range(part.shape[0] // SUB):
            k, rest = divmod(g, M_HALF * N_THIRD)
            m_half, n_third = divmod(rest, N_THIRD)
            kernel = part[at * SUB : (at + 1) * SUB, :]
            for j in range(4):
                term = kernel
                if j:
                    line = j * 12 + 2 * m_half
                    lanes = slice(k * LANES, (k + 1) * LANES)
                    term = kernel * jnp.where(
                        upper,
                        jnp.broadcast_to(got[line : line + 1, lanes], (SUB, LANES)),
                        jnp.broadcast_to(got[line + 1 : line + 2, lanes], (SUB, LANES)),
                    )
                key = (j, k, n_third)
                sums[key] = sums[key] + term if key in sums else term
            g += 1
    stacked = jnp.concatenate([sums[key] for key in sorted(sums)], axis=0)
    pad = jnp.zeros((shape[1] - stacked.shape[0], LANES), F32)
    return lax.dot_general(
        jnp.ones((shape[0], LANES), F32),
        jnp.concatenate([stacked, pad], axis=0),
        (((1,), (1,)), ((), ())),
        preferred_element_type=F32,
        precision=lax.Precision.HIGHEST,
    )


def columns_kernel(first_group, n_blocks, n_q, earlier, *refs):
    phase_ref, blocks, refs = refs[0], refs[1 : 1 + n_blocks], refs[1 + n_blocks :]
    mode_ref, near_ref, mine_ref, theirs_ref, freq_ref = refs[:5]
    if earlier is None:
        out_ref, field, far_rows = refs[5:]
    else:
        others, (total_ref, field, far_rows, out_ref) = refs[5 : 5 + earlier], refs[5 + earlier :]
    columns = out_ref.shape[0]
    step = pl.program_id(0)

    @pl.when(step == 0)
    def _():
        def two_pairs(p, carry):
            sides = []
            for side in range(2):
                sides.append(
                    jnp.concatenate(
                        [b[:, 2 * p + side].reshape(b.shape[0] * 16, LANES) for b in blocks], axis=0
                    )
                )
            both = jnp.concatenate(sides, axis=1)
            for parity in range(2):
                got = jnp.dot(
                    phase_ref[2 * n_q * parity : 2 * n_q * (parity + 1), :],
                    both,
                    preferred_element_type=F32,
                )
                for side in range(2):
                    column = 4 * p + 2 * side + parity
                    field[pl.ds(pl.multiple_of(column * COL_STRIDE, SUB), 2 * n_q), :] = got[
                        :, side * LANES : (side + 1) * LANES
                    ]
            return carry

        lax.fori_loop(0, columns // 4, two_pairs, 0, unroll=PHASE_UNROLL)
        far = (mine_ref[0, 0:16, :] + theirs_ref[0, 0:16, :]) * SCALE
        for unit in range(columns // (N_THIRD * SUB)):
            k, m_half = divmod(first_group // N_THIRD + unit, M_HALF)
            for side in range(2):
                m = 2 * m_half + side
                line = far[m : m + 1, k * LANES : (k + 1) * LANES]
                turned = jnp.transpose(jnp.broadcast_to(line, (LANES, LANES)))
                for j in range(4):
                    row = unit * SUB + side * 4 + j
                    far_rows[pl.ds(row * D_STRIDE, LANES), :] = turned

    lane = lax.broadcasted_iota(jnp.int32, (columns, LANES), 1)
    units = columns // (N_THIRD * SUB)
    nears = []
    for unit in range(units):
        k = (first_group // N_THIRD + unit) // M_HALF
        nears.append(near_ref[k * N_THIRD * SUB : (k + 1) * N_THIRD * SUB, :])
    near = jnp.concatenate(nears, axis=0).reshape(units, N_THIRD, SUB, LANES)

    def some_q(i, carry):
        rotated = []
        for j in range(UNROLL):
            q = step * Q_BLOCK + i * UNROLL + j
            real = field[pl.ds(q, columns, stride=COL_STRIDE), :].astype(BF16)
            imag = field[pl.ds(q + n_q, columns, stride=COL_STRIDE), :].astype(BF16)
            mode = mode_ref[i * UNROLL + j]
            turn = jnp.concatenate([-mode[:, LANES:], mode[:, :LANES]], axis=1)
            rotated.append(
                jnp.dot(
                    jnp.concatenate([real, imag], axis=1),
                    jnp.concatenate([mode, turn], axis=0),
                    preferred_element_type=F32,
                )
            )
        out = out_ref[...]
        for j in range(UNROLL):
            q = step * Q_BLOCK + i * UNROLL + j
            far = far_rows[pl.ds(q, units * SUB, stride=D_STRIDE), :]
            gap = (near - far.reshape(units, 1, SUB, LANES)).reshape(columns, LANES)
            w = freq_ref[pl.ds(q, 1), :]
            plus, minus = gap + w, gap - w
            weight = jnp.exp2(freq_ref[pl.ds(n_q + q, 1), :] - plus * plus) + jnp.exp2(
                freq_ref[pl.ds(2 * n_q + q, 1), :] - minus * minus
            )
            real, imag = rotated[j][:, :LANES], rotated[j][:, LANES:]
            terms = (real * real + imag * imag) * weight
            out = jnp.where(lane == q, jnp.sum(terms, axis=1, keepdims=True), out)
        out_ref[...] = out
        return carry

    lax.fori_loop(0, Q_BLOCK // UNROLL, some_q, 0)

    if earlier is not None:

        @pl.when(step == pl.num_programs(0) - 1)
        def _():
            got = totals(mine_ref[0] + theirs_ref[0], [*others, out_ref], total_ref.shape[1:])
            for i in range(total_ref.shape[0]):
                total_ref[i] = got


def columns_of(index, phase, blocks, mode, near, mine, theirs, freq, others=None):
    n_q = mode.shape[0]
    first, groups = PARTS[index]
    columns = SUB * groups
    fixed = lambda shape: pl.BlockSpec(shape, lambda s: (0,) * len(shape))
    operands = [phase, *blocks]
    rest = [near, mine, theirs, freq, *(others or [])]
    sums = (columns, LANES)
    out = sums if others is None else (N_INTERP, SUB, 2 * LANES)
    return pl.pallas_call(
        functools.partial(
            columns_kernel, first, len(blocks), n_q, None if others is None else len(others)
        ),
        grid=(n_q // Q_BLOCK,),
        out_shape=jax.ShapeDtypeStruct(out, F32),
        in_specs=[fixed(o.shape) for o in operands]
        + [pl.BlockSpec((Q_BLOCK, LANES, 2 * LANES), lambda s: (s, 0, 0))]
        + [fixed(o.shape) for o in rest],
        out_specs=fixed(out),
        scratch_shapes=[
            pltpu.VMEM((columns * COL_STRIDE, LANES), F32),
            pltpu.VMEM((columns // N_THIRD * D_STRIDE, LANES), F32),
        ]
        + ([] if others is None else [pltpu.VMEM(sums, F32)]),
        compiler_params=params(),
        cost_estimate=cost(1e5, 1e5),
        name="columns",
    )(*operands, mode, *rest)


def interp_pairs(dz, dy):
    return [
        (z * NY + y, (z + dz) % NZ * NY + (y + dy) % NY) for z in range(NZ) for y in range(NY)
    ]


def bte_pairs(dh, dx, dc):
    return [
        ((h * NX + x) * 2 + c, ((h + dh) % 2 * NX + (x + dx) % NX) * 2 + (c + dc) % 2)
        for h in range(2)
        for x in range(NX)
        for c in range(2)
    ]


def along_interp(value, dz, dy):
    return lax.ppermute(value, "interp", interp_pairs(dz, dy))


def along_bte(value, dh, dx, dc):
    return lax.ppermute(value, "bte", bte_pairs(dh, dx, dc))


def after(value, *others):
    return lax.optimization_barrier((value, *others))[0]


def both_ways(own):
    return along_interp(own, 0, 1), along_interp(own, 0, -1)


def local(
    coupling,
    rvectors,
    qpoints,
    polarization,
    frequencies,
    kbatch,
    kq_owner,
    kq_row,
    energy,
    band_mask,
    deviation,
    velocity,
    impurity,
):
    n_q = qpoints.shape[0]
    nbands = energy.shape[1]
    nmodes = frequencies.shape[1]
    q_total = n_q * lax.axis_size("interp")
    columns = coupling.shape[3]

    planes = jnp.swapaxes(coupling, 2, 3).reshape(-1, columns, nmodes)
    *own_parts, own_table, ids, near = prepare(
        kbatch,
        planes,
        energy.T,
        band_mask.T,
        jnp.transpose(deviation, (1, 2, 0)),
        kq_owner.reshape(1, -1),
        kq_row.reshape(1, -1),
    )
    own_first, own_second = own_parts

    other_ids = along_bte(ids, 1, 0, 0)
    phase, freq = tables(q_total, *after((qpoints.T, rvectors.T, frequencies.T), ids))
    other_table = along_bte(own_table, 0, 0, 1)

    def behind(own, *before):
        one, three = along_interp(own, 1, 0), along_interp(own, -1, 0)
        two = along_interp(after(one, *before), 1, 0)
        return jnp.stack([own, one]), jnp.stack([two, three])

    chip_table = jnp.stack([own_table, other_table])
    near_tables = [along_bte(chip_table, 0, dx, 0) for dx in (1, -1, 2)]

    first_near, first_late = behind(own_first, freq, other_ids)
    first_up, first_down = both_ways(first_near)
    late_up, late_down = both_ways(first_late)
    first_far = along_interp(first_up, 0, 1), along_interp(late_down, 0, -1)
    first = (first_near, first_late, first_up, late_up, first_down, late_down, *first_far)

    second_near, second_late = behind(
        after(own_second, first_late, other_ids), late_up, late_down, first_up, first_down, *near_tables
    )
    second_up, second_down = both_ways(after(second_near, first_up, late_down))
    second_late_up, second_late_down = both_ways(after(second_late, *first_far))

    pol = jnp.transpose(polarization, (1, 2, 3, 0)).reshape(2 * nmodes, nmodes, n_q)
    mode = modes(after(pol, second_late, *first_far))

    all_ids = jnp.concatenate([ids, other_ids], axis=1)
    found = lookup(after(all_ids, mode), [chip_table] + near_tables)
    mine, theirs = found, along_bte(found[1:], 1, 0, 0)

    second_far = (
        along_interp(after(second_up, *first_far, found), 0, 1),
        along_interp(after(second_late_down, *first_far, found), 0, -1),
    )
    second = (
        second_near,
        second_late,
        second_up,
        second_late_up,
        second_down,
        second_late_down,
        *second_far,
    )

    rest = (mode, near, mine, theirs, freq)
    sums = columns_of(0, phase, first, *rest)
    total = columns_of(1, phase, second, *rest, others=[sums])
    near_mask = band_mask[kbatch].astype(F32)

    total = lax.all_to_all(total, "interp", 0, 0, tiled=True)[:, 0].sum(axis=0)
    total = total[: 4 * 48].reshape(4, 2, N_THIRD, 2, 4).sum(axis=3).reshape(4, 2, nbands)
    scatter_rate = total[0]
    inflow = jnp.transpose(total[1:], (1, 0, 2))
    return near_mask[:, None, :] * (velocity + inflow) / (scatter_rate + impurity)[:, None, :]


def solution(mesh):
    in_specs = (
        P(None, "interp", None, "bte"),
        P(),
        P("interp", None),
        P("interp", None, None, None),
        P("interp", None),
        P("bte"),
        P(("interp", "bte"), None),
        P(("interp", "bte")),
        P("bte", None),
        P("bte", None),
        P("bte", None, None),
        P("bte", None, None),
        P("bte", None),
    )
    out_specs = P("bte", None, None)
    return jax.shard_map(local, mesh=mesh, in_specs=in_specs, out_specs=out_specs, check_vma=False)
```

```python
import functools

import jax
import jax.numpy as jnp
from jax import lax
from jax.experimental import pallas as pl
from jax.experimental.pallas import tpu as pltpu
from jax.sharding import PartitionSpec as P

GRID = 160
SMEARING = 0.5
THERMAL = 0.3
LOG2_E = 1.4426950408889634
SCALE = (LOG2_E / (2.0 * SMEARING**2)) ** 0.5

BF16 = jnp.bfloat16
F32 = jnp.float32
LANES = 128
SUB = 8
VMEM_LIMIT = 58 * 1024 * 1024

NZ, NY, NX = 4, 4, 4
N_INTERP = NZ * NY

M_HALF, N_THIRD = 6, 3
GROUPS = 2 * M_HALF * N_THIRD
PARTS = ((0, 12), (12, 24))

Q_BLOCK = 16
COL_STRIDE = 264
D_STRIDE = 136
D_BLOCK = 30
UNROLL = 16
PHASE_UNROLL = 3


def params():
    return pltpu.CompilerParams(vmem_limit_bytes=VMEM_LIMIT)


def whole(memory_space=pltpu.VMEM):
    return pl.BlockSpec(memory_space=memory_space)


def cost(flops, bytes_accessed, transcendentals=0):
    return pl.CostEstimate(
        flops=int(flops), bytes_accessed=int(bytes_accessed), transcendentals=int(transcendentals)
    )


def prepare_kernel(kbatch_ref, x_ref, energy_ref, mask_ref, dev_ref, owner_ref, row_ref, *refs):
    outs, (table, ids, near, rows) = refs[:-4], refs[-4:]
    planes, columns, nd = x_ref.shape
    bands, rows_own = energy_ref.shape
    stride = columns + SUB
    for j in range(planes):
        rows[pl.ds(j * stride, columns), 0:nd] = x_ref[j].astype(F32)
    keep = lax.broadcasted_iota(jnp.int32, (2 * SUB, LANES), 1) < nd
    for out, (first, count) in zip(outs, PARTS):
        for g in range(count):
            k, rest = divmod(first + g, M_HALF * N_THIRD)
            m_half, n_third = divmod(rest, N_THIRD)
            for pair in range(4):
                m = 2 * m_half + pair // 2
                n = 4 * n_third + 2 * (pair % 2)
                old = k * 144 + m * 12 + n
                one = rows[pl.ds(old, SUB, stride=stride), :]
                two = rows[pl.ds(old + 1, SUB, stride=stride), :]
                both = jnp.where(keep, jnp.concatenate([one, two], axis=0), 0.0)
                out[4 * g + pair] = both.astype(BF16)
    energies = energy_ref[...]
    mask = mask_ref[...].astype(F32)
    table[0:bands, :] = energies
    for c in range(3):
        table[(c + 1) * bands : (c + 2) * bands, :] = dev_ref[c] * mask
    ids[...] = owner_ref[...] * rows_own + row_ref[...]
    lane = lax.broadcasted_iota(jnp.int32, (bands, rows_own), 1)
    for k in range(2):
        line = jnp.sum(jnp.where(lane == kbatch_ref[k], energies, 0.0), axis=1, keepdims=True)
        line = jnp.broadcast_to(line * SCALE, (bands, LANES))
        for n_third in range(N_THIRD):
            some = line[4 * n_third : 4 * n_third + 4]
            first = (k * N_THIRD + n_third) * SUB
            near[first : first + SUB, :] = jnp.concatenate([some, some], axis=0)


def prepare(kbatch, planes, energy, mask, dev, owner, row):
    n, columns, _ = planes.shape
    bands, rows_own = energy.shape
    return pl.pallas_call(
        prepare_kernel,
        out_shape=[jax.ShapeDtypeStruct((4 * c, 16, LANES), BF16) for _, c in PARTS]
        + [
            jax.ShapeDtypeStruct((4 * bands, rows_own), F32),
            jax.ShapeDtypeStruct(owner.shape, jnp.int32),
            jax.ShapeDtypeStruct((2 * N_THIRD * SUB, LANES), F32),
        ],
        in_specs=[whole(pltpu.SMEM)] + [whole()] * 6,
        out_specs=[whole()] * (len(PARTS) + 3),
        scratch_shapes=[pltpu.VMEM((n * (columns + SUB), LANES), F32)],
        compiler_params=params(),
        cost_estimate=cost(1e5, 1e5),
        name="prepare",
    )(kbatch, planes, energy, mask, dev, owner, row)


def tables_kernel(n_q_total, q_ref, vec_ref, freq_ref, out, freq_out):
    n_q = q_ref.shape[1]
    own = lax.axis_index("interp")
    z, y = own // NY, own % NY
    points = [
        jnp.transpose(jnp.broadcast_to(q_ref[c : c + 1, :].astype(F32), (LANES, n_q)))
        for c in range(3)
    ]
    points = [jnp.concatenate([p, p], axis=1) for p in points]
    vectors = vec_ref[...].astype(F32).astype(BF16)
    lane = lax.broadcasted_iota(jnp.int32, (1, 2 * LANES), 1)
    block, parity, part, vector = lane // 16, lane // 8 % 2, lane // 4 % 2, lane % 4
    number = lax.broadcasted_iota(jnp.int32, (vec_ref.shape[1], 2 * LANES), 0)
    dz, turn = block % 4, block // 4
    dy = jnp.where(turn == 2, 3, jnp.where(turn == 3, 2, turn))
    source = (z - dz + NZ) % NZ * NY + (y - dy + NY) % NY
    pick = jnp.where(number == source * 4 + vector, 1.0, 0.0).astype(BF16)
    chosen = jnp.dot(vectors, pick, preferred_element_type=F32)
    product = sum(points[c] * chosen[c : c + 1, :] for c in range(3))
    product = product + (part * (GRID // 4)).astype(F32)
    for row, turned in enumerate((product, product - GRID // 4)):
        turned = turned - GRID * jnp.floor((turned + 0.5) * (1.0 / GRID))
        value = jnp.cos((2.0 * jnp.pi / GRID) * turned)
        for side in range(2):
            first = (2 * side + row) * n_q
            out[first : first + n_q, :] = jnp.where(parity == side, value, 0.0).astype(BF16)
    modes = freq_ref.shape[0]
    w = jnp.concatenate([freq_ref[...], jnp.ones((LANES - modes, n_q), F32)], axis=0)
    w = jnp.transpose(w)
    occupy = 1.0 / (jnp.exp(w / THERMAL) - 1.0)
    share = 1.0 / (w * n_q_total)
    freq_out[0:n_q, :] = w * SCALE
    freq_out[n_q : 2 * n_q, :] = jnp.log(occupy * share) * LOG2_E
    freq_out[2 * n_q : 3 * n_q, :] = jnp.log((occupy + 1.0) * share) * LOG2_E


def tables(n_q_total, points, vectors, freq):
    n_q = points.shape[1]
    return pl.pallas_call(
        functools.partial(tables_kernel, n_q_total),
        out_shape=[
            jax.ShapeDtypeStruct((4 * n_q, 2 * LANES), BF16),
            jax.ShapeDtypeStruct((3 * n_q, LANES), F32),
        ],
        in_specs=[whole()] * 3,
        out_specs=[whole()] * 2,
        compiler_params=params(),
        cost_estimate=cost(1e5, 1e5),
        name="tables",
    )(points, vectors, freq)


def modes_kernel(nd, nu, turn_steps, pol_ref, out_ref, rows):
    step = pl.program_id(0)

    @pl.when(step < turn_steps)
    def _():
        pad = jnp.zeros((LANES - nu, LANES), F32)

        def one(t, carry):
            plane = jnp.concatenate([pol_ref[t].astype(F32), pad], axis=0)
            first = pl.multiple_of((step * D_BLOCK + t) * D_STRIDE, SUB)
            rows[pl.ds(first, LANES), :] = jnp.transpose(plane)
            return carry

        lax.fori_loop(0, D_BLOCK, one, 0, unroll=10)

    @pl.when(step >= turn_steps)
    def _():
        pad = jnp.zeros((LANES - nd, LANES), F32)

        def one_q(i, carry):
            q = (step - turn_steps) * Q_BLOCK + i
            real = rows[pl.ds(q, nd, stride=D_STRIDE), :]
            imag = rows[pl.ds(nd * D_STRIDE + q, nd, stride=D_STRIDE), :]
            out_ref[i, :, 0:LANES] = jnp.concatenate([real, pad], axis=0).astype(BF16)
            out_ref[i, :, LANES:] = jnp.concatenate([imag, pad], axis=0).astype(BF16)
            return carry

        lax.fori_loop(0, Q_BLOCK, one_q, 0, unroll=4)


def modes(pol):
    planes, nu, n_q = pol.shape
    nd = planes // 2
    turn_steps = planes // D_BLOCK
    return pl.pallas_call(
        functools.partial(modes_kernel, nd, nu, turn_steps),
        grid=(turn_steps + n_q // Q_BLOCK,),
        out_shape=jax.ShapeDtypeStruct((n_q, LANES, 2 * LANES), BF16),
        in_specs=[
            pl.BlockSpec((D_BLOCK, nu, n_q), lambda s: (jnp.minimum(s, turn_steps - 1), 0, 0))
        ],
        out_specs=pl.BlockSpec(
            (Q_BLOCK, LANES, 2 * LANES), lambda s: (jnp.maximum(s - turn_steps, 0), 0, 0)
        ),
        scratch_shapes=[pltpu.VMEM((planes * D_STRIDE, LANES), F32)],
        compiler_params=params(),
        cost_estimate=cost(1e5, 1e5),
        name="modes",
    )(pol)


def lookup_kernel(ids_ref, *refs):
    out = refs[-1]
    n_rows = refs[0].shape[-1]
    me = lax.axis_index("bte")
    half, x, core = me // (2 * NX), me // 2 % NX, me % 2
    ids = ids_ref[...]
    wanted = ids.shape[1]
    row = lax.broadcasted_iota(jnp.int32, (n_rows, wanted), 0)
    total = None
    for ref, dx in zip(refs[:-1], (0, 1, -1, 2)):
        for dc in range(2):
            owner = (half * NX + (x - dx + NX) % NX) * 2 + (core + dc) % 2
            table = ref[dc]
            high = table.astype(BF16)
            rest = table - high.astype(F32)
            middle = rest.astype(BF16)
            low = (rest - middle.astype(F32)).astype(BF16)
            pick = jnp.where(row == ids - owner * n_rows, 1.0, 0.0).astype(BF16)
            got = jnp.dot(
                jnp.concatenate([high, middle, low], axis=0), pick, preferred_element_type=F32
            )
            total = got if total is None else total + got
    n = refs[0].shape[1]
    found = (total[2 * n :] + total[n : 2 * n]) + total[:n]
    out[0] = found[:, : wanted // 2]
    out[1] = found[:, wanted // 2 :]


def lookup(ids, tables):
    n = tables[0].shape[1]
    return pl.pallas_call(
        lookup_kernel,
        out_shape=jax.ShapeDtypeStruct((2, n, ids.shape[1] // 2), F32),
        in_specs=[whole()] * (1 + len(tables)),
        out_specs=whole(),
        compiler_params=params(),
        cost_estimate=cost(1e5, 1e5),
        name="lookup",
    )(ids, *tables)


def totals(got, parts, shape):
    upper = lax.broadcasted_iota(jnp.int32, (SUB, LANES), 0) < 4
    sums = {}
    g = 0
    for part in parts:
        for at in range(part.shape[0] // SUB):
            k, rest = divmod(g, M_HALF * N_THIRD)
            m_half, n_third = divmod(rest, N_THIRD)
            kernel = part[at * SUB : (at + 1) * SUB, :]
            for j in range(4):
                term = kernel
                if j:
                    line = j * 12 + 2 * m_half
                    lanes = slice(k * LANES, (k + 1) * LANES)
                    term = kernel * jnp.where(
                        upper,
                        jnp.broadcast_to(got[line : line + 1, lanes], (SUB, LANES)),
                        jnp.broadcast_to(got[line + 1 : line + 2, lanes], (SUB, LANES)),
                    )
                key = (j, k, n_third)
                sums[key] = sums[key] + term if key in sums else term
            g += 1
    stacked = jnp.concatenate([sums[key] for key in sorted(sums)], axis=0)
    pad = jnp.zeros((shape[1] - stacked.shape[0], LANES), F32)
    return lax.dot_general(
        jnp.ones((shape[0], LANES), F32),
        jnp.concatenate([stacked, pad], axis=0),
        (((1,), (1,)), ((), ())),
        preferred_element_type=F32,
        precision=lax.Precision.HIGHEST,
    )


def columns_kernel(first_group, n_blocks, n_q, earlier, *refs):
    phase_ref, blocks, refs = refs[0], refs[1 : 1 + n_blocks], refs[1 + n_blocks :]
    mode_ref, near_ref, mine_ref, theirs_ref, freq_ref = refs[:5]
    if earlier is None:
        out_ref, field, far_rows = refs[5:]
    else:
        others, (total_ref, field, far_rows, out_ref) = refs[5 : 5 + earlier], refs[5 + earlier :]
    columns = out_ref.shape[0]
    step = pl.program_id(0)

    @pl.when(step == 0)
    def _():
        def two_pairs(p, carry):
            sides = []
            for side in range(2):
                sides.append(
                    jnp.concatenate(
                        [b[:, 2 * p + side].reshape(b.shape[0] * 16, LANES) for b in blocks], axis=0
                    )
                )
            both = jnp.concatenate(sides, axis=1)
            for parity in range(2):
                got = jnp.dot(
                    phase_ref[2 * n_q * parity : 2 * n_q * (parity + 1), :],
                    both,
                    preferred_element_type=F32,
                )
                for side in range(2):
                    column = 4 * p + 2 * side + parity
                    field[pl.ds(pl.multiple_of(column * COL_STRIDE, SUB), 2 * n_q), :] = got[
                        :, side * LANES : (side + 1) * LANES
                    ]
            return carry

        lax.fori_loop(0, columns // 4, two_pairs, 0, unroll=PHASE_UNROLL)
        far = (mine_ref[0, 0:16, :] + theirs_ref[0, 0:16, :]) * SCALE
        for unit in range(columns // (N_THIRD * SUB)):
            k, m_half = divmod(first_group // N_THIRD + unit, M_HALF)
            for side in range(2):
                m = 2 * m_half + side
                line = far[m : m + 1, k * LANES : (k + 1) * LANES]
                turned = jnp.transpose(jnp.broadcast_to(line, (LANES, LANES)))
                for j in range(4):
                    row = unit * SUB + side * 4 + j
                    far_rows[pl.ds(row * D_STRIDE, LANES), :] = turned

    lane = lax.broadcasted_iota(jnp.int32, (columns, LANES), 1)
    units = columns // (N_THIRD * SUB)
    nears = []
    for unit in range(units):
        k = (first_group // N_THIRD + unit) // M_HALF
        nears.append(near_ref[k * N_THIRD * SUB : (k + 1) * N_THIRD * SUB, :])
    near = jnp.concatenate(nears, axis=0).reshape(units, N_THIRD, SUB, LANES)

    def some_q(i, carry):
        rotated = []
        for j in range(UNROLL):
            q = step * Q_BLOCK + i * UNROLL + j
            real = field[pl.ds(q, columns, stride=COL_STRIDE), :].astype(BF16)
            imag = field[pl.ds(q + n_q, columns, stride=COL_STRIDE), :].astype(BF16)
            mode = mode_ref[i * UNROLL + j]
            turn = jnp.concatenate([-mode[:, LANES:], mode[:, :LANES]], axis=1)
            rotated.append(
                jnp.dot(
                    jnp.concatenate([real, imag], axis=1),
                    jnp.concatenate([mode, turn], axis=0),
                    preferred_element_type=F32,
                )
            )
        out = out_ref[...]
        for j in range(UNROLL):
            q = step * Q_BLOCK + i * UNROLL + j
            far = far_rows[pl.ds(q, units * SUB, stride=D_STRIDE), :]
            gap = (near - far.reshape(units, 1, SUB, LANES)).reshape(columns, LANES)
            w = freq_ref[pl.ds(q, 1), :]
            plus, minus = gap + w, gap - w
            weight = jnp.exp2(freq_ref[pl.ds(n_q + q, 1), :] - plus * plus) + jnp.exp2(
                freq_ref[pl.ds(2 * n_q + q, 1), :] - minus * minus
            )
            real, imag = rotated[j][:, :LANES], rotated[j][:, LANES:]
            terms = (real * real + imag * imag) * weight
            out = jnp.where(lane == q, jnp.sum(terms, axis=1, keepdims=True), out)
        out_ref[...] = out
        return carry

    lax.fori_loop(0, Q_BLOCK // UNROLL, some_q, 0)

    if earlier is not None:

        @pl.when(step == pl.num_programs(0) - 1)
        def _():
            got = totals(mine_ref[0] + theirs_ref[0], [*others, out_ref], total_ref.shape[1:])
            for i in range(total_ref.shape[0]):
                total_ref[i] = got


def columns_of(index, phase, blocks, mode, near, mine, theirs, freq, others=None):
    n_q = mode.shape[0]
    first, groups = PARTS[index]
    columns = SUB * groups
    fixed = lambda shape: pl.BlockSpec(shape, lambda s: (0,) * len(shape))
    operands = [phase, *blocks]
    rest = [near, mine, theirs, freq, *(others or [])]
    sums = (columns, LANES)
    out = sums if others is None else (N_INTERP, SUB, 2 * LANES)
    return pl.pallas_call(
        functools.partial(
            columns_kernel, first, len(blocks), n_q, None if others is None else len(others)
        ),
        grid=(n_q // Q_BLOCK,),
        out_shape=jax.ShapeDtypeStruct(out, F32),
        in_specs=[fixed(o.shape) for o in operands]
        + [pl.BlockSpec((Q_BLOCK, LANES, 2 * LANES), lambda s: (s, 0, 0))]
        + [fixed(o.shape) for o in rest],
        out_specs=fixed(out),
        scratch_shapes=[
            pltpu.VMEM((columns * COL_STRIDE, LANES), F32),
            pltpu.VMEM((columns // N_THIRD * D_STRIDE, LANES), F32),
        ]
        + ([] if others is None else [pltpu.VMEM(sums, F32)]),
        compiler_params=params(),
        cost_estimate=cost(1e5, 1e5),
        name="columns",
    )(*operands, mode, *rest)


def interp_pairs(dz, dy):
    return [
        (z * NY + y, (z + dz) % NZ * NY + (y + dy) % NY) for z in range(NZ) for y in range(NY)
    ]


def bte_pairs(dh, dx, dc):
    return [
        ((h * NX + x) * 2 + c, ((h + dh) % 2 * NX + (x + dx) % NX) * 2 + (c + dc) % 2)
        for h in range(2)
        for x in range(NX)
        for c in range(2)
    ]


def along_interp(value, dz, dy):
    return lax.ppermute(value, "interp", interp_pairs(dz, dy))


def along_bte(value, dh, dx, dc):
    return lax.ppermute(value, "bte", bte_pairs(dh, dx, dc))


def after(value, *others):
    return lax.optimization_barrier((value, *others))[0]


def both_ways(own):
    return along_interp(own, 0, 1), along_interp(own, 0, -1)


def local(
    coupling,
    rvectors,
    qpoints,
    polarization,
    frequencies,
    kbatch,
    kq_owner,
    kq_row,
    energy,
    band_mask,
    deviation,
    velocity,
    impurity,
):
    n_q = qpoints.shape[0]
    nbands = energy.shape[1]
    nmodes = frequencies.shape[1]
    q_total = n_q * lax.axis_size("interp")
    columns = coupling.shape[3]

    planes = jnp.swapaxes(coupling, 2, 3).reshape(-1, columns, nmodes)
    *own_parts, own_table, ids, near = prepare(
        kbatch,
        planes,
        energy.T,
        band_mask.T,
        jnp.transpose(deviation, (1, 2, 0)),
        kq_owner.reshape(1, -1),
        kq_row.reshape(1, -1),
    )
    own_first, own_second = own_parts

    other_ids = along_bte(ids, 1, 0, 0)
    phase, freq = tables(q_total, *after((qpoints.T, rvectors.T, frequencies.T), ids))
    other_table = along_bte(own_table, 0, 0, 1)

    def behind(own, *before):
        one, three = along_interp(own, 1, 0), along_interp(own, -1, 0)
        two = along_interp(after(one, *before), 1, 0)
        return jnp.stack([own, one]), jnp.stack([two, three])

    chip_table = jnp.stack([own_table, other_table])
    near_tables = [along_bte(chip_table, 0, dx, 0) for dx in (1, -1, 2)]

    all_ids = jnp.concatenate([ids, other_ids], axis=1)
    found = lookup(all_ids, [chip_table] + near_tables)
    mine, theirs = found, along_bte(found[1:], 1, 0, 0)

    first_near, first_late = behind(own_first, freq, other_ids)
    first_up, first_down = both_ways(first_near)
    late_up, late_down = both_ways(first_late)
    first_far = along_interp(first_up, 0, 1), along_interp(late_down, 0, -1)
    first = (first_near, first_late, first_up, late_up, first_down, late_down, *first_far)

    second_near, second_late = behind(
        after(own_second, first_late, other_ids), late_up, late_down, first_up, first_down, found
    )
    second_up, second_down = both_ways(after(second_near, first_up, late_down))
    second_late_up, second_late_down = both_ways(after(second_late, *first_far))

    pol = jnp.transpose(polarization, (1, 2, 3, 0)).reshape(2 * nmodes, nmodes, n_q)
    mode = modes(after(pol, second_late, *first_far))

    second_far = (
        along_interp(after(second_up, mode, theirs), 0, 1),
        along_interp(after(second_late_down, mode, theirs), 0, -1),
    )
    second = (
        second_near,
        second_late,
        second_up,
        second_late_up,
        second_down,
        second_late_down,
        *second_far,
    )

    rest = (mode, near, mine, theirs, freq)
    sums = columns_of(0, phase, first, *rest)
    total = columns_of(1, phase, second, *rest, others=[sums])
    near_mask = band_mask[kbatch].astype(F32)

    total = lax.all_to_all(total, "interp", 0, 0, tiled=True)[:, 0].sum(axis=0)
    total = total[: 4 * 48].reshape(4, 2, N_THIRD, 2, 4).sum(axis=3).reshape(4, 2, nbands)
    scatter_rate = total[0]
    inflow = jnp.transpose(total[1:], (1, 0, 2))
    return near_mask[:, None, :] * (velocity + inflow) / (scatter_rate + impurity)[:, None, :]


def solution(mesh):
    in_specs = (
        P(None, "interp", None, "bte"),
        P(),
        P("interp", None),
        P("interp", None, None, None),
        P("interp", None),
        P("bte"),
        P(("interp", "bte"), None),
        P(("interp", "bte")),
        P("bte", None),
        P("bte", None),
        P("bte", None, None),
        P("bte", None, None),
        P("bte", None),
    )
    out_specs = P("bte", None, None)
    return jax.shard_map(local, mesh=mesh, in_specs=in_specs, out_specs=out_specs, check_vma=False)
```

```python
import functools

import jax
import jax.numpy as jnp
from jax import lax
from jax.experimental import pallas as pl
from jax.experimental.pallas import tpu as pltpu
from jax.sharding import PartitionSpec as P

GRID = 160
SMEARING = 0.5
THERMAL = 0.3
LOG2_E = 1.4426950408889634
SCALE = (LOG2_E / (2.0 * SMEARING**2)) ** 0.5

BF16 = jnp.bfloat16
F32 = jnp.float32
LANES = 128
SUB = 8
VMEM_LIMIT = 58 * 1024 * 1024

NZ, NY, NX = 4, 4, 4
N_INTERP = NZ * NY

M_HALF, N_THIRD = 6, 3
GROUPS = 2 * M_HALF * N_THIRD
PARTS = ((0, 18), (18, 18))

Q_BLOCK = 16
COL_STRIDE = 264
D_STRIDE = 136
D_BLOCK = 30
UNROLL = 16
PHASE_UNROLL = 3


def params():
    return pltpu.CompilerParams(vmem_limit_bytes=VMEM_LIMIT)


def whole(memory_space=pltpu.VMEM):
    return pl.BlockSpec(memory_space=memory_space)


def cost(flops, bytes_accessed, transcendentals=0):
    return pl.CostEstimate(
        flops=int(flops), bytes_accessed=int(bytes_accessed), transcendentals=int(transcendentals)
    )


def prepare_kernel(kbatch_ref, x_ref, energy_ref, mask_ref, dev_ref, owner_ref, row_ref, *refs):
    outs, (table, ids, near, rows) = refs[:-4], refs[-4:]
    planes, columns, nd = x_ref.shape
    bands, rows_own = energy_ref.shape
    stride = columns + SUB
    for j in range(planes):
        rows[pl.ds(j * stride, columns), 0:nd] = x_ref[j].astype(F32)
    keep = lax.broadcasted_iota(jnp.int32, (2 * SUB, LANES), 1) < nd
    for out, (first, count) in zip(outs, PARTS):
        for g in range(count):
            k, rest = divmod(first + g, M_HALF * N_THIRD)
            m_half, n_third = divmod(rest, N_THIRD)
            for pair in range(4):
                m = 2 * m_half + pair // 2
                n = 4 * n_third + 2 * (pair % 2)
                old = k * 144 + m * 12 + n
                one = rows[pl.ds(old, SUB, stride=stride), :]
                two = rows[pl.ds(old + 1, SUB, stride=stride), :]
                both = jnp.where(keep, jnp.concatenate([one, two], axis=0), 0.0)
                out[4 * g + pair] = both.astype(BF16)
    energies = energy_ref[...]
    mask = mask_ref[...].astype(F32)
    table[0:bands, :] = energies
    for c in range(3):
        table[(c + 1) * bands : (c + 2) * bands, :] = dev_ref[c] * mask
    ids[...] = owner_ref[...] * rows_own + row_ref[...]
    lane = lax.broadcasted_iota(jnp.int32, (bands, rows_own), 1)
    for k in range(2):
        line = jnp.sum(jnp.where(lane == kbatch_ref[k], energies, 0.0), axis=1, keepdims=True)
        line = jnp.broadcast_to(line * SCALE, (bands, LANES))
        for n_third in range(N_THIRD):
            some = line[4 * n_third : 4 * n_third + 4]
            first = (k * N_THIRD + n_third) * SUB
            near[first : first + SUB, :] = jnp.concatenate([some, some], axis=0)


def prepare(kbatch, planes, energy, mask, dev, owner, row):
    n, columns, _ = planes.shape
    bands, rows_own = energy.shape
    return pl.pallas_call(
        prepare_kernel,
        out_shape=[jax.ShapeDtypeStruct((4 * c, 16, LANES), BF16) for _, c in PARTS]
        + [
            jax.ShapeDtypeStruct((4 * bands, rows_own), F32),
            jax.ShapeDtypeStruct(owner.shape, jnp.int32),
            jax.ShapeDtypeStruct((2 * N_THIRD * SUB, LANES), F32),
        ],
        in_specs=[whole(pltpu.SMEM)] + [whole()] * 6,
        out_specs=[whole()] * (len(PARTS) + 3),
        scratch_shapes=[pltpu.VMEM((n * (columns + SUB), LANES), F32)],
        compiler_params=params(),
        cost_estimate=cost(1e5, 1e5),
        name="prepare",
    )(kbatch, planes, energy, mask, dev, owner, row)


def tables_kernel(n_q_total, q_ref, vec_ref, freq_ref, out, freq_out):
    n_q = q_ref.shape[1]
    own = lax.axis_index("interp")
    z, y = own // NY, own % NY
    points = [
        jnp.transpose(jnp.broadcast_to(q_ref[c : c + 1, :].astype(F32), (LANES, n_q)))
        for c in range(3)
    ]
    points = [jnp.concatenate([p, p], axis=1) for p in points]
    vectors = vec_ref[...].astype(F32).astype(BF16)
    lane = lax.broadcasted_iota(jnp.int32, (1, 2 * LANES), 1)
    block, parity, part, vector = lane // 16, lane // 8 % 2, lane // 4 % 2, lane % 4
    number = lax.broadcasted_iota(jnp.int32, (vec_ref.shape[1], 2 * LANES), 0)
    dz, turn = block % 4, block // 4
    dy = jnp.where(turn == 2, 3, jnp.where(turn == 3, 2, turn))
    source = (z - dz + NZ) % NZ * NY + (y - dy + NY) % NY
    pick = jnp.where(number == source * 4 + vector, 1.0, 0.0).astype(BF16)
    chosen = jnp.dot(vectors, pick, preferred_element_type=F32)
    product = sum(points[c] * chosen[c : c + 1, :] for c in range(3))
    product = product + (part * (GRID // 4)).astype(F32)
    for row, turned in enumerate((product, product - GRID // 4)):
        turned = turned - GRID * jnp.floor((turned + 0.5) * (1.0 / GRID))
        value = jnp.cos((2.0 * jnp.pi / GRID) * turned)
        for side in range(2):
            first = (2 * side + row) * n_q
            out[first : first + n_q, :] = jnp.where(parity == side, value, 0.0).astype(BF16)
    modes = freq_ref.shape[0]
    w = jnp.concatenate([freq_ref[...], jnp.ones((LANES - modes, n_q), F32)], axis=0)
    w = jnp.transpose(w)
    occupy = 1.0 / (jnp.exp(w / THERMAL) - 1.0)
    share = 1.0 / (w * n_q_total)
    freq_out[0:n_q, :] = w * SCALE
    freq_out[n_q : 2 * n_q, :] = jnp.log(occupy * share) * LOG2_E
    freq_out[2 * n_q : 3 * n_q, :] = jnp.log((occupy + 1.0) * share) * LOG2_E


def tables(n_q_total, points, vectors, freq):
    n_q = points.shape[1]
    return pl.pallas_call(
        functools.partial(tables_kernel, n_q_total),
        out_shape=[
            jax.ShapeDtypeStruct((4 * n_q, 2 * LANES), BF16),
            jax.ShapeDtypeStruct((3 * n_q, LANES), F32),
        ],
        in_specs=[whole()] * 3,
        out_specs=[whole()] * 2,
        compiler_params=params(),
        cost_estimate=cost(1e5, 1e5),
        name="tables",
    )(points, vectors, freq)


def modes_kernel(nd, nu, turn_steps, pol_ref, out_ref, rows):
    step = pl.program_id(0)

    @pl.when(step < turn_steps)
    def _():
        pad = jnp.zeros((LANES - nu, LANES), F32)

        def one(t, carry):
            plane = jnp.concatenate([pol_ref[t].astype(F32), pad], axis=0)
            first = pl.multiple_of((step * D_BLOCK + t) * D_STRIDE, SUB)
            rows[pl.ds(first, LANES), :] = jnp.transpose(plane)
            return carry

        lax.fori_loop(0, D_BLOCK, one, 0, unroll=10)

    @pl.when(step >= turn_steps)
    def _():
        pad = jnp.zeros((LANES - nd, LANES), F32)

        def one_q(i, carry):
            q = (step - turn_steps) * Q_BLOCK + i
            real = rows[pl.ds(q, nd, stride=D_STRIDE), :]
            imag = rows[pl.ds(nd * D_STRIDE + q, nd, stride=D_STRIDE), :]
            out_ref[i, :, 0:LANES] = jnp.concatenate([real, pad], axis=0).astype(BF16)
            out_ref[i, :, LANES:] = jnp.concatenate([imag, pad], axis=0).astype(BF16)
            return carry

        lax.fori_loop(0, Q_BLOCK, one_q, 0, unroll=4)


def modes(pol):
    planes, nu, n_q = pol.shape
    nd = planes // 2
    turn_steps = planes // D_BLOCK
    return pl.pallas_call(
        functools.partial(modes_kernel, nd, nu, turn_steps),
        grid=(turn_steps + n_q // Q_BLOCK,),
        out_shape=jax.ShapeDtypeStruct((n_q, LANES, 2 * LANES), BF16),
        in_specs=[
            pl.BlockSpec((D_BLOCK, nu, n_q), lambda s: (jnp.minimum(s, turn_steps - 1), 0, 0))
        ],
        out_specs=pl.BlockSpec(
            (Q_BLOCK, LANES, 2 * LANES), lambda s: (jnp.maximum(s - turn_steps, 0), 0, 0)
        ),
        scratch_shapes=[pltpu.VMEM((planes * D_STRIDE, LANES), F32)],
        compiler_params=params(),
        cost_estimate=cost(1e5, 1e5),
        name="modes",
    )(pol)


def lookup_kernel(ids_ref, *refs):
    out = refs[-1]
    n_rows = refs[0].shape[-1]
    me = lax.axis_index("bte")
    half, x, core = me // (2 * NX), me // 2 % NX, me % 2
    ids = ids_ref[...]
    wanted = ids.shape[1]
    row = lax.broadcasted_iota(jnp.int32, (n_rows, wanted), 0)
    total = None
    for ref, dx in zip(refs[:-1], (0, 1, -1, 2)):
        for dc in range(2):
            owner = (half * NX + (x - dx + NX) % NX) * 2 + (core + dc) % 2
            table = ref[dc]
            high = table.astype(BF16)
            rest = table - high.astype(F32)
            middle = rest.astype(BF16)
            low = (rest - middle.astype(F32)).astype(BF16)
            pick = jnp.where(row == ids - owner * n_rows, 1.0, 0.0).astype(BF16)
            got = jnp.dot(
                jnp.concatenate([high, middle, low], axis=0), pick, preferred_element_type=F32
            )
            total = got if total is None else total + got
    n = refs[0].shape[1]
    found = (total[2 * n :] + total[n : 2 * n]) + total[:n]
    out[0] = found[:, : wanted // 2]
    out[1] = found[:, wanted // 2 :]


def lookup(ids, tables):
    n = tables[0].shape[1]
    return pl.pallas_call(
        lookup_kernel,
        out_shape=jax.ShapeDtypeStruct((2, n, ids.shape[1] // 2), F32),
        in_specs=[whole()] * (1 + len(tables)),
        out_specs=whole(),
        compiler_params=params(),
        cost_estimate=cost(1e5, 1e5),
        name="lookup",
    )(ids, *tables)


def totals(got, parts, shape):
    upper = lax.broadcasted_iota(jnp.int32, (SUB, LANES), 0) < 4
    sums = {}
    g = 0
    for part in parts:
        for at in range(part.shape[0] // SUB):
            k, rest = divmod(g, M_HALF * N_THIRD)
            m_half, n_third = divmod(rest, N_THIRD)
            kernel = part[at * SUB : (at + 1) * SUB, :]
            for j in range(4):
                term = kernel
                if j:
                    line = j * 12 + 2 * m_half
                    lanes = slice(k * LANES, (k + 1) * LANES)
                    term = kernel * jnp.where(
                        upper,
                        jnp.broadcast_to(got[line : line + 1, lanes], (SUB, LANES)),
                        jnp.broadcast_to(got[line + 1 : line + 2, lanes], (SUB, LANES)),
                    )
                key = (j, k, n_third)
                sums[key] = sums[key] + term if key in sums else term
            g += 1
    stacked = jnp.concatenate([sums[key] for key in sorted(sums)], axis=0)
    pad = jnp.zeros((shape[1] - stacked.shape[0], LANES), F32)
    return lax.dot_general(
        jnp.ones((shape[0], LANES), F32),
        jnp.concatenate([stacked, pad], axis=0),
        (((1,), (1,)), ((), ())),
        preferred_element_type=F32,
        precision=lax.Precision.HIGHEST,
    )


def columns_kernel(first_group, n_blocks, n_q, earlier, *refs):
    phase_ref, blocks, refs = refs[0], refs[1 : 1 + n_blocks], refs[1 + n_blocks :]
    mode_ref, near_ref, mine_ref, theirs_ref, freq_ref = refs[:5]
    if earlier is None:
        out_ref, field, far_rows = refs[5:]
    else:
        others, (total_ref, field, far_rows, out_ref) = refs[5 : 5 + earlier], refs[5 + earlier :]
    columns = out_ref.shape[0]
    step = pl.program_id(0)

    @pl.when(step == 0)
    def _():
        def two_pairs(p, carry):
            sides = []
            for side in range(2):
                sides.append(
                    jnp.concatenate(
                        [b[:, 2 * p + side].reshape(b.shape[0] * 16, LANES) for b in blocks], axis=0
                    )
                )
            both = jnp.concatenate(sides, axis=1)
            for parity in range(2):
                got = jnp.dot(
                    phase_ref[2 * n_q * parity : 2 * n_q * (parity + 1), :],
                    both,
                    preferred_element_type=F32,
                )
                for side in range(2):
                    column = 4 * p + 2 * side + parity
                    field[pl.ds(pl.multiple_of(column * COL_STRIDE, SUB), 2 * n_q), :] = got[
                        :, side * LANES : (side + 1) * LANES
                    ]
            return carry

        lax.fori_loop(0, columns // 4, two_pairs, 0, unroll=PHASE_UNROLL)
        far = (mine_ref[0, 0:16, :] + theirs_ref[0, 0:16, :]) * SCALE
        for unit in range(columns // (N_THIRD * SUB)):
            k, m_half = divmod(first_group // N_THIRD + unit, M_HALF)
            for side in range(2):
                m = 2 * m_half + side
                line = far[m : m + 1, k * LANES : (k + 1) * LANES]
                turned = jnp.transpose(jnp.broadcast_to(line, (LANES, LANES)))
                for j in range(4):
                    row = unit * SUB + side * 4 + j
                    far_rows[pl.ds(row * D_STRIDE, LANES), :] = turned

    lane = lax.broadcasted_iota(jnp.int32, (columns, LANES), 1)
    units = columns // (N_THIRD * SUB)
    nears = []
    for unit in range(units):
        k = (first_group // N_THIRD + unit) // M_HALF
        nears.append(near_ref[k * N_THIRD * SUB : (k + 1) * N_THIRD * SUB, :])
    near = jnp.concatenate(nears, axis=0).reshape(units, N_THIRD, SUB, LANES)

    def some_q(i, carry):
        rotated = []
        for j in range(UNROLL):
            q = step * Q_BLOCK + i * UNROLL + j
            real = field[pl.ds(q, columns, stride=COL_STRIDE), :].astype(BF16)
            imag = field[pl.ds(q + n_q, columns, stride=COL_STRIDE), :].astype(BF16)
            mode = mode_ref[i * UNROLL + j]
            turn = jnp.concatenate([-mode[:, LANES:], mode[:, :LANES]], axis=1)
            rotated.append(
                jnp.dot(
                    jnp.concatenate([real, imag], axis=1),
                    jnp.concatenate([mode, turn], axis=0),
                    preferred_element_type=F32,
                )
            )
        out = out_ref[...]
        for j in range(UNROLL):
            q = step * Q_BLOCK + i * UNROLL + j
            far = far_rows[pl.ds(q, units * SUB, stride=D_STRIDE), :]
            gap = (near - far.reshape(units, 1, SUB, LANES)).reshape(columns, LANES)
            w = freq_ref[pl.ds(q, 1), :]
            plus, minus = gap + w, gap - w
            weight = jnp.exp2(freq_ref[pl.ds(n_q + q, 1), :] - plus * plus) + jnp.exp2(
                freq_ref[pl.ds(2 * n_q + q, 1), :] - minus * minus
            )
            real, imag = rotated[j][:, :LANES], rotated[j][:, LANES:]
            terms = (real * real + imag * imag) * weight
            out = jnp.where(lane == q, jnp.sum(terms, axis=1, keepdims=True), out)
        out_ref[...] = out
        return carry

    lax.fori_loop(0, Q_BLOCK // UNROLL, some_q, 0)

    if earlier is not None:

        @pl.when(step == pl.num_programs(0) - 1)
        def _():
            got = totals(mine_ref[0] + theirs_ref[0], [*others, out_ref], total_ref.shape[1:])
            for i in range(total_ref.shape[0]):
                total_ref[i] = got


def columns_of(index, phase, blocks, mode, near, mine, theirs, freq, others=None):
    n_q = mode.shape[0]
    first, groups = PARTS[index]
    columns = SUB * groups
    fixed = lambda shape: pl.BlockSpec(shape, lambda s: (0,) * len(shape))
    operands = [phase, *blocks]
    rest = [near, mine, theirs, freq, *(others or [])]
    sums = (columns, LANES)
    out = sums if others is None else (N_INTERP, SUB, 2 * LANES)
    return pl.pallas_call(
        functools.partial(
            columns_kernel, first, len(blocks), n_q, None if others is None else len(others)
        ),
        grid=(n_q // Q_BLOCK,),
        out_shape=jax.ShapeDtypeStruct(out, F32),
        in_specs=[fixed(o.shape) for o in operands]
        + [pl.BlockSpec((Q_BLOCK, LANES, 2 * LANES), lambda s: (s, 0, 0))]
        + [fixed(o.shape) for o in rest],
        out_specs=fixed(out),
        scratch_shapes=[
            pltpu.VMEM((columns * COL_STRIDE, LANES), F32),
            pltpu.VMEM((columns // N_THIRD * D_STRIDE, LANES), F32),
        ]
        + ([] if others is None else [pltpu.VMEM(sums, F32)]),
        compiler_params=params(),
        cost_estimate=cost(1e5, 1e5),
        name="columns",
    )(*operands, mode, *rest)


def interp_pairs(dz, dy):
    return [
        (z * NY + y, (z + dz) % NZ * NY + (y + dy) % NY) for z in range(NZ) for y in range(NY)
    ]


def bte_pairs(dh, dx, dc):
    return [
        ((h * NX + x) * 2 + c, ((h + dh) % 2 * NX + (x + dx) % NX) * 2 + (c + dc) % 2)
        for h in range(2)
        for x in range(NX)
        for c in range(2)
    ]


def along_interp(value, dz, dy):
    return lax.ppermute(value, "interp", interp_pairs(dz, dy))


def along_bte(value, dh, dx, dc):
    return lax.ppermute(value, "bte", bte_pairs(dh, dx, dc))


def after(value, *others):
    return lax.optimization_barrier((value, *others))[0]


def both_ways(own):
    return along_interp(own, 0, 1), along_interp(own, 0, -1)


def local(
    coupling,
    rvectors,
    qpoints,
    polarization,
    frequencies,
    kbatch,
    kq_owner,
    kq_row,
    energy,
    band_mask,
    deviation,
    velocity,
    impurity,
):
    n_q = qpoints.shape[0]
    nbands = energy.shape[1]
    nmodes = frequencies.shape[1]
    q_total = n_q * lax.axis_size("interp")
    columns = coupling.shape[3]

    planes = jnp.swapaxes(coupling, 2, 3).reshape(-1, columns, nmodes)
    *own_parts, own_table, ids, near = prepare(
        kbatch,
        planes,
        energy.T,
        band_mask.T,
        jnp.transpose(deviation, (1, 2, 0)),
        kq_owner.reshape(1, -1),
        kq_row.reshape(1, -1),
    )
    own_first, own_second = own_parts

    other_ids = along_bte(ids, 1, 0, 0)
    phase, freq = tables(q_total, *after((qpoints.T, rvectors.T, frequencies.T), ids))
    other_table = along_bte(own_table, 0, 0, 1)

    def behind(own, *before):
        one, three = along_interp(own, 1, 0), along_interp(own, -1, 0)
        two = along_interp(after(one, *before), 1, 0)
        return jnp.stack([own, one]), jnp.stack([two, three])

    chip_table = jnp.stack([own_table, other_table])
    near_tables = [along_bte(chip_table, 0, dx, 0) for dx in (1, -1, 2)]

    all_ids = jnp.concatenate([ids, other_ids], axis=1)
    found = lookup(all_ids, [chip_table] + near_tables)
    mine, theirs = found, along_bte(found[1:], 1, 0, 0)

    first_near, first_late = behind(own_first, freq, other_ids)
    first_up, first_down = both_ways(first_near)
    late_up, late_down = both_ways(first_late)
    first_far = along_interp(first_up, 0, 1), along_interp(late_down, 0, -1)
    first = (first_near, first_late, first_up, late_up, first_down, late_down, *first_far)

    second_near, second_late = behind(
        after(own_second, first_late, other_ids), late_up, late_down, first_up, first_down, found
    )
    second_up, second_down = both_ways(after(second_near, first_up, late_down))
    second_late_up, second_late_down = both_ways(after(second_late, *first_far))

    pol = jnp.transpose(polarization, (1, 2, 3, 0)).reshape(2 * nmodes, nmodes, n_q)
    mode = modes(after(pol, second_late, *first_far))

    second_far = (
        along_interp(after(second_up, mode, theirs), 0, 1),
        along_interp(after(second_late_down, mode, theirs), 0, -1),
    )
    second = (
        second_near,
        second_late,
        second_up,
        second_late_up,
        second_down,
        second_late_down,
        *second_far,
    )

    rest = (mode, near, mine, theirs, freq)
    sums = columns_of(0, phase, first, *rest)
    total = columns_of(1, phase, second, *rest, others=[sums])
    near_mask = band_mask[kbatch].astype(F32)

    total = lax.all_to_all(total, "interp", 0, 0, tiled=True)[:, 0].sum(axis=0)
    total = total[: 4 * 48].reshape(4, 2, N_THIRD, 2, 4).sum(axis=3).reshape(4, 2, nbands)
    scatter_rate = total[0]
    inflow = jnp.transpose(total[1:], (1, 0, 2))
    return near_mask[:, None, :] * (velocity + inflow) / (scatter_rate + impurity)[:, None, :]


def solution(mesh):
    in_specs = (
        P(None, "interp", None, "bte"),
        P(),
        P("interp", None),
        P("interp", None, None, None),
        P("interp", None),
        P("bte"),
        P(("interp", "bte"), None),
        P(("interp", "bte")),
        P("bte", None),
        P("bte", None),
        P("bte", None, None),
        P("bte", None, None),
        P("bte", None),
    )
    out_specs = P("bte", None, None)
    return jax.shard_map(local, mesh=mesh, in_specs=in_specs, out_specs=out_specs, check_vma=False)
```
